256 devices in a mesh: tm: 32 (over y, z), chan: 8 (over x, core).
Axes of the slice: x: 4, y: 4, z: 8, core: 2. Of those that a mesh axis runs over, the one named last changes fastest.
Arguments:
- samples: bfloat16 [65536, 1024], P('tm', 'chan'), may hold values from -30 to 30
- candidates: int32 [32, 8], P('tm'), may hold values from 1 to 2047
- segment_start: int32 [32], P('tm'), may hold values from 0 to 1, as said below
Outputs:
- window_cov: float32 [32, 1024, 1024], P('tm', 'chan')
- segment_cov: float32 [32, 1024, 1024], P('tm', 'chan')
- cusum: float32 [32, 8, 1024, 1024], P('tm', None, 'chan')
The draws below stay inside these ranges and needn't reach their ends.
Inputs may be any that keep to these rules, and one draw needn't show every extreme that they name: `segment_start`: block 0 always begins a segment; only blocks of even index begin segments, so every segment holds two or more blocks; block 16 never begins one.
All inputs are finite; a program needn't handle non-finite values.
Results may differ from the reference program's by a relative error of at most 0.0003.
The reference program's roundings to bfloat16 on the way (of `centered`) count: a program that leaves them out, or rounds other values in their place, can miss the bound.
Values may be sent and summed in bfloat16 or wider, within the bound.
No kernel may reach another device: no remote copies, remote signals or barrier semaphores. Data moves between devices by JAX's collectives and lax.ppermute only.
A program may use at most 128 MiB of HBM per device.

```python
import math
import jax
import jax.numpy as jnp
from jax import lax

CHANNELS = 1024
S_DEV = 2048
HALO_ROWS = 1024
K_SPLITS = 8
TOTAL_ROWS = 65536
N_TM = 32


def draw_samples(key, part):
    key = jax.random.fold_in(key, 11)
    key_list = jax.random.split(key, 4)
    channel_scale = jnp.exp(jax.random.uniform(key_list[0], (CHANNELS,), jnp.float32, math.log(0.3), math.log(3.0)))
    group_count = TOTAL_ROWS // 128
    regime = jnp.exp(jax.random.uniform(key_list[1], (group_count,), jnp.float32, math.log(0.5), math.log(2.0)))
    row_scale = jnp.repeat(regime, 128)
    shifted = jax.random.uniform(key_list[2], (CHANNELS,), jnp.float32, -0.5, 0.5)
    noise_field = jnp.clip(jax.random.normal(key_list[3], (TOTAL_ROWS, CHANNELS), jnp.float32), -4.0, 4.0)
    values = channel_scale[None, :] * row_scale[:, None] * noise_field + shifted[None, :]
    return values.astype(jnp.bfloat16)


def draw_segment_start(key, part):
    key = jax.random.fold_in(key, 23)
    blocks = jnp.arange(N_TM, dtype=jnp.int32)
    rolls = jax.random.randint(key, (N_TM,), 0, 5)
    even_block = (blocks % 2 == 0).astype(jnp.int32)
    not_middle = (blocks != N_TM // 2).astype(jnp.int32)
    picked = (rolls < 2).astype(jnp.int32) * even_block * not_middle
    boundary = jnp.maximum(picked, (blocks == 0).astype(jnp.int32))
    return boundary.astype(jnp.int32)


def with_ends(drawn, rng, low, top_value):
    longest = drawn.shape.index(max(drawn.shape))
    spots = []
    for shift in (0, 1):
        where = [jax.random.randint(jax.random.fold_in(rng, axis), (), 0, length) for axis, length in enumerate(drawn.shape)]
        where[longest] = (where[longest] + shift) % drawn.shape[longest]
        spots.append(tuple(where))
    return drawn.at[spots[0]].set(low).at[spots[1]].set(top_value)


def setup_inputs(seed: int = 0) -> dict:
    streams_of = jax.random.split(jax.random.key(seed), 4)
    return {
        "samples": draw_samples(jax.random.fold_in(streams_of[3], 71), 0),
        "candidates": with_ends(jax.random.randint(streams_of[1], (N_TM, K_SPLITS), 1, S_DEV), jax.random.fold_in(streams_of[1], 1), 1, S_DEV - 1).astype(jnp.int32),
        "segment_start": draw_segment_start(jax.random.fold_in(streams_of[3], 71), 0),
    }


def choose(keeper, first, second):
    return tuple(jnp.where(keeper, first_item, second_item) for first_item, second_item in zip(first, second))


def merge_states(first, second):
    count_first, mean_first, spread_first = first
    count_second, mean_second, spread_second = second
    total_count = count_first + count_second
    safe_count = jnp.maximum(total_count, 1.0)
    difference = mean_second - mean_first
    merged_mean = mean_first + difference * (count_second / safe_count)
    merged_spread = spread_first + spread_second + (count_first * count_second / safe_count) * (difference[:, None] * difference[None, :])
    return total_count, merged_mean, merged_spread


def forward_join(earlier, latter):
    merged = merge_states(earlier[:3], latter[:3])
    keeper = latter[3] > 0.5
    return choose(keeper, latter[:3], merged) + (jnp.maximum(earlier[3], latter[3]),)


def backward_join(earlier, latter):
    merged = merge_states(latter[:3], earlier[:3])
    keeper = latter[3] > 0.5
    return choose(keeper, latter[:3], merged) + (jnp.maximum(earlier[3], latter[3]),)


def local_state(count_value, mean_value, column_sum, gram_part):
    return (count_value, mean_value + column_sum / count_value, gram_part - column_sum[:, None] * column_sum[None, :] / count_value)


def reference(samples, candidates, segment_start):
    padded = jnp.concatenate([jnp.zeros((HALO_ROWS, CHANNELS), jnp.bfloat16), samples], axis=0)
    indices = jnp.arange(N_TM, dtype=jnp.int32)

    def own_block(block_index):
        window = lax.dynamic_slice_in_dim(padded, block_index * S_DEV, HALO_ROWS + S_DEV, 0)
        own_rows = window[HALO_ROWS:]
        block_mean = jnp.sum(own_rows.astype(jnp.float32), axis=0) / S_DEV
        centered = (own_rows.astype(jnp.float32) - block_mean).astype(jnp.bfloat16)
        own_sum = jnp.sum(centered.astype(jnp.float32), axis=0)
        own_gram = jnp.dot(centered.T, centered, preferred_element_type=jnp.float32)
        return window, block_mean, centered, own_sum, own_gram

    def first_pass(block_index):
        window, block_mean, centered, own_sum, own_gram = own_block(block_index)
        halo_live = (block_index > 0).astype(jnp.float32)
        prior_rows = ((window[:HALO_ROWS].astype(jnp.float32) - block_mean) * halo_live).astype(jnp.bfloat16)
        halo_sum = jnp.sum(prior_rows.astype(jnp.float32), axis=0)
        halo_gram = jnp.dot(prior_rows.T, prior_rows, preferred_element_type=jnp.float32)
        window_count = S_DEV + halo_live * HALO_ROWS
        window_sum = halo_sum + own_sum
        window_cov = (halo_gram + own_gram - window_sum[:, None] * window_sum[None, :] / window_count) / (window_count - 1.0)
        state = local_state(jnp.float32(S_DEV), block_mean, own_sum, own_gram)
        return window_cov, state[1], state[2]

    window_cov, state_means, state_spreads = lax.map(first_pass, indices)
    start_flags = segment_start.astype(jnp.float32)
    counts = jnp.full((N_TM,), S_DEV, jnp.float32)
    identity = (jnp.float32(0.0), jnp.zeros((CHANNELS,), jnp.float32), jnp.zeros((CHANNELS, CHANNELS), jnp.float32), jnp.float32(0.0))

    def forward_step(carried, leaf_item):
        return forward_join(carried, leaf_item), carried

    unused_forward, before = lax.scan(forward_step, identity, (counts, state_means, state_spreads, start_flags))
    backward_leaves = (jnp.where(start_flags > 0.5, 0.0, counts), jnp.where(start_flags[:, None] > 0.5, 0.0, state_means), jnp.where(start_flags[:, None, None] > 0.5, 0.0, state_spreads), start_flags)

    def backward_step(carried, leaf_item):
        return backward_join(carried, leaf_item), carried

    unused_backward, suffix_all = lax.scan(backward_step, identity, backward_leaves, reverse=True)

    def second_pass(packed):
        block_index, split_points, start_flag, before_item, after_item = packed
        window, block_mean, centered, own_sum, own_gram = own_block(block_index)
        positions = jnp.arange(S_DEV, dtype=jnp.int32)
        row_masks = (positions[None, :] < split_points[:, None]).astype(jnp.float32)
        wide_rows = centered.astype(jnp.float32)
        left_sums = jnp.dot(row_masks, wide_rows, preferred_element_type=jnp.float32, precision=lax.Precision.HIGHEST)
        left_grams = jnp.einsum("ksa,sb->kab", row_masks[:, :, None] * wide_rows[None, :, :], wide_rows, precision=lax.Precision.HIGHEST)
        empty_state = identity[:3]
        prefix = choose(start_flag > 0.5, empty_state, before_item[:3])
        suffix = after_item[:3]
        block_state = local_state(jnp.float32(S_DEV), block_mean, own_sum, own_gram)
        total_state = merge_states(merge_states(prefix, block_state), suffix)
        segment_cov = total_state[2] / total_state[0]
        left_counts = split_points.astype(jnp.float32)
        state_map = jax.vmap(local_state, in_axes=(0, None, 0, 0))
        left_local = state_map(left_counts, block_mean, left_sums, left_grams)
        right_local = state_map(S_DEV - left_counts, block_mean, own_sum - left_sums, own_gram - left_grams)
        left_state = jax.vmap(merge_states, in_axes=(None, 0))(prefix, left_local)
        right_state = jax.vmap(merge_states, in_axes=(0, None))(right_local, suffix)
        count_left = left_state[0]
        count_right = right_state[0]
        count_all = count_left + count_right
        weight = count_left * count_right / (count_all * count_all)
        cusum_tiles = weight[:, None, None] * (left_state[2] / count_left[:, None, None] - right_state[2] / count_right[:, None, None])
        return segment_cov, cusum_tiles

    segment_cov, cusum_tiles = lax.map(second_pass, (indices, candidates, start_flags, before, suffix_all))
    return window_cov, segment_cov, cusum_tiles
```

```python
import jax
import jax.numpy as jnp
from jax import lax
from jax.experimental import pallas as pl
from jax.experimental.pallas import tpu as pltpu
from jax.sharding import PartitionSpec as P

F32, BF16 = jnp.float32, jnp.bfloat16
ROWS, HALO, WIDTH, BLOCKS, SPLITS, CHIPS = 2048, 1024, 128, 32, 8, 4
PAIR = 2 * WIDTH
HIGH = lax.Precision.HIGHEST
TRANSPOSED = (((0,), (0,)), ((), ()))
SM = pl.BlockSpec(memory_space=pltpu.SMEM)
HBM = pl.BlockSpec(memory_space=pltpu.HBM)
MIB = 2**20


def whole(*shape):
    return pl.BlockSpec(shape, lambda *_: (0,) * len(shape))


def array(*shape, dtype=F32):
    return jax.ShapeDtypeStruct(shape, dtype)


def params(grant):
    return pltpu.CompilerParams(
        vmem_limit_bytes=grant * MIB, dimension_semantics=("arbitrary",)
    )


def cost(microseconds):
    return pl.CostEstimate(
        flops=int(microseconds * 1e9), bytes_accessed=MIB, transcendentals=0
    )


def center_shard(raw_ref, out_ref, at):
    step = 256

    def add(i, total):
        piece = raw_ref[pl.ds(i * step, step), :].astype(F32)
        return total + jnp.sum(piece.reshape(step // 8, 8, WIDTH), axis=0)

    total = lax.fori_loop(0, ROWS // step, add, jnp.zeros((8, WIDTH), F32), unroll=2)
    mean = jnp.sum(total, axis=0, keepdims=True) / ROWS

    def shift(i, _):
        piece = raw_ref[pl.ds(i * step, step), :].astype(F32) - mean
        out_ref[pl.ds(i * step, step), pl.ds(at, WIDTH)] = piece.astype(BF16)
        return 0

    lax.fori_loop(0, ROWS // step, shift, 0, unroll=2)
    return mean


def center_pair(first_ref, second_ref, at, off, cent_ref, stat_ref):
    stat_ref[0] = jnp.zeros((8, PAIR), F32)
    stat_ref[0, 0:1, pl.ds(at, WIDTH)] = center_shard(first_ref, cent_ref, at)
    stat_ref[0, 0:1, pl.ds(off, WIDTH)] = center_shard(second_ref, cent_ref, off)
    total = jnp.dot(jnp.ones((16, ROWS), BF16), cent_ref[...], preferred_element_type=F32)[0:1]
    stat_ref[0, 1:2, :] = total
    stat_ref[0, 2:3, :] = stat_ref[0, 0:1, :] + total / ROWS


def turned_dot(left, right):
    return lax.dot_general(left, right, TRANSPOSED, preferred_element_type=F32)


def wide(value):
    return jnp.concatenate([value, value], axis=1)


def left_part(where_ref, flipped, cent_ref, left_ref, sums_ref):
    index = lax.broadcasted_iota(jnp.int32, (16, ROWS), 0)
    place = lax.broadcasted_iota(jnp.int32, (16, ROWS), 1)
    limit = jnp.zeros((16, ROWS), jnp.int32)
    for j in range(SPLITS):
        limit = jnp.where(index == j, where_ref[12 + j], limit)
    masks = jnp.where(place < limit, 1.0, 0.0).astype(BF16)
    cent = cent_ref[...]
    sums_ref[0] = jnp.dot(masks, cent, preferred_element_type=F32)[0:8]
    for i in range(SPLITS // 4):
        kept = jnp.concatenate([flipped * masks[j : j + 1, :] for j in range(4 * i, 4 * i + 4)], axis=0)
        part = jnp.dot(kept, cent, preferred_element_type=F32)
        for j in range(4):
            left_ref[0, 4 * i + j] = part[j * WIDTH : (j + 1) * WIDTH]


def first_kernel(
    where_ref, mine_ref, other_ref,
    left_ref, sums_ref, gram_ref, stat_ref, flip_hbm, total_hbm, flip_ref, spread_ref, total_ref, rider_ref, cent_ref,
):
    core = where_ref[2]
    at = pl.multiple_of(core * WIDTH, WIDTH)
    off = pl.multiple_of((1 - core) * WIDTH, WIDTH)
    center_pair(mine_ref, other_ref, at, off, cent_ref, stat_ref)
    rider_ref[...] = jnp.zeros((8, WIDTH), F32)
    rider_ref[0:1, :] = stat_ref[0, 2:3, 0:WIDTH]
    rider_ref[1:2, :] = stat_ref[0, 2:3, WIDTH:PAIR]
    rider_ref[2:3, :] = jnp.full((1, WIDTH), where_ref[20], jnp.int32).astype(F32)
    flip_ref[...] = cent_ref[:, pl.ds(at, WIDTH)].T
    flipped = flip_ref[...]
    flip_hbm[...] = flipped
    gram = jnp.dot(flipped, cent_ref[...], preferred_element_type=F32)
    gram_ref[0] = gram
    total = jnp.dot(flipped, jnp.ones((ROWS, WIDTH), BF16), preferred_element_type=F32)
    total_ref[...] = total
    total_hbm[...] = total
    spread_ref[...] = gram - wide(total) * (stat_ref[0, 1:2, :] / ROWS)
    left_part(where_ref, flipped, cent_ref, left_ref, sums_ref)


def near_kernel(
    where_ref, first_ref, second_ref, flip_ref, total_ref,
    left_ref, sums_ref, gram_ref, stat_ref, spread_ref, cent_ref,
):
    center_pair(first_ref, second_ref, 0, WIDTH, cent_ref, stat_ref)
    flipped = flip_ref[...]
    gram = jnp.dot(flipped, cent_ref[...], preferred_element_type=F32)
    gram_ref[0] = gram
    spread_ref[...] = gram - wide(total_ref[...]) * (stat_ref[0, 1:2, :] / ROWS)
    left_part(where_ref, flipped, cent_ref, left_ref, sums_ref)


def side_kernel(
    where_ref, first_ref, second_ref, flip_ref, left_ref, sums_ref, gram_ref, stat_ref, cent_ref
):
    center_pair(first_ref, second_ref, 0, WIDTH, cent_ref, stat_ref)
    flipped = flip_ref[...]
    gram_ref[0] = jnp.dot(flipped, cent_ref[...], preferred_element_type=F32)
    left_part(where_ref, flipped, cent_ref, left_ref, sums_ref)


def far_kernel(
    where_ref, first_ref, second_ref, flip_ref, total_ref, spread0_ref, spread1_ref, rider_ref,
    gram_ref, stat_ref, out_ref, cent_ref, held_ref,
):
    rider = rider_ref[0:4, :]
    for q in range(BLOCKS):
        spread, lane = ((spread0_ref, spread1_ref)[q // 16], WIDTH * (q // 8 % 2))
        row = 16 * (q % 8)
        out_ref[q, 0:16, :] = spread[row : row + 16, lane : lane + WIDTH]
        out_ref[q, 20:24, :] = rider
    center_pair(first_ref, second_ref, 0, WIDTH, cent_ref, stat_ref)
    gram = jnp.dot(flip_ref[...], cent_ref[...], preferred_element_type=F32)
    gram_ref[0] = gram
    spread = gram - wide(total_ref[...]) * (stat_ref[0, 1:2, :] / ROWS)
    held_ref[...] = jnp.where(where_ref[3] == 0, spread[:, 0:WIDTH], spread[:, WIDTH:PAIR])
    for q in range(BLOCKS):
        out_ref[q, 16:20, :] = held_ref[4 * q : 4 * q + 4, :]


def rest_kernel(where_ref, cent_ref, flip_ref, left_ref, sums_ref):
    left_part(where_ref, flip_ref[...], cent_ref, left_ref, sums_ref)


ALL = [
    array(CHIPS, SPLITS, WIDTH, PAIR),
    array(CHIPS, 8, PAIR),
    array(CHIPS, WIDTH, PAIR),
    array(CHIPS, 8, PAIR),
]


def call(
    kernel, name, inputs, outputs, *, fetched=(), stored=(), kept=(), pair=0, scratch=(), us=3, grant=24
):
    count, held, made = len(inputs), len(kept), len(outputs)
    sliced = [i < len(ALL) and outputs[i] in ALL for i in range(made)]
    sizes = [(1, *out.shape[1:]) if cut else out.shape for out, cut in zip(outputs, sliced)]
    buffers = [pltpu.VMEM(inputs[i].shape, inputs[i].dtype) for i in fetched]
    buffers += [pltpu.VMEM(sizes[i], outputs[i].dtype) for i in stored]

    def body(*refs):
        ins, refs = list(refs[:count]), refs[count + held :]
        outs, refs = list(refs[:made]), refs[made:]
        own, buffer, sem = refs[: len(scratch)], refs[len(scratch) : -1], refs[-1]
        copies = []
        for c, i in enumerate(fetched):
            copies.append(pltpu.make_async_copy(ins[i], buffer[c], sem.at[c]))
            ins[i] = buffer[c]
        for copy in copies:
            copy.start()
        for copy in copies:
            copy.wait()
        copies = []
        for c, i in enumerate(stored, len(fetched)):
            target = outs[i].at[pl.ds(pair, 1)] if sliced[i] else outs[i]
            copies.append(pltpu.make_async_copy(buffer[c], target, sem.at[c]))
            outs[i] = buffer[c]
        kernel(*ins, *outs, *own)
        for copy in copies:
            copy.start()
        for copy in copies:
            copy.wait()

    ins = [SM if value.dtype == jnp.int32 else whole(*value.shape) for value in inputs]
    for i in fetched:
        ins[i] = HBM
    outs = [HBM if i in stored else whole(*out.shape) for i, out in enumerate(outputs)]
    return pl.pallas_call(
        body,
        out_shape=outputs,
        grid=(1,),
        in_specs=ins + [HBM] * held,
        out_specs=outs,
        input_output_aliases={count + i: i for i in range(held)},
        scratch_shapes=[pltpu.VMEM(shape, dtype) for shape, dtype in scratch]
        + buffers
        + [pltpu.SemaphoreType.DMA((max(len(buffers), 1),))],
        compiler_params=params(grant),
        cost_estimate=cost(us),
        name=name,
    )(*inputs, *kept)


def scan_kernel(arrived_ref, both_ref, means_ref, flags_ref):
    for b in range(BLOCKS):
        rider = arrived_ref[b, 16:24, :]
        means_ref[0, b : b + 1, :] = rider[4:5, :]
        means_ref[1, b : b + 1, :] = rider[5:6, :]
        flags_ref[b : b + 1, :] = rider[6:7, :]
    scan(arrived_ref, flags_ref, both_ref, 0, 16, 0)
    scan(arrived_ref, flags_ref, both_ref, 16, 4, 32)


def scan(arrived_ref, flags_ref, both_ref, row, size, at):
    zero = jnp.zeros((size, WIDTH), F32)
    running = zero
    for b in range(BLOCKS):
        begins = flags_ref[b : b + 1, :] > 0.5
        running = jnp.where(begins, zero, running)
        both_ref[b, at : at + size, :] = running
        running = running + arrived_ref[b, row : row + size, :]
    running = zero
    for b in reversed(range(BLOCKS)):
        begins = flags_ref[b : b + 1, :] > 0.5
        both_ref[b, at + size : at + 2 * size, :] = running
        running = jnp.where(begins, zero, running + arrived_ref[b, row : row + size, :])


def prep_kernel(
    where_ref, sums_ref, gram_ref, stat_ref, own_means_ref, ahead_ref, behind_ref, far_ref, flags_ref,
    turned_ref, cols_ref, coef_ref, before_ref, after_ref, vectors,
):
    here = where_ref[0]
    core = where_ref[2]
    away = 1 - core
    flags = flags_ref[...]
    spot = lax.broadcasted_iota(jnp.int32, (BLOCKS, WIDTH), 0)
    low = lax.broadcasted_iota(jnp.int32, (BLOCKS, BLOCKS), 1)
    high = lax.broadcasted_iota(jnp.int32, (BLOCKS, BLOCKS), 0)
    upto = jnp.dot((low <= high).astype(F32), flags, preferred_element_type=F32)
    mine = jnp.sum(jnp.where(spot <= here, flags, 0.0), axis=0, keepdims=True)
    same = jnp.abs(upto - mine) < 0.5
    masks = [
        jnp.where(same & (spot < here), 1.0, 0.0),
        jnp.where(same & (spot > here), 1.0, 0.0),
    ]
    totals = [jnp.sum(mask, axis=0, keepdims=True) for mask in masks]
    count_p, count_s = totals[0] * ROWS, totals[1] * ROWS

    def pooled(means, side):
        mask = masks[side]
        mean = jnp.sum(means * mask, axis=0, keepdims=True) / jnp.maximum(totals[side], 1.0)
        return mean, (means - mean) * mask

    def pick(value):
        return jnp.where(core == 0, value[:, 0:WIDTH], value[:, WIDTH:PAIR])

    row_means = own_means_ref[core]
    row_p, row_part_p = pooled(row_means, 0)
    row_s, row_part_s = pooled(row_means, 1)
    row_stat = pick(stat_ref[0])
    row_sums = pick(sums_ref[0])

    index = lax.broadcasted_iota(jnp.int32, (SPLITS, WIDTH), 0)
    k = jnp.zeros((SPLITS, WIDTH), jnp.int32)
    for j in range(SPLITS):
        k = jnp.where(index == j, where_ref[12 + j], k)
    k = k.astype(F32)
    rest = ROWS - k
    row_right = row_stat[1:2] - row_sums
    row_d = row_stat[0:1] + row_sums / k - row_p
    row_e = row_s - (row_stat[0:1] + row_right / rest)
    n_left, n_right = count_p + k, rest + count_s
    n = n_left + n_right
    weight = n_left * n_right / (n * n)
    a, b = weight / n_left, weight / n_right
    coef_ref[0:8, :] = a
    coef_ref[8:16, :] = b
    vectors[0:8, :] = -a * row_sums / k
    vectors[8:16, :] = a * (count_p * k / n_left) * row_d
    vectors[16:24, :] = b * row_right / rest
    vectors[24:32, :] = -b * (rest * count_s / n_right) * row_e
    total = count_p + ROWS
    n = total + count_s
    row_d = row_stat[2:3] - row_p
    row_e = row_s - (row_p + row_d * (ROWS / total))
    coef_ref[16:24, :] = jnp.broadcast_to(1.0 / n, (8, WIDTH))
    vectors[32:WIDTH, :] = jnp.zeros((WIDTH - 32, WIDTH), F32)
    vectors[32:33, :] = row_stat[1:2] / -ROWS / n
    vectors[33:34, :] = (count_p * ROWS / total) / n * row_d
    vectors[34:35, :] = (total * count_s / n) / n * row_e
    turned_ref[...] = vectors[...].T

    columns = (
        (own_means_ref[0], own_means_ref[1]),
        (ahead_ref[core], behind_ref[away]),
        (far_ref[core], far_ref[away]),
        (ahead_ref[away], behind_ref[core]),
    )
    for u in range(8):
        r, lanes = u // 2, slice(WIDTH * (u % 2), WIDTH * (u % 2) + WIDTH)
        means = columns[r][u % 2]
        col_p, col_part_p = pooled(means, 0)
        col_s, col_part_s = pooled(means, 1)
        stat = stat_ref[r, :, lanes]
        col_left = sums_ref[r, :, lanes]
        col_right = stat[1:2] - col_left
        cols_ref[u, 0:8, :] = col_left
        cols_ref[u, 8:16, :] = stat[0:1] + col_left / k - col_p
        cols_ref[u, 16:24, :] = col_right
        cols_ref[u, 24:32, :] = col_s - (stat[0:1] + col_right / rest)
        col_d = stat[2:3] - col_p
        cols_ref[u, 32:40, :] = jnp.zeros((8, WIDTH), F32)
        cols_ref[u, 32:33, :] = stat[1:2]
        cols_ref[u, 33:34, :] = col_d
        cols_ref[u, 34:35, :] = col_s - (col_p + col_d * (ROWS / total))

        def between(row_part, col_part):
            return ROWS * lax.dot_general(
                row_part, col_part, TRANSPOSED, precision=HIGH, preferred_element_type=F32
            )

        before_ref[u] = between(row_part_p, col_part_p)
        after_ref[u] = gram_ref[r, :, lanes] + between(row_part_s, col_part_s)


def prep_terms(where, sums, gram, stat, own, ahead, behind, far, flags):
    square = array(8, WIDTH, WIDTH)
    return call(
        prep_kernel,
        "prep_terms",
        [where, sums, gram, stat, own, ahead, behind, far, flags],
        [array(WIDTH, WIDTH), array(8, 40, WIDTH), array(24, WIDTH), square, square],
        fetched=(1, 2, 3, 4, 8),
        stored=(0, 1, 2, 3, 4),
        scratch=[((WIDTH, WIDTH), F32)],
        us=4,
        grant=16,
    )


def load_near(ref, p_ref, s_ref):
    for g in range(8):
        p_ref[16 * g : 16 * g + 16, :] = ref[g, 0:16, :]
        s_ref[16 * g : 16 * g + 16, :] = ref[g, 16:32, :]


def load_far(ref, p_ref, s_ref):
    for q in range(BLOCKS):
        p_ref[4 * q : 4 * q + 4, :] = ref[q, 0:4, :]
        s_ref[4 * q : 4 * q + 4, :] = ref[q, 4:8, :]


def output_kernel(
    where_ref, back_ref, opposite_ref, next_ref, before_ref, left_hbm, prefix_hbm, suffix_hbm, cols_hbm, turned_hbm, coef_hbm,
    cusum_hbm, seg_hbm,
    left_ref, prefix_ref, suffix_ref, cols_ref, turned_ref, coef_ref, cusum_ref, seg_ref, p_ref, s_ref, sem, out_sem,
):
    loads = [
        pltpu.make_async_copy(source, target, sem.at[c])
        for c, (source, target) in enumerate(
            (
                (prefix_hbm, prefix_ref),
                (suffix_hbm, suffix_ref),
                (cols_hbm, cols_ref),
                (turned_hbm, turned_ref),
                (coef_hbm, coef_ref),
                (left_hbm, left_ref),
            )
        )
    ]
    for load in loads:
        load.start()
    held = where_ref[3]
    for load in loads[:5]:
        load.wait()

    def add(u, turn):
        prefix, suffix = p_ref[...], s_ref[...]
        if turn:
            prefix, suffix = prefix.T, suffix.T
        prefix_ref[u] = prefix_ref[u] + prefix
        suffix_ref[u] = suffix_ref[u] + suffix

    for u in range(4):
        load_near(back_ref.at[pl.ds(8 * u, 8)], p_ref, s_ref)
        add(u, False)
    load_far(back_ref.at[:, pl.ds(32, 8)], p_ref, s_ref)
    add(4 + held, False)
    load_far(opposite_ref, p_ref, s_ref)
    add(5 - held, True)
    load_near(next_ref, p_ref, s_ref)
    add(6, True)
    load_near(before_ref, p_ref, s_ref)
    add(7, True)

    def spread_out(row, count):
        return [
            jnp.broadcast_to(turned_ref[:, i : i + 1], (WIDTH, WIDTH))
            for i in range(row, 35, 8 if count == 4 else 1)
        ][:count]

    def lanes(u):
        return pl.ds(pl.multiple_of(where_ref[4 + u] * WIDTH, WIDTH), WIDTH)

    turned = spread_out(32, 3)
    for u in range(8):
        value = (prefix_ref[u] + suffix_ref[u]) * coef_ref[16:17, :]
        for i in range(3):
            value = value + turned[i] * cols_ref[u, 32 + i : 33 + i, :]
        seg_ref[0, :, lanes(u)] = value
    store = pltpu.make_async_copy(seg_ref, seg_hbm, out_sem.at[SPLITS])
    store.start()
    stores = [store]
    loads[5].wait()
    for j in range(SPLITS):
        turned = spread_out(j, 4)
        a, b = coef_ref[j : j + 1, :], coef_ref[8 + j : 9 + j, :]
        for u in range(8):
            half = WIDTH * (u % 2)
            value = (a + b) * left_ref[u // 2, j, :, half : half + WIDTH]
            value = value + a * prefix_ref[u] - b * suffix_ref[u]
            for i in range(4):
                value = value + turned[i] * cols_ref[u, 8 * i + j : 8 * i + j + 1, :]
            cusum_ref[0, j, :, lanes(u)] = value
        store = pltpu.make_async_copy(
            cusum_ref.at[:, pl.ds(j, 1)], cusum_hbm.at[:, pl.ds(j, 1)], out_sem.at[j]
        )
        store.start()
        stores.append(store)
    for store in stores:
        store.wait()


OUTPUTS = [array(1, SPLITS, WIDTH, CHIPS * PAIR), array(1, WIDTH, CHIPS * PAIR)]


def outputs(where, back, opposite, following, before, left, prefix, suffix, cols, turned, coef):
    blocks = [back, opposite, following, before]
    terms = [prefix, suffix, cols, turned, coef]
    buffers = [left, *terms, *OUTPUTS, array(WIDTH, WIDTH), array(WIDTH, WIDTH)]
    return pl.pallas_call(
        output_kernel,
        out_shape=OUTPUTS,
        grid=(1,),
        in_specs=[SM] + [whole(*value.shape) for value in blocks] + [HBM] * 6,
        out_specs=[HBM, HBM],
        scratch_shapes=[pltpu.VMEM(value.shape, F32) for value in buffers]
        + [pltpu.SemaphoreType.DMA((6,)), pltpu.SemaphoreType.DMA((SPLITS + 1,))],
        compiler_params=params(24),
        cost_estimate=cost(5),
        name="outputs",
    )(where, *blocks, left, *terms)


def window_kernel(
    where_ref, mine_ref, other_ref, gram_ref, stat_ref, total_ref,
    out_ref, cent_ref, flip_ref, sum_ref,
):
    halves = (
        (mine_ref, 0), (other_ref, 0), (mine_ref, HALO), (other_ref, 3 * HALO),
        (mine_ref, 2 * HALO), (other_ref, 2 * HALO), (other_ref, HALO), (mine_ref, 3 * HALO),
    )
    live = jnp.where(where_ref[0] > 0, 1.0, 0.0).astype(F32)
    core = where_ref[2]
    at = pl.multiple_of(core * WIDTH, WIDTH)
    off = pl.multiple_of((1 - core) * WIDTH, WIDTH)
    count = ROWS + live * HALO
    scale = wide(1.0 / jnp.full((1, WIDTH), count, F32))
    unbias = wide(1.0 / jnp.full((1, WIDTH), count - 1.0, F32))
    step = 256
    for r in range(CHIPS):
        lanes = (at, off) if r == 0 else (0, WIDTH)
        for (raw, row), lane in zip(halves[2 * r : 2 * r + 2], lanes):
            mean = stat_ref[r, 0:1, pl.ds(lane, WIDTH)]

            def shift(i, _, raw=raw, row=row, lane=lane, mean=mean):
                piece = (raw[pl.ds(row + i * step, step), :].astype(F32) - mean) * live
                cent_ref[pl.ds(i * step, step), pl.ds(lane, WIDTH)] = piece.astype(BF16)
                return 0

            lax.fori_loop(0, HALO // step, shift, 0, unroll=2)
        if r == 0:
            flip_ref[...] = cent_ref[:, pl.ds(at, WIDTH)].T
            flipped = flip_ref[...]
            row_sum = jnp.dot(flipped, jnp.ones((HALO, WIDTH), BF16), preferred_element_type=F32)
            sum_ref[...] = row_sum + total_ref[...]
        cent = cent_ref[...]
        halo = jnp.dot(flip_ref[...], cent, preferred_element_type=F32)
        col_sum = jnp.dot(jnp.ones((16, HALO), BF16), cent, preferred_element_type=F32)[0:1]
        col_sum = col_sum + stat_ref[r, 1:2, :]
        value = (halo + gram_ref[r] - wide(sum_ref[...]) * (col_sum * scale)) * unbias
        for c in range(2):
            lane = pl.multiple_of(where_ref[4 + 2 * r + c] * WIDTH, WIDTH)
            out_ref[0, :, pl.ds(lane, WIDTH)] = value[:, c * WIDTH : (c + 1) * WIDTH]


def to_chan(value, target):
    count = lax.axis_size("chan")
    return lax.ppermute(value, "chan", [(s, target(s) % count) for s in range(count)])


def exchange(value):
    return lax.all_to_all(value, "tm", 0, 0, tiled=True)


def after(value, *others):
    return lax.optimization_barrier((value, *others))[0]


def local(samples, candidates, segment_start):
    here, index = lax.axis_index("tm"), lax.axis_index("chan")
    chip, core = index // 2, index % 2
    nearby = [2 * chip, 2 * chip + 1]
    for step, side in ((1, core), (3, 1 - core), (2, core), (2, 1 - core), (1, 1 - core), (3, core)):
        nearby.append(2 * ((chip + step) % CHIPS) + side)
    held = jnp.where(chip < CHIPS // 2, 0, 1)
    where = jnp.stack([here, chip, core, held] + nearby).astype(jnp.int32)
    where = jnp.concatenate([where, candidates[0], segment_start])

    behind = to_chan(samples, lambda s: s + 2)
    ahead = to_chan(samples, lambda s: s - 2)
    other = to_chan(samples, lambda s: s ^ 1)
    prior = lax.ppermute(samples[ROWS - HALO :], "tm", [(b, b + 1) for b in range(BLOCKS - 1)])
    flip_shape, square = array(WIDTH, ROWS, dtype=BF16), array(WIDTH, WIDTH)
    left, sums, gram, stat, late_flipped, late_total, flipped, spread0, total, rider = call(
        first_kernel,
        "first_pair",
        [where, samples, other],
        ALL + [flip_shape, square, flip_shape, array(WIDTH, PAIR), square, array(8, WIDTH)],
        fetched=(1,),
        stored=(0, 1, 2, 3, 4, 5),
        scratch=[((ROWS, PAIR), BF16)],
    )
    behind, ahead, prior, flipped = lax.optimization_barrier((behind, ahead, prior, flipped))
    half = ROWS // 2
    far_low = to_chan(behind[:half], lambda s: s + 2)
    far_high = to_chan(ahead[half:], lambda s: s - 2)
    behind_other = to_chan(behind, lambda s: s ^ 1)
    ahead_other = to_chan(ahead, lambda s: s ^ 1)
    left, sums, gram, stat, spread1 = call(
        near_kernel,
        "near_pair",
        [where, ahead, behind_other, flipped, total],
        ALL + [array(WIDTH, PAIR)],
        stored=(0, 1, 2, 3),
        kept=(left, sums, gram, stat),
        pair=1,
        scratch=[((ROWS, PAIR), BF16)],
    )
    left, sums, gram, stat = call(
        side_kernel,
        "side_pair",
        [where, ahead_other, behind, flipped],
        ALL,
        stored=(0, 1, 2, 3),
        kept=(left, sums, gram, stat),
        pair=3,
        scratch=[((ROWS, PAIR), BF16)],
    )
    far_low, far_high, stat = lax.optimization_barrier((far_low, far_high, stat))
    far = jnp.concatenate([far_low, far_high], axis=0)
    far_other = to_chan(far, lambda s: s ^ 1)
    gram, stat, pieces, cent = call(
        far_kernel,
        "far_pair",
        [where, far, far_other, flipped, total, spread0, spread1, rider],
        ALL[2:] + [array(BLOCKS, 24, WIDTH), array(ROWS, PAIR, dtype=BF16)],
        stored=(0, 1, 3),
        kept=(gram, stat),
        pair=2,
        scratch=[((WIDTH, WIDTH), F32)],
        us=2,
    )
    arrived = exchange(pieces)

    left, sums = call(
        rest_kernel,
        "rest_left",
        [where, cent, late_flipped],
        ALL[:2],
        fetched=(1, 2),
        stored=(0, 1),
        kept=(left, sums),
        pair=2,
    )
    prior = after(prior, left)
    prior_behind = to_chan(prior, lambda s: s + 2)
    prior_ahead = to_chan(prior, lambda s: s - 2)
    arrived, prior_behind, prior_ahead = lax.optimization_barrier(
        (arrived, prior_behind, prior_ahead)
    )
    scanned, own_means, flags = call(
        scan_kernel,
        "scan_pieces",
        [arrived],
        [array(BLOCKS, 40, WIDTH), array(2, BLOCKS, WIDTH), array(BLOCKS, WIDTH)],
        stored=(0, 1, 2),
        us=1,
    )
    back = exchange(scanned)
    ahead_means = to_chan(own_means, lambda s: s - 2)
    behind_means = to_chan(own_means, lambda s: s + 2)
    far_means = to_chan(own_means, lambda s: s + 4)
    turned, cols, coef, prefix, suffix = prep_terms(
        where, sums, gram, stat, own_means, ahead_means, behind_means, far_means, flags
    )
    prior_behind, prior_ahead, _ = lax.optimization_barrier((prior_behind, prior_ahead, flags))
    half = HALO // 2
    mine = jnp.concatenate(
        [
            prior,
            prior_ahead,
            to_chan(prior_behind[:half], lambda s: s + 2),
            to_chan(prior_ahead[half:], lambda s: s - 2),
            prior_behind,
        ],
        axis=0,
    )
    window_cov = call(
        window_kernel,
        "window_output",
        [where, mine, to_chan(mine, lambda s: s ^ 1), gram, after(stat, coef), late_total],
        [array(1, WIDTH, CHIPS * PAIR)],
        fetched=(3, 4, 5),
        stored=(0,),
        scratch=[((HALO, PAIR), BF16), ((WIDTH, HALO), BF16), ((WIDTH, WIDTH), F32)],
    )[0]
    back, coef, window_cov = lax.optimization_barrier((back, coef, window_cov))
    before = to_chan(back[16:24, 0:32], lambda s: s + 2)
    following = to_chan(back[24:32, 0:32], lambda s: (s - 2) ^ 1)
    opposite = to_chan(back[:, 32:40], lambda s: s + 4 if s < 4 else (s - 4) ^ 1)
    cusum, segment_cov = outputs(
        where, back, opposite, following, before, left, prefix, suffix, cols, turned, coef
    )
    return window_cov, segment_cov, cusum


def solution(mesh):
    placed = (P("tm", "chan"), P("tm", None), P("tm"))
    return jax.shard_map(
        local,
        mesh=mesh,
        in_specs=placed,
        out_specs=(P("tm", "chan", None), P("tm", "chan", None), P("tm", None, "chan", None)),
        check_vma=False,
    )
```

```python
import jax
import jax.numpy as jnp
from jax import lax
from jax.experimental import pallas as pl
from jax.experimental.pallas import tpu as pltpu
from jax.sharding import PartitionSpec as P

F32, BF16 = jnp.float32, jnp.bfloat16
ROWS, HALO, WIDTH, BLOCKS, SPLITS, CHIPS = 2048, 1024, 128, 32, 8, 4
PAIR = 2 * WIDTH
HIGH = lax.Precision.HIGHEST
TRANSPOSED = (((0,), (0,)), ((), ()))
SM = pl.BlockSpec(memory_space=pltpu.SMEM)
HBM = pl.BlockSpec(memory_space=pltpu.HBM)
MIB = 2**20


def whole(*shape):
    return pl.BlockSpec(shape, lambda *_: (0,) * len(shape))


def array(*shape, dtype=F32):
    return jax.ShapeDtypeStruct(shape, dtype)


def params(grant):
    return pltpu.CompilerParams(
        vmem_limit_bytes=grant * MIB, dimension_semantics=("arbitrary",)
    )


def cost(microseconds):
    return pl.CostEstimate(
        flops=int(microseconds * 1e9), bytes_accessed=MIB, transcendentals=0
    )


def center_shard(raw_ref, out_ref, at):
    step = 256

    def add(i, total):
        piece = raw_ref[pl.ds(i * step, step), :].astype(F32)
        return total + jnp.sum(piece.reshape(step // 8, 8, WIDTH), axis=0)

    total = lax.fori_loop(0, ROWS // step, add, jnp.zeros((8, WIDTH), F32), unroll=2)
    mean = jnp.sum(total, axis=0, keepdims=True) / ROWS

    def shift(i, _):
        piece = raw_ref[pl.ds(i * step, step), :].astype(F32) - mean
        out_ref[pl.ds(i * step, step), pl.ds(at, WIDTH)] = piece.astype(BF16)
        return 0

    lax.fori_loop(0, ROWS // step, shift, 0, unroll=2)
    return mean


def center_pair(first_ref, second_ref, at, off, cent_ref, stat_ref):
    stat_ref[0] = jnp.zeros((8, PAIR), F32)
    stat_ref[0, 0:1, pl.ds(at, WIDTH)] = center_shard(first_ref, cent_ref, at)
    stat_ref[0, 0:1, pl.ds(off, WIDTH)] = center_shard(second_ref, cent_ref, off)
    total = jnp.dot(jnp.ones((16, ROWS), BF16), cent_ref[...], preferred_element_type=F32)[0:1]
    stat_ref[0, 1:2, :] = total
    stat_ref[0, 2:3, :] = stat_ref[0, 0:1, :] + total / ROWS


def turned_dot(left, right):
    return lax.dot_general(left, right, TRANSPOSED, preferred_element_type=F32)


def wide(value):
    return jnp.concatenate([value, value], axis=1)


def left_part(where_ref, flipped, cent_ref, left_ref, sums_ref, block=0):
    index = lax.broadcasted_iota(jnp.int32, (16, ROWS), 0)
    place = lax.broadcasted_iota(jnp.int32, (16, ROWS), 1)
    limit = jnp.zeros((16, ROWS), jnp.int32)
    for j in range(SPLITS):
        limit = jnp.where(index == j, where_ref[12 + j], limit)
    masks = jnp.where(place < limit, 1.0, 0.0).astype(BF16)
    cent = cent_ref[...]
    sums_ref[block] = jnp.dot(masks, cent, preferred_element_type=F32)[0:8]
    for i in range(SPLITS // 4):
        kept = jnp.concatenate([flipped * masks[j : j + 1, :] for j in range(4 * i, 4 * i + 4)], axis=0)
        part = jnp.dot(kept, cent, preferred_element_type=F32)
        for j in range(4):
            for c in range(2):
                rows, lanes = slice(j * WIDTH, (j + 1) * WIDTH), slice(c * WIDTH, (c + 1) * WIDTH)
                left_ref[c, 4 * i + j] = part[rows, lanes]


def first_kernel(
    where_ref, mine_ref, other_ref,
    left_ref, sums_ref, gram_ref, stat_ref, flip_hbm, total_hbm, flip_ref, spread_ref, total_ref, rider_ref, cent_ref,
):
    core = where_ref[2]
    at = pl.multiple_of(core * WIDTH, WIDTH)
    off = pl.multiple_of((1 - core) * WIDTH, WIDTH)
    center_pair(mine_ref, other_ref, at, off, cent_ref, stat_ref)
    rider_ref[...] = jnp.zeros((8, WIDTH), F32)
    rider_ref[0:1, :] = stat_ref[0, 2:3, 0:WIDTH]
    rider_ref[1:2, :] = stat_ref[0, 2:3, WIDTH:PAIR]
    rider_ref[2:3, :] = jnp.full((1, WIDTH), where_ref[20], jnp.int32).astype(F32)
    flip_ref[...] = cent_ref[:, pl.ds(at, WIDTH)].T
    flipped = flip_ref[...]
    flip_hbm[...] = flipped
    gram = jnp.dot(flipped, cent_ref[...], preferred_element_type=F32)
    gram_ref[0] = gram
    total = jnp.dot(flipped, jnp.ones((ROWS, WIDTH), BF16), preferred_element_type=F32)
    total_ref[...] = total
    total_hbm[...] = total
    spread_ref[...] = gram - wide(total) * (stat_ref[0, 1:2, :] / ROWS)
    left_part(where_ref, flipped, cent_ref, left_ref, sums_ref)


def near_kernel(
    where_ref, first_ref, second_ref, flip_ref, total_ref,
    left_ref, sums_ref, gram_ref, stat_ref, spread_ref, cent_ref,
):
    center_pair(first_ref, second_ref, 0, WIDTH, cent_ref, stat_ref)
    flipped = flip_ref[...]
    gram = jnp.dot(flipped, cent_ref[...], preferred_element_type=F32)
    gram_ref[0] = gram
    spread_ref[...] = gram - wide(total_ref[...]) * (stat_ref[0, 1:2, :] / ROWS)
    left_part(where_ref, flipped, cent_ref, left_ref, sums_ref)


def side_kernel(where_ref, first_ref, second_ref, flip_ref, gram_ref, stat_ref, cent_ref):
    center_pair(first_ref, second_ref, 0, WIDTH, cent_ref, stat_ref)
    gram_ref[0] = jnp.dot(flip_ref[...], cent_ref[...], preferred_element_type=F32)


def far_kernel(
    where_ref, first_ref, second_ref, flip_ref, total_ref, spread0_ref, spread1_ref, rider_ref,
    gram_ref, stat_ref, out_ref, cent_ref, held_ref,
):
    rider = rider_ref[0:4, :]
    for q in range(BLOCKS):
        spread, lane = ((spread0_ref, spread1_ref)[q // 16], WIDTH * (q // 8 % 2))
        row = 16 * (q % 8)
        out_ref[q, 0:16, :] = spread[row : row + 16, lane : lane + WIDTH]
        out_ref[q, 20:24, :] = rider
    center_pair(first_ref, second_ref, 0, WIDTH, cent_ref, stat_ref)
    gram = jnp.dot(flip_ref[...], cent_ref[...], preferred_element_type=F32)
    gram_ref[0] = gram
    spread = gram - wide(total_ref[...]) * (stat_ref[0, 1:2, :] / ROWS)
    held_ref[...] = jnp.where(where_ref[3] == 0, spread[:, 0:WIDTH], spread[:, WIDTH:PAIR])
    for q in range(BLOCKS):
        out_ref[q, 16:20, :] = held_ref[4 * q : 4 * q + 4, :]


def rest_kernel(where_ref, far_ref, side_ref, flip_ref, far_left_ref, side_left_ref, sums_ref):
    flipped = flip_ref[...]
    left_part(where_ref, flipped, far_ref, far_left_ref, sums_ref, 0)
    left_part(where_ref, flipped, side_ref, side_left_ref, sums_ref, 1)


ALL = [
    array(CHIPS, 8, PAIR),
    array(CHIPS, WIDTH, PAIR),
    array(CHIPS, 8, PAIR),
]


STORE = array(96, 8, WIDTH, WIDTH)
SHARD_PAIR = (2, SPLITS, WIDTH, WIDTH)


def call(
    kernel, name, inputs, outputs, *, store=None, puts=(), fetched=(), stored=(), kept=(),
    pair=0, span=1, scratch=(), us=3, grant=24,
):
    kept = (*([store] if store is not None else []), *kept)
    count, made, first = len(inputs), len(outputs), 1 if puts else 0
    sliced = [out in ALL for out in outputs]
    sizes = [(span, *out.shape[1:]) if cut else out.shape for out, cut in zip(outputs, sliced)]
    buffers = [pltpu.VMEM(inputs[i].shape, inputs[i].dtype) for i in fetched]
    buffers += [pltpu.VMEM(shape, F32) for shape, _ in puts]
    buffers += [pltpu.VMEM(sizes[i], outputs[i].dtype) for i in stored]

    def body(*refs):
        ins, refs = list(refs[:count]), refs[count + len(kept) :]
        slots, outs, refs = refs[:first], list(refs[first : first + made]), refs[first + made :]
        own, buffer, sem = refs[: len(scratch)], refs[len(scratch) : -1], refs[-1]
        copies = []
        for c, i in enumerate(fetched):
            copies.append(pltpu.make_async_copy(ins[i], buffer[c], sem.at[c]))
            ins[i] = buffer[c]
        for copy in copies:
            copy.start()
        for copy in copies:
            copy.wait()
        copies, mine = [], []
        for c, (_, place) in enumerate(puts, len(fetched)):
            copies.append(pltpu.make_async_copy(buffer[c], slots[0].at[place], sem.at[c]))
            mine.append(buffer[c])
        for c, i in enumerate(stored, len(fetched) + len(puts)):
            target = outs[i].at[pl.ds(pair, span)] if sliced[i] else outs[i]
            copies.append(pltpu.make_async_copy(buffer[c], target, sem.at[c]))
            outs[i] = buffer[c]
        kernel(*ins, *mine, *outs, *own)
        for copy in copies:
            copy.start()
        for copy in copies:
            copy.wait()

    ins = [SM if value.dtype == jnp.int32 else whole(*value.shape) for value in inputs]
    for i in fetched:
        ins[i] = HBM
    outs = [HBM if i in stored else whole(*out.shape) for i, out in enumerate(outputs)]
    aliased = range(first if store is None else 0, first + len(kept))
    return pl.pallas_call(
        body,
        out_shape=[STORE] * first + outputs,
        grid=(1,),
        in_specs=ins + [HBM] * len(kept),
        out_specs=[HBM] * first + outs,
        input_output_aliases={count + i: out for i, out in zip(range(len(kept)), aliased)},
        scratch_shapes=[pltpu.VMEM(shape, dtype) for shape, dtype in scratch]
        + buffers
        + [pltpu.SemaphoreType.DMA((max(len(buffers), 1),))],
        compiler_params=params(grant),
        cost_estimate=cost(us),
        name=name,
    )(*inputs, *kept)


def scan_kernel(arrived_ref, both_ref, means_ref, flags_ref):
    for b in range(BLOCKS):
        rider = arrived_ref[b, 16:24, :]
        means_ref[0, b : b + 1, :] = rider[4:5, :]
        means_ref[1, b : b + 1, :] = rider[5:6, :]
        flags_ref[b : b + 1, :] = rider[6:7, :]
    scan(arrived_ref, flags_ref, both_ref, 0, 16, 0)
    scan(arrived_ref, flags_ref, both_ref, 16, 4, 32)


def scan(arrived_ref, flags_ref, both_ref, row, size, at):
    zero = jnp.zeros((size, WIDTH), F32)
    running = zero
    for b in range(BLOCKS):
        begins = flags_ref[b : b + 1, :] > 0.5
        running = jnp.where(begins, zero, running)
        both_ref[b, at : at + size, :] = running
        running = running + arrived_ref[b, row : row + size, :]
    running = zero
    for b in reversed(range(BLOCKS)):
        begins = flags_ref[b : b + 1, :] > 0.5
        both_ref[b, at + size : at + 2 * size, :] = running
        running = jnp.where(begins, zero, running + arrived_ref[b, row : row + size, :])


def prep_kernel(
    where_ref, sums_ref, gram_ref, stat_ref, own_means_ref, ahead_ref, behind_ref, far_ref, flags_ref,
    turned_ref, cols_ref, coef_ref, before_ref, after_ref, vectors,
):
    here = where_ref[0]
    core = where_ref[2]
    away = 1 - core
    flags = flags_ref[...]
    spot = lax.broadcasted_iota(jnp.int32, (BLOCKS, WIDTH), 0)
    low = lax.broadcasted_iota(jnp.int32, (BLOCKS, BLOCKS), 1)
    high = lax.broadcasted_iota(jnp.int32, (BLOCKS, BLOCKS), 0)
    upto = jnp.dot((low <= high).astype(F32), flags, preferred_element_type=F32)
    mine = jnp.sum(jnp.where(spot <= here, flags, 0.0), axis=0, keepdims=True)
    same = jnp.abs(upto - mine) < 0.5
    masks = [
        jnp.where(same & (spot < here), 1.0, 0.0),
        jnp.where(same & (spot > here), 1.0, 0.0),
    ]
    totals = [jnp.sum(mask, axis=0, keepdims=True) for mask in masks]
    count_p, count_s = totals[0] * ROWS, totals[1] * ROWS

    def pooled(means, side):
        mask = masks[side]
        mean = jnp.sum(means * mask, axis=0, keepdims=True) / jnp.maximum(totals[side], 1.0)
        return mean, (means - mean) * mask

    def pick(value):
        return jnp.where(core == 0, value[:, 0:WIDTH], value[:, WIDTH:PAIR])

    row_means = own_means_ref[core]
    row_p, row_part_p = pooled(row_means, 0)
    row_s, row_part_s = pooled(row_means, 1)
    row_stat = pick(stat_ref[0])
    row_sums = pick(sums_ref[0])

    index = lax.broadcasted_iota(jnp.int32, (SPLITS, WIDTH), 0)
    k = jnp.zeros((SPLITS, WIDTH), jnp.int32)
    for j in range(SPLITS):
        k = jnp.where(index == j, where_ref[12 + j], k)
    k = k.astype(F32)
    rest = ROWS - k
    row_right = row_stat[1:2] - row_sums
    row_d = row_stat[0:1] + row_sums / k - row_p
    row_e = row_s - (row_stat[0:1] + row_right / rest)
    n_left, n_right = count_p + k, rest + count_s
    n = n_left + n_right
    weight = n_left * n_right / (n * n)
    a, b = weight / n_left, weight / n_right
    coef_ref[0:8, :] = a
    coef_ref[8:16, :] = b
    vectors[0:8, :] = -a * row_sums / k
    vectors[8:16, :] = a * (count_p * k / n_left) * row_d
    vectors[16:24, :] = b * row_right / rest
    vectors[24:32, :] = -b * (rest * count_s / n_right) * row_e
    total = count_p + ROWS
    n = total + count_s
    row_d = row_stat[2:3] - row_p
    row_e = row_s - (row_p + row_d * (ROWS / total))
    coef_ref[16:24, :] = jnp.broadcast_to(1.0 / n, (8, WIDTH))
    vectors[32:WIDTH, :] = jnp.zeros((WIDTH - 32, WIDTH), F32)
    vectors[32:33, :] = row_stat[1:2] / -ROWS / n
    vectors[33:34, :] = (count_p * ROWS / total) / n * row_d
    vectors[34:35, :] = (total * count_s / n) / n * row_e
    turned_ref[...] = vectors[...].T

    columns = (
        (own_means_ref[0], own_means_ref[1]),
        (ahead_ref[core], behind_ref[away]),
        (far_ref[core], far_ref[away]),
        (ahead_ref[away], behind_ref[core]),
    )
    for u in range(8):
        r, lanes = u // 2, slice(WIDTH * (u % 2), WIDTH * (u % 2) + WIDTH)
        means = columns[r][u % 2]
        col_p, col_part_p = pooled(means, 0)
        col_s, col_part_s = pooled(means, 1)
        stat = stat_ref[r, :, lanes]
        col_left = sums_ref[r, :, lanes]
        col_right = stat[1:2] - col_left
        cols_ref[u, 0:8, :] = col_left
        cols_ref[u, 8:16, :] = stat[0:1] + col_left / k - col_p
        cols_ref[u, 16:24, :] = col_right
        cols_ref[u, 24:32, :] = col_s - (stat[0:1] + col_right / rest)
        col_d = stat[2:3] - col_p
        cols_ref[u, 32:40, :] = jnp.zeros((8, WIDTH), F32)
        cols_ref[u, 32:33, :] = stat[1:2]
        cols_ref[u, 33:34, :] = col_d
        cols_ref[u, 34:35, :] = col_s - (col_p + col_d * (ROWS / total))

        def between(row_part, col_part):
            return ROWS * lax.dot_general(
                row_part, col_part, TRANSPOSED, precision=HIGH, preferred_element_type=F32
            )

        before_ref[u] = between(row_part_p, col_part_p)
        after_ref[u] = gram_ref[r, :, lanes] + between(row_part_s, col_part_s)


def prep_terms(where, sums, gram, stat, own, ahead, behind, far, flags, store):
    square = (8, WIDTH, WIDTH)
    return call(
        prep_kernel,
        "prep_terms",
        [where, sums, gram, stat, own, ahead, behind, far, flags],
        [],
        store=store,
        puts=(
            ((WIDTH, WIDTH), (11, 0)),
            ((8, 40, WIDTH), (10, slice(None), pl.ds(0, 40))),
            ((24, WIDTH), (11, 1, pl.ds(0, 24))),
            (square, 8),
            (square, 9),
        ),
        fetched=(1, 2, 3, 4, 8),
        scratch=[((WIDTH, WIDTH), F32)],
        us=0.1,
        grant=16,
    )[0]


def load_near(ref, p_ref, s_ref):
    for g in range(8):
        p_ref[16 * g : 16 * g + 16, :] = ref[g, 0:16, :]
        s_ref[16 * g : 16 * g + 16, :] = ref[g, 16:32, :]


def load_far(ref, p_ref, s_ref):
    for q in range(BLOCKS):
        p_ref[4 * q : 4 * q + 4, :] = ref[q, 0:4, :]
        s_ref[4 * q : 4 * q + 4, :] = ref[q, 4:8, :]


def output_kernel(
    where_ref, back_ref, opposite_ref, next_ref, before_ref, store_hbm, cusum_hbm, seg_hbm,
    left_ref, prefix_ref, suffix_ref, cols_ref, turned_ref, coef_ref, cusum_ref, seg_ref, p_ref, s_ref, sem, out_sem,
):
    loads = [
        pltpu.make_async_copy(source, target, sem.at[c])
        for c, (source, target) in enumerate(
            (
                (store_hbm.at[8], prefix_ref),
                (store_hbm.at[9], suffix_ref),
                (store_hbm.at[10, :, pl.ds(0, 40)], cols_ref),
                (store_hbm.at[11, 0], turned_ref),
                (store_hbm.at[11, 1, pl.ds(0, 24)], coef_ref),
                (store_hbm.at[pl.ds(0, 8)], left_ref),
            )
        )
    ]
    for load in loads:
        load.start()
    held = where_ref[3]
    for load in loads[:5]:
        load.wait()

    def add(u, turn):
        prefix, suffix = p_ref[...], s_ref[...]
        if turn:
            prefix, suffix = prefix.T, suffix.T
        prefix_ref[u] = prefix_ref[u] + prefix
        suffix_ref[u] = suffix_ref[u] + suffix

    for u in range(4):
        load_near(back_ref.at[pl.ds(8 * u, 8)], p_ref, s_ref)
        add(u, False)
    load_far(back_ref.at[:, pl.ds(32, 8)], p_ref, s_ref)
    add(4 + held, False)
    load_far(opposite_ref, p_ref, s_ref)
    add(5 - held, True)
    load_near(next_ref, p_ref, s_ref)
    add(6, True)
    load_near(before_ref, p_ref, s_ref)
    add(7, True)

    def spread_out(row, count):
        return [
            jnp.broadcast_to(turned_ref[:, i : i + 1], (WIDTH, WIDTH))
            for i in range(row, 35, 8 if count == 4 else 1)
        ][:count]

    def lanes(u):
        return pl.ds(pl.multiple_of(where_ref[4 + u] * WIDTH, WIDTH), WIDTH)

    turned = spread_out(32, 3)
    for u in range(8):
        value = (prefix_ref[u] + suffix_ref[u]) * coef_ref[16:17, :]
        for i in range(3):
            value = value + turned[i] * cols_ref[u, 32 + i : 33 + i, :]
        seg_ref[0, :, lanes(u)] = value
    store = pltpu.make_async_copy(seg_ref, seg_hbm, out_sem.at[SPLITS])
    store.start()
    stores = [store]
    loads[5].wait()
    for j in range(SPLITS):
        turned = spread_out(j, 4)
        a, b = coef_ref[j : j + 1, :], coef_ref[8 + j : 9 + j, :]
        for u in range(8):
            value = (a + b) * left_ref[u, j]
            value = value + a * prefix_ref[u] - b * suffix_ref[u]
            for i in range(4):
                value = value + turned[i] * cols_ref[u, 8 * i + j : 8 * i + j + 1, :]
            cusum_ref[0, j, :, lanes(u)] = value
        store = pltpu.make_async_copy(
            cusum_ref.at[:, pl.ds(j, 1)], cusum_hbm.at[:, pl.ds(j, 1)], out_sem.at[j]
        )
        store.start()
        stores.append(store)
    for store in stores:
        store.wait()


OUTPUTS = [array(1, SPLITS, WIDTH, CHIPS * PAIR), array(1, WIDTH, CHIPS * PAIR)]


def outputs(where, back, opposite, following, before, store):
    blocks = [back, opposite, following, before]
    square = array(8, WIDTH, WIDTH)
    buffers = [array(8, SPLITS, WIDTH, WIDTH), square, square, array(8, 40, WIDTH)]
    buffers += [array(WIDTH, WIDTH), array(24, WIDTH), *OUTPUTS, array(WIDTH, WIDTH), array(WIDTH, WIDTH)]
    return pl.pallas_call(
        output_kernel,
        out_shape=OUTPUTS,
        grid=(1,),
        in_specs=[SM] + [whole(*value.shape) for value in blocks] + [HBM],
        out_specs=[HBM, HBM],
        scratch_shapes=[pltpu.VMEM(value.shape, F32) for value in buffers]
        + [pltpu.SemaphoreType.DMA((6,)), pltpu.SemaphoreType.DMA((SPLITS + 1,))],
        compiler_params=params(24),
        cost_estimate=cost(5),
        name="outputs",
    )(where, *blocks, store)


def window_kernel(
    where_ref, mine_ref, other_ref, gram_ref, stat_ref, total_ref,
    out_ref, cent_ref, flip_ref, sum_ref,
):
    halves = (
        (mine_ref, 0), (other_ref, 0), (mine_ref, HALO), (other_ref, 3 * HALO),
        (mine_ref, 2 * HALO), (other_ref, 2 * HALO), (other_ref, HALO), (mine_ref, 3 * HALO),
    )
    live = jnp.where(where_ref[0] > 0, 1.0, 0.0).astype(F32)
    core = where_ref[2]
    at = pl.multiple_of(core * WIDTH, WIDTH)
    off = pl.multiple_of((1 - core) * WIDTH, WIDTH)
    count = ROWS + live * HALO
    scale = wide(1.0 / jnp.full((1, WIDTH), count, F32))
    unbias = wide(1.0 / jnp.full((1, WIDTH), count - 1.0, F32))
    step = 256
    for r in range(CHIPS):
        lanes = (at, off) if r == 0 else (0, WIDTH)
        for (raw, row), lane in zip(halves[2 * r : 2 * r + 2], lanes):
            mean = stat_ref[r, 0:1, pl.ds(lane, WIDTH)]

            def shift(i, _, raw=raw, row=row, lane=lane, mean=mean):
                piece = (raw[pl.ds(row + i * step, step), :].astype(F32) - mean) * live
                cent_ref[pl.ds(i * step, step), pl.ds(lane, WIDTH)] = piece.astype(BF16)
                return 0

            lax.fori_loop(0, HALO // step, shift, 0, unroll=2)
        if r == 0:
            flip_ref[...] = cent_ref[:, pl.ds(at, WIDTH)].T
            flipped = flip_ref[...]
            row_sum = jnp.dot(flipped, jnp.ones((HALO, WIDTH), BF16), preferred_element_type=F32)
            sum_ref[...] = row_sum + total_ref[...]
        cent = cent_ref[...]
        halo = jnp.dot(flip_ref[...], cent, preferred_element_type=F32)
        col_sum = jnp.dot(jnp.ones((16, HALO), BF16), cent, preferred_element_type=F32)[0:1]
        col_sum = col_sum + stat_ref[r, 1:2, :]
        value = (halo + gram_ref[r] - wide(sum_ref[...]) * (col_sum * scale)) * unbias
        for c in range(2):
            lane = pl.multiple_of(where_ref[4 + 2 * r + c] * WIDTH, WIDTH)
            out_ref[0, :, pl.ds(lane, WIDTH)] = value[:, c * WIDTH : (c + 1) * WIDTH]


def to_chan(value, target):
    count = lax.axis_size("chan")
    return lax.ppermute(value, "chan", [(s, target(s) % count) for s in range(count)])


def exchange(value):
    return lax.all_to_all(value, "tm", 0, 0, tiled=True)


def after(value, *others):
    return lax.optimization_barrier((value, *others))[0]


def local(samples, candidates, segment_start):
    here, index = lax.axis_index("tm"), lax.axis_index("chan")
    chip, core = index // 2, index % 2
    nearby = [2 * chip, 2 * chip + 1]
    for step, side in ((1, core), (3, 1 - core), (2, core), (2, 1 - core), (1, 1 - core), (3, core)):
        nearby.append(2 * ((chip + step) % CHIPS) + side)
    held = jnp.where(chip < CHIPS // 2, 0, 1)
    where = jnp.stack([here, chip, core, held] + nearby).astype(jnp.int32)
    where = jnp.concatenate([where, candidates[0], segment_start])

    behind = to_chan(samples, lambda s: s + 2)
    ahead = to_chan(samples, lambda s: s - 2)
    other = to_chan(samples, lambda s: s ^ 1)
    prior = lax.ppermute(samples[ROWS - HALO :], "tm", [(b, b + 1) for b in range(BLOCKS - 1)])
    flip_shape, square = array(WIDTH, ROWS, dtype=BF16), array(WIDTH, WIDTH)
    store, sums, gram, stat, late_flipped, late_total, flipped, spread0, total, rider = call(
        first_kernel,
        "first_pair",
        [where, samples, other],
        ALL + [flip_shape, square, flip_shape, array(WIDTH, PAIR), square, array(8, WIDTH)],
        puts=((SHARD_PAIR, pl.ds(0, 2)),),
        fetched=(1,),
        stored=(0, 1, 2, 3, 4),
        scratch=[((ROWS, PAIR), BF16)],
    )
    behind, ahead, prior, flipped = lax.optimization_barrier((behind, ahead, prior, flipped))
    half = ROWS // 2
    far_low = to_chan(behind[:half], lambda s: s + 2)
    far_high = to_chan(ahead[half:], lambda s: s - 2)
    behind_other = to_chan(behind, lambda s: s ^ 1)
    ahead_other = to_chan(ahead, lambda s: s ^ 1)
    store, sums, gram, stat, spread1 = call(
        near_kernel,
        "near_pair",
        [where, ahead, behind_other, flipped, total],
        ALL + [array(WIDTH, PAIR)],
        store=store,
        puts=((SHARD_PAIR, pl.ds(2, 2)),),
        stored=(0, 1, 2),
        kept=(sums, gram, stat),
        pair=1,
        scratch=[((ROWS, PAIR), BF16)],
    )
    cent_shape = array(ROWS, PAIR, dtype=BF16)
    gram, stat, side = call(
        side_kernel,
        "side_pair",
        [where, ahead_other, behind, flipped],
        ALL[1:] + [cent_shape],
        stored=(0, 1),
        kept=(gram, stat),
        pair=3,
        us=0.1,
    )
    far_low, far_high, stat = lax.optimization_barrier((far_low, far_high, stat))
    far = jnp.concatenate([far_low, far_high], axis=0)
    far_other = to_chan(far, lambda s: s ^ 1)
    gram, stat, pieces, cent = call(
        far_kernel,
        "far_pair",
        [where, far, far_other, flipped, total, spread0, spread1, rider],
        ALL[1:] + [array(BLOCKS, 24, WIDTH), cent_shape],
        stored=(0, 1, 3),
        kept=(gram, stat),
        pair=2,
        scratch=[((WIDTH, WIDTH), F32)],
        us=0.1,
    )
    arrived = exchange(pieces)

    store, sums = call(
        rest_kernel,
        "rest_left",
        [where, cent, side, late_flipped],
        ALL[:1],
        store=store,
        puts=((SHARD_PAIR, pl.ds(4, 2)), (SHARD_PAIR, pl.ds(6, 2))),
        fetched=(1, 3),
        stored=(0,),
        kept=(sums,),
        pair=2,
        span=2,
        us=4,
    )
    prior = after(prior, sums)
    prior_behind = to_chan(prior, lambda s: s + 2)
    prior_ahead = to_chan(prior, lambda s: s - 2)
    arrived, prior_behind, prior_ahead = lax.optimization_barrier(
        (arrived, prior_behind, prior_ahead)
    )
    scanned, own_means, flags = call(
        scan_kernel,
        "scan_pieces",
        [arrived],
        [array(BLOCKS, 40, WIDTH), array(2, BLOCKS, WIDTH), array(BLOCKS, WIDTH)],
        stored=(0, 1, 2),
        us=1,
    )
    back = exchange(scanned)
    ahead_means = to_chan(own_means, lambda s: s - 2)
    behind_means = to_chan(own_means, lambda s: s + 2)
    far_means = to_chan(own_means, lambda s: s + 4)
    store = prep_terms(
        where, sums, gram, stat, own_means, ahead_means, behind_means, far_means, flags, store
    )
    prior_behind, prior_ahead, _ = lax.optimization_barrier((prior_behind, prior_ahead, flags))
    half = HALO // 2
    mine = jnp.concatenate(
        [
            prior,
            prior_ahead,
            to_chan(prior_behind[:half], lambda s: s + 2),
            to_chan(prior_ahead[half:], lambda s: s - 2),
            prior_behind,
        ],
        axis=0,
    )
    window_cov = call(
        window_kernel,
        "window_output",
        [where, mine, to_chan(mine, lambda s: s ^ 1), gram, stat, late_total],
        [array(1, WIDTH, CHIPS * PAIR)],
        fetched=(3, 4, 5),
        stored=(0,),
        scratch=[((HALO, PAIR), BF16), ((WIDTH, HALO), BF16), ((WIDTH, WIDTH), F32)],
        us=0.1,
    )[0]
    back, store, window_cov = lax.optimization_barrier((back, store, window_cov))
    before = to_chan(back[16:24, 0:32], lambda s: s + 2)
    following = to_chan(back[24:32, 0:32], lambda s: (s - 2) ^ 1)
    opposite = to_chan(back[:, 32:40], lambda s: s + 4 if s < 4 else (s - 4) ^ 1)
    cusum, segment_cov = outputs(
        where, back, opposite, following, before, store
    )
    return window_cov, segment_cov, cusum


def solution(mesh):
    placed = (P("tm", "chan"), P("tm", None), P("tm"))
    return jax.shard_map(
        local,
        mesh=mesh,
        in_specs=placed,
        out_specs=(P("tm", "chan", None), P("tm", "chan", None), P("tm", None, "chan", None)),
        check_vma=False,
    )
```

```python
import jax
import jax.numpy as jnp
from jax import lax
from jax.experimental import pallas as pl
from jax.experimental.pallas import tpu as pltpu
from jax.sharding import PartitionSpec as P

F32, BF16 = jnp.float32, jnp.bfloat16
ROWS, HALO, WIDTH, BLOCKS, SPLITS, CHIPS = 2048, 1024, 128, 32, 8, 4
PAIR = 2 * WIDTH
HIGH = lax.Precision.HIGHEST
TRANSPOSED = (((0,), (0,)), ((), ()))
SM = pl.BlockSpec(memory_space=pltpu.SMEM)
HBM = pl.BlockSpec(memory_space=pltpu.HBM)
MIB = 2**20


def whole(*shape):
    return pl.BlockSpec(shape, lambda *_: (0,) * len(shape))


def array(*shape, dtype=F32):
    return jax.ShapeDtypeStruct(shape, dtype)


def params(grant):
    return pltpu.CompilerParams(
        vmem_limit_bytes=grant * MIB, dimension_semantics=("arbitrary",)
    )


def cost(microseconds):
    return pl.CostEstimate(
        flops=int(microseconds * 1e9), bytes_accessed=MIB, transcendentals=0
    )


def center_shard(raw_ref, out_ref, at):
    step = 256

    def add(i, total):
        piece = raw_ref[pl.ds(i * step, step), :].astype(F32)
        return total + jnp.sum(piece.reshape(step // 8, 8, WIDTH), axis=0)

    total = lax.fori_loop(0, ROWS // step, add, jnp.zeros((8, WIDTH), F32), unroll=2)
    mean = jnp.sum(total, axis=0, keepdims=True) / ROWS

    def shift(i, _):
        piece = raw_ref[pl.ds(i * step, step), :].astype(F32) - mean
        out_ref[pl.ds(i * step, step), pl.ds(at, WIDTH)] = piece.astype(BF16)
        return 0

    lax.fori_loop(0, ROWS // step, shift, 0, unroll=2)
    return mean


def center_pair(first_ref, second_ref, at, off, cent_ref, stat_ref):
    stat_ref[0] = jnp.zeros((8, PAIR), F32)
    stat_ref[0, 0:1, pl.ds(at, WIDTH)] = center_shard(first_ref, cent_ref, at)
    stat_ref[0, 0:1, pl.ds(off, WIDTH)] = center_shard(second_ref, cent_ref, off)
    total = jnp.dot(jnp.ones((16, ROWS), BF16), cent_ref[...], preferred_element_type=F32)[0:1]
    stat_ref[0, 1:2, :] = total
    stat_ref[0, 2:3, :] = stat_ref[0, 0:1, :] + total / ROWS


def turned_dot(left, right):
    return lax.dot_general(left, right, TRANSPOSED, preferred_element_type=F32)


def wide(value):
    return jnp.concatenate([value, value], axis=1)


def left_part(where_ref, flipped, cent_ref, left_ref, sums_ref, block=0):
    index = lax.broadcasted_iota(jnp.int32, (16, ROWS), 0)
    place = lax.broadcasted_iota(jnp.int32, (16, ROWS), 1)
    limit = jnp.zeros((16, ROWS), jnp.int32)
    for j in range(SPLITS):
        limit = jnp.where(index == j, where_ref[12 + j], limit)
    masks = jnp.where(place < limit, 1.0, 0.0).astype(BF16)
    cent = cent_ref[...]
    sums_ref[block] = jnp.dot(masks, cent, preferred_element_type=F32)[0:8]
    for i in range(SPLITS // 4):
        kept = jnp.concatenate([flipped * masks[j : j + 1, :] for j in range(4 * i, 4 * i + 4)], axis=0)
        part = jnp.dot(kept, cent, preferred_element_type=F32)
        for j in range(4):
            for c in range(2):
                rows, lanes = slice(j * WIDTH, (j + 1) * WIDTH), slice(c * WIDTH, (c + 1) * WIDTH)
                left_ref[c, 4 * i + j] = part[rows, lanes]


def first_kernel(
    where_ref, mine_ref, other_ref,
    left_ref, sums_ref, gram_ref, stat_ref, flip_hbm, total_hbm, flip_ref, spread_ref, total_ref, rider_ref, cent_ref,
):
    core = where_ref[2]
    at = pl.multiple_of(core * WIDTH, WIDTH)
    off = pl.multiple_of((1 - core) * WIDTH, WIDTH)
    center_pair(mine_ref, other_ref, at, off, cent_ref, stat_ref)
    rider_ref[...] = jnp.zeros((8, WIDTH), F32)
    rider_ref[0:1, :] = stat_ref[0, 2:3, 0:WIDTH]
    rider_ref[1:2, :] = stat_ref[0, 2:3, WIDTH:PAIR]
    rider_ref[2:3, :] = jnp.full((1, WIDTH), where_ref[20], jnp.int32).astype(F32)
    flip_ref[...] = cent_ref[:, pl.ds(at, WIDTH)].T
    flipped = flip_ref[...]
    flip_hbm[...] = flipped
    gram = jnp.dot(flipped, cent_ref[...], preferred_element_type=F32)
    gram_ref[0] = gram
    total = jnp.dot(flipped, jnp.ones((ROWS, WIDTH), BF16), preferred_element_type=F32)
    total_ref[...] = total
    total_hbm[...] = total
    spread_ref[...] = gram - wide(total) * (stat_ref[0, 1:2, :] / ROWS)
    left_part(where_ref, flipped, cent_ref, left_ref, sums_ref)


def near_kernel(
    where_ref, first_ref, second_ref, flip_ref, total_ref,
    left_ref, sums_ref, gram_ref, stat_ref, spread_ref, cent_ref,
):
    center_pair(first_ref, second_ref, 0, WIDTH, cent_ref, stat_ref)
    flipped = flip_ref[...]
    gram = jnp.dot(flipped, cent_ref[...], preferred_element_type=F32)
    gram_ref[0] = gram
    spread_ref[...] = gram - wide(total_ref[...]) * (stat_ref[0, 1:2, :] / ROWS)
    left_part(where_ref, flipped, cent_ref, left_ref, sums_ref)


def side_kernel(where_ref, first_ref, second_ref, flip_ref, gram_ref, stat_ref, cent_ref):
    center_pair(first_ref, second_ref, 0, WIDTH, cent_ref, stat_ref)
    gram_ref[0] = jnp.dot(flip_ref[...], cent_ref[...], preferred_element_type=F32)


def far_kernel(
    where_ref, first_ref, second_ref, flip_ref, total_ref, spread0_ref, spread1_ref, rider_ref,
    gram_ref, stat_ref, out_ref, cent_ref, held_ref,
):
    rider = rider_ref[0:4, :]
    for q in range(BLOCKS):
        spread, lane = ((spread0_ref, spread1_ref)[q // 16], WIDTH * (q // 8 % 2))
        row = 16 * (q % 8)
        out_ref[q, 0:16, :] = spread[row : row + 16, lane : lane + WIDTH]
        out_ref[q, 20:24, :] = rider
    center_pair(first_ref, second_ref, 0, WIDTH, cent_ref, stat_ref)
    gram = jnp.dot(flip_ref[...], cent_ref[...], preferred_element_type=F32)
    gram_ref[0] = gram
    spread = gram - wide(total_ref[...]) * (stat_ref[0, 1:2, :] / ROWS)
    held_ref[...] = jnp.where(where_ref[3] == 0, spread[:, 0:WIDTH], spread[:, WIDTH:PAIR])
    for q in range(BLOCKS):
        out_ref[q, 16:20, :] = held_ref[4 * q : 4 * q + 4, :]


def rest_kernel(where_ref, far_ref, side_ref, flip_ref, far_left_ref, side_left_ref, sums_ref):
    flipped = flip_ref[...]
    left_part(where_ref, flipped, far_ref, far_left_ref, sums_ref, 0)
    left_part(where_ref, flipped, side_ref, side_left_ref, sums_ref, 1)


ALL = [
    array(CHIPS, 8, PAIR),
    array(CHIPS, WIDTH, PAIR),
    array(CHIPS, 8, PAIR),
]


STORE = array(96, 8, WIDTH, WIDTH)
SHARD_PAIR = (2, SPLITS, WIDTH, WIDTH)


def call(
    kernel, name, inputs, outputs, *, store=None, puts=(), fetched=(), stored=(), kept=(),
    pair=0, span=1, scratch=(), us=3, grant=24,
):
    kept = (*([store] if store is not None else []), *kept)
    count, made, first = len(inputs), len(outputs), 1 if puts else 0
    sliced = [out in ALL for out in outputs]
    sizes = [(span, *out.shape[1:]) if cut else out.shape for out, cut in zip(outputs, sliced)]
    buffers = [pltpu.VMEM(inputs[i].shape, inputs[i].dtype) for i in fetched]
    buffers += [pltpu.VMEM(shape, F32) for shape, _ in puts]
    buffers += [pltpu.VMEM(sizes[i], outputs[i].dtype) for i in stored]

    def body(*refs):
        ins, refs = list(refs[:count]), refs[count + len(kept) :]
        slots, outs, refs = refs[:first], list(refs[first : first + made]), refs[first + made :]
        own, buffer, sem = refs[: len(scratch)], refs[len(scratch) : -1], refs[-1]
        copies = []
        for c, i in enumerate(fetched):
            copies.append(pltpu.make_async_copy(ins[i], buffer[c], sem.at[c]))
            ins[i] = buffer[c]
        for copy in copies:
            copy.start()
        for copy in copies:
            copy.wait()
        copies, mine = [], []
        for c, (_, place) in enumerate(puts, len(fetched)):
            copies.append(pltpu.make_async_copy(buffer[c], slots[0].at[place], sem.at[c]))
            mine.append(buffer[c])
        for c, i in enumerate(stored, len(fetched) + len(puts)):
            target = outs[i].at[pl.ds(pair, span)] if sliced[i] else outs[i]
            copies.append(pltpu.make_async_copy(buffer[c], target, sem.at[c]))
            outs[i] = buffer[c]
        kernel(*ins, *mine, *outs, *own)
        for copy in copies:
            copy.start()
        for copy in copies:
            copy.wait()

    ins = [SM if value.dtype == jnp.int32 else whole(*value.shape) for value in inputs]
    for i in fetched:
        ins[i] = HBM
    outs = [HBM if i in stored else whole(*out.shape) for i, out in enumerate(outputs)]
    aliased = range(first if store is None else 0, first + len(kept))
    return pl.pallas_call(
        body,
        out_shape=[STORE] * first + outputs,
        grid=(1,),
        in_specs=ins + [HBM] * len(kept),
        out_specs=[HBM] * first + outs,
        input_output_aliases={count + i: out for i, out in zip(range(len(kept)), aliased)},
        scratch_shapes=[pltpu.VMEM(shape, dtype) for shape, dtype in scratch]
        + buffers
        + [pltpu.SemaphoreType.DMA((max(len(buffers), 1),))],
        compiler_params=params(grant),
        cost_estimate=cost(us),
        name=name,
    )(*inputs, *kept)


def scan_kernel(arrived_ref, both_ref, means_ref, flags_ref):
    for b in range(BLOCKS):
        rider = arrived_ref[b, 16:24, :]
        means_ref[0, b : b + 1, :] = rider[4:5, :]
        means_ref[1, b : b + 1, :] = rider[5:6, :]
        flags_ref[b : b + 1, :] = rider[6:7, :]
    scan(arrived_ref, flags_ref, both_ref, 0, 16, 0)
    scan(arrived_ref, flags_ref, both_ref, 16, 4, 32)


def scan(arrived_ref, flags_ref, both_ref, row, size, at):
    zero = jnp.zeros((size, WIDTH), F32)
    running = zero
    for b in range(BLOCKS):
        begins = flags_ref[b : b + 1, :] > 0.5
        running = jnp.where(begins, zero, running)
        both_ref[b, at : at + size, :] = running
        running = running + arrived_ref[b, row : row + size, :]
    running = zero
    for b in reversed(range(BLOCKS)):
        begins = flags_ref[b : b + 1, :] > 0.5
        both_ref[b, at + size : at + 2 * size, :] = running
        running = jnp.where(begins, zero, running + arrived_ref[b, row : row + size, :])


def prep_kernel(
    where_ref, sums_ref, gram_ref, stat_ref, own_means_ref, ahead_ref, behind_ref, far_ref, flags_ref,
    turned_ref, cols_ref, coef_ref, before_ref, after_ref, vectors,
):
    here = where_ref[0]
    core = where_ref[2]
    away = 1 - core
    flags = flags_ref[...]
    spot = lax.broadcasted_iota(jnp.int32, (BLOCKS, WIDTH), 0)
    low = lax.broadcasted_iota(jnp.int32, (BLOCKS, BLOCKS), 1)
    high = lax.broadcasted_iota(jnp.int32, (BLOCKS, BLOCKS), 0)
    upto = jnp.dot((low <= high).astype(F32), flags, preferred_element_type=F32)
    mine = jnp.sum(jnp.where(spot <= here, flags, 0.0), axis=0, keepdims=True)
    same = jnp.abs(upto - mine) < 0.5
    masks = [
        jnp.where(same & (spot < here), 1.0, 0.0),
        jnp.where(same & (spot > here), 1.0, 0.0),
    ]
    totals = [jnp.sum(mask, axis=0, keepdims=True) for mask in masks]
    count_p, count_s = totals[0] * ROWS, totals[1] * ROWS

    def pooled(means, side):
        mask = masks[side]
        mean = jnp.sum(means * mask, axis=0, keepdims=True) / jnp.maximum(totals[side], 1.0)
        return mean, (means - mean) * mask

    def pick(value):
        return jnp.where(core == 0, value[:, 0:WIDTH], value[:, WIDTH:PAIR])

    row_means = own_means_ref[core]
    row_p, row_part_p = pooled(row_means, 0)
    row_s, row_part_s = pooled(row_means, 1)
    row_stat = pick(stat_ref[0])
    row_sums = pick(sums_ref[0])

    index = lax.broadcasted_iota(jnp.int32, (SPLITS, WIDTH), 0)
    k = jnp.zeros((SPLITS, WIDTH), jnp.int32)
    for j in range(SPLITS):
        k = jnp.where(index == j, where_ref[12 + j], k)
    k = k.astype(F32)
    rest = ROWS - k
    row_right = row_stat[1:2] - row_sums
    row_d = row_stat[0:1] + row_sums / k - row_p
    row_e = row_s - (row_stat[0:1] + row_right / rest)
    n_left, n_right = count_p + k, rest + count_s
    n = n_left + n_right
    weight = n_left * n_right / (n * n)
    a, b = weight / n_left, weight / n_right
    coef_ref[0:8, :] = a
    coef_ref[8:16, :] = b
    vectors[0:8, :] = -a * row_sums / k
    vectors[8:16, :] = a * (count_p * k / n_left) * row_d
    vectors[16:24, :] = b * row_right / rest
    vectors[24:32, :] = -b * (rest * count_s / n_right) * row_e
    total = count_p + ROWS
    n = total + count_s
    row_d = row_stat[2:3] - row_p
    row_e = row_s - (row_p + row_d * (ROWS / total))
    coef_ref[16:24, :] = jnp.broadcast_to(1.0 / n, (8, WIDTH))
    vectors[32:WIDTH, :] = jnp.zeros((WIDTH - 32, WIDTH), F32)
    vectors[32:33, :] = row_stat[1:2] / -ROWS / n
    vectors[33:34, :] = (count_p * ROWS / total) / n * row_d
    vectors[34:35, :] = (total * count_s / n) / n * row_e
    turned_ref[...] = vectors[...].T

    columns = (
        (own_means_ref[0], own_means_ref[1]),
        (ahead_ref[core], behind_ref[away]),
        (far_ref[core], far_ref[away]),
        (ahead_ref[away], behind_ref[core]),
    )
    for u in range(8):
        r, lanes = u // 2, slice(WIDTH * (u % 2), WIDTH * (u % 2) + WIDTH)
        means = columns[r][u % 2]
        col_p, col_part_p = pooled(means, 0)
        col_s, col_part_s = pooled(means, 1)
        stat = stat_ref[r, :, lanes]
        col_left = sums_ref[r, :, lanes]
        col_right = stat[1:2] - col_left
        cols_ref[u, 0:8, :] = col_left
        cols_ref[u, 8:16, :] = stat[0:1] + col_left / k - col_p
        cols_ref[u, 16:24, :] = col_right
        cols_ref[u, 24:32, :] = col_s - (stat[0:1] + col_right / rest)
        col_d = stat[2:3] - col_p
        cols_ref[u, 32:40, :] = jnp.zeros((8, WIDTH), F32)
        cols_ref[u, 32:33, :] = stat[1:2]
        cols_ref[u, 33:34, :] = col_d
        cols_ref[u, 34:35, :] = col_s - (col_p + col_d * (ROWS / total))

        def between(row_part, col_part):
            return ROWS * lax.dot_general(
                row_part, col_part, TRANSPOSED, precision=HIGH, preferred_element_type=F32
            )

        before_ref[u] = between(row_part_p, col_part_p)
        after_ref[u] = gram_ref[r, :, lanes] + between(row_part_s, col_part_s)


def prep_terms(where, sums, gram, stat, own, ahead, behind, far, flags, store):
    square = (8, WIDTH, WIDTH)
    return call(
        prep_kernel,
        "prep_terms",
        [where, sums, gram, stat, own, ahead, behind, far, flags],
        [],
        store=store,
        puts=(
            ((WIDTH, WIDTH), (11, 0)),
            ((8, 40, WIDTH), (10, slice(None), pl.ds(0, 40))),
            ((24, WIDTH), (11, 1, pl.ds(0, 24))),
            (square, 8),
            (square, 9),
        ),
        fetched=(1, 2, 3, 4, 8),
        scratch=[((WIDTH, WIDTH), F32)],
        us=0.1,
        grant=16,
    )[0]


def load_near(ref, p_ref, s_ref):
    for g in range(8):
        p_ref[16 * g : 16 * g + 16, :] = ref[g, 0:16, :]
        s_ref[16 * g : 16 * g + 16, :] = ref[g, 16:32, :]


def load_far(ref, p_ref, s_ref):
    for q in range(BLOCKS):
        p_ref[4 * q : 4 * q + 4, :] = ref[q, 0:4, :]
        s_ref[4 * q : 4 * q + 4, :] = ref[q, 4:8, :]


def shard_lanes(where_ref, u):
    return pl.ds(pl.multiple_of(where_ref[4 + u] * WIDTH, WIDTH), WIDTH)


def most_kernel(
    where_ref, back_ref, store_hbm, most_ref, seg_ref, coef_ref,
    left_ref, prefix_ref, suffix_ref, cols_ref, turned_ref, p_ref, s_ref, sem,
):
    loads = [
        pltpu.make_async_copy(source, target, sem.at[c])
        for c, (source, target) in enumerate(
            (
                (store_hbm.at[8], prefix_ref),
                (store_hbm.at[9], suffix_ref),
                (store_hbm.at[10, :, pl.ds(0, 40)], cols_ref),
                (store_hbm.at[11, 0], turned_ref),
                (store_hbm.at[11, 1, pl.ds(0, 24)], coef_ref),
                (store_hbm.at[pl.ds(0, 8)], left_ref),
            )
        )
    ]
    for load in loads:
        load.start()
    held = where_ref[3]
    for load in loads[:5]:
        load.wait()

    def add(u):
        prefix_ref[u] = prefix_ref[u] + p_ref[...]
        suffix_ref[u] = suffix_ref[u] + s_ref[...]

    for u in range(4):
        load_near(back_ref.at[pl.ds(8 * u, 8)], p_ref, s_ref)
        add(u)
    load_far(back_ref.at[:, pl.ds(32, 8)], p_ref, s_ref)
    add(4 + held)

    def spread_out(rows):
        return [jnp.broadcast_to(turned_ref[:, i : i + 1], (WIDTH, WIDTH)) for i in rows]

    turned = spread_out(range(32, 35))
    for u in range(8):
        value = (prefix_ref[u] + suffix_ref[u]) * coef_ref[16:17, :]
        for i in range(3):
            value = value + turned[i] * cols_ref[u, 32 + i : 33 + i, :]
        seg_ref[:, shard_lanes(where_ref, u)] = value
    loads[5].wait()
    for j in range(SPLITS):
        turned = spread_out(range(j, 32, 8))
        a, b = coef_ref[j : j + 1, :], coef_ref[8 + j : 9 + j, :]
        for u in range(8):
            value = (a + b) * left_ref[u, j] + a * prefix_ref[u] - b * suffix_ref[u]
            for i in range(4):
                value = value + turned[i] * cols_ref[u, 8 * i + j : 8 * i + j + 1, :]
            most_ref[j, :, shard_lanes(where_ref, u)] = value


def last_kernel(
    where_ref, most_ref, most_seg_ref, coef_ref, opposite_ref, next_ref, before_ref, cusum_hbm, seg_hbm,
    cusum_ref, seg_ref, prefix_ref, suffix_ref, p_ref, s_ref, sem,
):
    shards = (5 - where_ref[3], 6, 7)
    for v, (ref, load) in enumerate(
        ((opposite_ref, load_far), (next_ref, load_near), (before_ref, load_near))
    ):
        load(ref, p_ref, s_ref)
        prefix_ref[v] = p_ref[...].T
        suffix_ref[v] = s_ref[...].T
    seg_ref[0] = most_seg_ref[...]
    for v, u in enumerate(shards):
        lanes = shard_lanes(where_ref, u)
        added = (prefix_ref[v] + suffix_ref[v]) * coef_ref[16:17, :]
        seg_ref[0, :, lanes] = most_seg_ref[:, lanes] + added
    stores = [pltpu.make_async_copy(seg_ref, seg_hbm, sem.at[SPLITS])]
    stores[0].start()
    for j in range(SPLITS):
        a, b = coef_ref[j : j + 1, :], coef_ref[8 + j : 9 + j, :]
        cusum_ref[0, j] = most_ref[j]
        for v, u in enumerate(shards):
            lanes = shard_lanes(where_ref, u)
            cusum_ref[0, j, :, lanes] = most_ref[j, :, lanes] + a * prefix_ref[v] - b * suffix_ref[v]
        store = pltpu.make_async_copy(
            cusum_ref.at[:, pl.ds(j, 1)], cusum_hbm.at[:, pl.ds(j, 1)], sem.at[j]
        )
        store.start()
        stores.append(store)
    for store in stores:
        store.wait()


OUTPUTS = [array(1, SPLITS, WIDTH, CHIPS * PAIR), array(1, WIDTH, CHIPS * PAIR)]
MOST = [array(SPLITS, WIDTH, CHIPS * PAIR), array(WIDTH, CHIPS * PAIR), array(24, WIDTH)]


def most_outputs(where, back, store):
    square = array(8, WIDTH, WIDTH)
    buffers = [array(8, SPLITS, WIDTH, WIDTH), square, square, array(8, 40, WIDTH)]
    buffers += [array(WIDTH, WIDTH)] * 3
    return pl.pallas_call(
        most_kernel,
        out_shape=MOST,
        grid=(1,),
        in_specs=[SM, whole(*back.shape), HBM],
        out_specs=[whole(*value.shape) for value in MOST],
        scratch_shapes=[pltpu.VMEM(value.shape, F32) for value in buffers]
        + [pltpu.SemaphoreType.DMA((6,))],
        compiler_params=params(24),
        cost_estimate=cost(5),
        name="most_outputs",
    )(where, back, store)


def last_outputs(where, most, opposite, following, before):
    inputs = [*most, opposite, following, before]
    buffers = [*OUTPUTS, array(3, WIDTH, WIDTH), array(3, WIDTH, WIDTH)]
    buffers += [array(WIDTH, WIDTH)] * 2
    return pl.pallas_call(
        last_kernel,
        out_shape=OUTPUTS,
        grid=(1,),
        in_specs=[SM] + [whole(*value.shape) for value in inputs],
        out_specs=[HBM, HBM],
        scratch_shapes=[pltpu.VMEM(value.shape, F32) for value in buffers]
        + [pltpu.SemaphoreType.DMA((SPLITS + 1,))],
        compiler_params=params(24),
        cost_estimate=cost(3),
        name="last_outputs",
    )(where, *inputs)


def window_kernel(
    where_ref, mine_ref, other_ref, gram_ref, stat_ref, total_ref,
    out_ref, cent_ref, flip_ref, sum_ref,
):
    halves = (
        (mine_ref, 0), (other_ref, 0), (mine_ref, HALO), (other_ref, 3 * HALO),
        (mine_ref, 2 * HALO), (other_ref, 2 * HALO), (other_ref, HALO), (mine_ref, 3 * HALO),
    )
    live = jnp.where(where_ref[0] > 0, 1.0, 0.0).astype(F32)
    core = where_ref[2]
    at = pl.multiple_of(core * WIDTH, WIDTH)
    off = pl.multiple_of((1 - core) * WIDTH, WIDTH)
    count = ROWS + live * HALO
    scale = wide(1.0 / jnp.full((1, WIDTH), count, F32))
    unbias = wide(1.0 / jnp.full((1, WIDTH), count - 1.0, F32))
    step = 256
    for r in range(CHIPS):
        lanes = (at, off) if r == 0 else (0, WIDTH)
        for (raw, row), lane in zip(halves[2 * r : 2 * r + 2], lanes):
            mean = stat_ref[r, 0:1, pl.ds(lane, WIDTH)]

            def shift(i, _, raw=raw, row=row, lane=lane, mean=mean):
                piece = (raw[pl.ds(row + i * step, step), :].astype(F32) - mean) * live
                cent_ref[pl.ds(i * step, step), pl.ds(lane, WIDTH)] = piece.astype(BF16)
                return 0

            lax.fori_loop(0, HALO // step, shift, 0, unroll=2)
        if r == 0:
            flip_ref[...] = cent_ref[:, pl.ds(at, WIDTH)].T
            flipped = flip_ref[...]
            row_sum = jnp.dot(flipped, jnp.ones((HALO, WIDTH), BF16), preferred_element_type=F32)
            sum_ref[...] = row_sum + total_ref[...]
        cent = cent_ref[...]
        halo = jnp.dot(flip_ref[...], cent, preferred_element_type=F32)
        col_sum = jnp.dot(jnp.ones((16, HALO), BF16), cent, preferred_element_type=F32)[0:1]
        col_sum = col_sum + stat_ref[r, 1:2, :]
        value = (halo + gram_ref[r] - wide(sum_ref[...]) * (col_sum * scale)) * unbias
        for c in range(2):
            lane = pl.multiple_of(where_ref[4 + 2 * r + c] * WIDTH, WIDTH)
            out_ref[0, :, pl.ds(lane, WIDTH)] = value[:, c * WIDTH : (c + 1) * WIDTH]


def to_chan(value, target):
    count = lax.axis_size("chan")
    return lax.ppermute(value, "chan", [(s, target(s) % count) for s in range(count)])


def exchange(value):
    return lax.all_to_all(value, "tm", 0, 0, tiled=True)


def after(value, *others):
    return lax.optimization_barrier((value, *others))[0]


def local(samples, candidates, segment_start):
    here, index = lax.axis_index("tm"), lax.axis_index("chan")
    chip, core = index // 2, index % 2
    nearby = [2 * chip, 2 * chip + 1]
    for step, side in ((1, core), (3, 1 - core), (2, core), (2, 1 - core), (1, 1 - core), (3, core)):
        nearby.append(2 * ((chip + step) % CHIPS) + side)
    held = jnp.where(chip < CHIPS // 2, 0, 1)
    where = jnp.stack([here, chip, core, held] + nearby).astype(jnp.int32)
    where = jnp.concatenate([where, candidates[0], segment_start])

    behind = to_chan(samples, lambda s: s + 2)
    ahead = to_chan(samples, lambda s: s - 2)
    other = to_chan(samples, lambda s: s ^ 1)
    prior = lax.ppermute(samples[ROWS - HALO :], "tm", [(b, b + 1) for b in range(BLOCKS - 1)])
    flip_shape, square = array(WIDTH, ROWS, dtype=BF16), array(WIDTH, WIDTH)
    store, sums, gram, stat, late_flipped, late_total, flipped, spread0, total, rider = call(
        first_kernel,
        "first_pair",
        [where, samples, other],
        ALL + [flip_shape, square, flip_shape, array(WIDTH, PAIR), square, array(8, WIDTH)],
        puts=((SHARD_PAIR, pl.ds(0, 2)),),
        fetched=(1,),
        stored=(0, 1, 2, 3, 4),
        scratch=[((ROWS, PAIR), BF16)],
    )
    behind, ahead, prior, flipped = lax.optimization_barrier((behind, ahead, prior, flipped))
    half = ROWS // 2
    far_low = to_chan(behind[:half], lambda s: s + 2)
    far_high = to_chan(ahead[half:], lambda s: s - 2)
    behind_other = to_chan(behind, lambda s: s ^ 1)
    ahead_other = to_chan(ahead, lambda s: s ^ 1)
    store, sums, gram, stat, spread1 = call(
        near_kernel,
        "near_pair",
        [where, ahead, behind_other, flipped, total],
        ALL + [array(WIDTH, PAIR)],
        store=store,
        puts=((SHARD_PAIR, pl.ds(2, 2)),),
        stored=(0, 1, 2),
        kept=(sums, gram, stat),
        pair=1,
        scratch=[((ROWS, PAIR), BF16)],
    )
    cent_shape = array(ROWS, PAIR, dtype=BF16)
    gram, stat, side = call(
        side_kernel,
        "side_pair",
        [where, ahead_other, behind, flipped],
        ALL[1:] + [cent_shape],
        stored=(0, 1),
        kept=(gram, stat),
        pair=3,
        us=0.1,
    )
    far_low, far_high, stat, prior = lax.optimization_barrier((far_low, far_high, stat, prior))
    prior_behind = to_chan(prior, lambda s: s + 2)
    prior_ahead = to_chan(prior, lambda s: s - 2)
    far = jnp.concatenate([far_low, far_high], axis=0)
    far_other = to_chan(far, lambda s: s ^ 1)
    gram, stat, pieces, cent = call(
        far_kernel,
        "far_pair",
        [where, far, far_other, flipped, total, spread0, spread1, rider],
        ALL[1:] + [array(BLOCKS, 24, WIDTH), cent_shape],
        stored=(0, 1, 2, 3),
        kept=(gram, stat),
        pair=2,
        scratch=[((WIDTH, WIDTH), F32)],
        us=0.1,
    )
    arrived = exchange(pieces)

    cent, prior_behind, prior_ahead = lax.optimization_barrier((cent, prior_behind, prior_ahead))
    half = HALO // 2
    prior_low = to_chan(prior_behind[:half], lambda s: s + 2)
    prior_high = to_chan(prior_ahead[half:], lambda s: s - 2)
    store, sums = call(
        rest_kernel,
        "rest_left",
        [where, cent, side, late_flipped],
        ALL[:1],
        store=store,
        puts=((SHARD_PAIR, pl.ds(4, 2)), (SHARD_PAIR, pl.ds(6, 2))),
        fetched=(1, 3),
        stored=(0,),
        kept=(sums,),
        pair=2,
        span=2,
        us=4,
    )
    arrived, prior_low, prior_high, sums = lax.optimization_barrier(
        (arrived, prior_low, prior_high, sums)
    )
    prior = jnp.concatenate([prior, prior_ahead, prior_low, prior_high, prior_behind], axis=0)
    prior_other = to_chan(prior, lambda s: s ^ 1)
    scanned, own_means, flags = call(
        scan_kernel,
        "scan_pieces",
        [arrived],
        [array(BLOCKS, 40, WIDTH), array(2, BLOCKS, WIDTH), array(BLOCKS, WIDTH)],
        stored=(0, 1, 2),
        us=1,
    )
    back = exchange(scanned)
    ahead_means = to_chan(own_means, lambda s: s - 2)
    behind_means = to_chan(own_means, lambda s: s + 2)
    far_means = to_chan(own_means, lambda s: s + 4)
    store = prep_terms(
        where, sums, gram, stat, own_means, ahead_means, behind_means, far_means, flags, store
    )
    window_cov = call(
        window_kernel,
        "window_output",
        [where, prior, prior_other, gram, stat, late_total],
        [array(1, WIDTH, CHIPS * PAIR)],
        fetched=(3, 4, 5),
        stored=(0,),
        scratch=[((HALO, PAIR), BF16), ((WIDTH, HALO), BF16), ((WIDTH, WIDTH), F32)],
        us=0.1,
    )[0]
    back, store, window_cov = lax.optimization_barrier((back, store, window_cov))
    before = to_chan(back[16:24, 0:32], lambda s: s + 2)
    following = to_chan(back[24:32, 0:32], lambda s: (s - 2) ^ 1)
    opposite = to_chan(back[:, 32:40], lambda s: s + 4 if s < 4 else (s - 4) ^ 1)
    most = most_outputs(where, back, store)
    cusum, segment_cov = last_outputs(where, most, opposite, following, before)
    return window_cov, segment_cov, cusum


def solution(mesh):
    placed = (P("tm", "chan"), P("tm", None), P("tm"))
    return jax.shard_map(
        local,
        mesh=mesh,
        in_specs=placed,
        out_specs=(P("tm", "chan", None), P("tm", "chan", None), P("tm", None, "chan", None)),
        check_vma=False,
    )
```

```python
import jax
import jax.numpy as jnp
from jax import lax
from jax.experimental import pallas as pl
from jax.experimental.pallas import tpu as pltpu
from jax.sharding import PartitionSpec as P

F32, BF16 = jnp.float32, jnp.bfloat16
ROWS, HALO, WIDTH, BLOCKS, SPLITS, CHIPS = 2048, 1024, 128, 32, 8, 4
PAIR = 2 * WIDTH
HIGH = lax.Precision.HIGHEST
TRANSPOSED = (((0,), (0,)), ((), ()))
SM = pl.BlockSpec(memory_space=pltpu.SMEM)
HBM = pl.BlockSpec(memory_space=pltpu.HBM)
MIB = 2**20


def whole(*shape):
    return pl.BlockSpec(shape, lambda *_: (0,) * len(shape))


def array(*shape, dtype=F32):
    return jax.ShapeDtypeStruct(shape, dtype)


def params(grant):
    return pltpu.CompilerParams(
        vmem_limit_bytes=grant * MIB, dimension_semantics=("arbitrary",)
    )


def cost(microseconds):
    return pl.CostEstimate(
        flops=int(microseconds * 1e9), bytes_accessed=MIB, transcendentals=0
    )


def center_shard(raw_ref, out_ref, at):
    step = 256

    def add(i, total):
        piece = raw_ref[pl.ds(i * step, step), :].astype(F32)
        return total + jnp.sum(piece.reshape(step // 8, 8, WIDTH), axis=0)

    total = lax.fori_loop(0, ROWS // step, add, jnp.zeros((8, WIDTH), F32), unroll=2)
    mean = jnp.sum(total, axis=0, keepdims=True) / ROWS

    def shift(i, _):
        piece = raw_ref[pl.ds(i * step, step), :].astype(F32) - mean
        out_ref[pl.ds(i * step, step), pl.ds(at, WIDTH)] = piece.astype(BF16)
        return 0

    lax.fori_loop(0, ROWS // step, shift, 0, unroll=2)
    return mean


def center_pair(first_ref, second_ref, at, off, cent_ref, stat_ref):
    stat_ref[0] = jnp.zeros((8, PAIR), F32)
    stat_ref[0, 0:1, pl.ds(at, WIDTH)] = center_shard(first_ref, cent_ref, at)
    stat_ref[0, 0:1, pl.ds(off, WIDTH)] = center_shard(second_ref, cent_ref, off)
    total = jnp.dot(jnp.ones((16, ROWS), BF16), cent_ref[...], preferred_element_type=F32)[0:1]
    stat_ref[0, 1:2, :] = total
    stat_ref[0, 2:3, :] = stat_ref[0, 0:1, :] + total / ROWS


def turned_dot(left, right):
    return lax.dot_general(left, right, TRANSPOSED, preferred_element_type=F32)


def wide(value):
    return jnp.concatenate([value, value], axis=1)


def left_part(where_ref, flipped, cent_ref, left_ref, sums_ref, block=0):
    index = lax.broadcasted_iota(jnp.int32, (16, ROWS), 0)
    place = lax.broadcasted_iota(jnp.int32, (16, ROWS), 1)
    limit = jnp.zeros((16, ROWS), jnp.int32)
    for j in range(SPLITS):
        limit = jnp.where(index == j, where_ref[12 + j], limit)
    masks = jnp.where(place < limit, 1.0, 0.0).astype(BF16)
    cent = cent_ref[...]
    sums_ref[block] = jnp.dot(masks, cent, preferred_element_type=F32)[0:8]
    for i in range(SPLITS // 4):
        kept = jnp.concatenate([flipped * masks[j : j + 1, :] for j in range(4 * i, 4 * i + 4)], axis=0)
        part = jnp.dot(kept, cent, preferred_element_type=F32)
        for j in range(4):
            for c in range(2):
                rows, lanes = slice(j * WIDTH, (j + 1) * WIDTH), slice(c * WIDTH, (c + 1) * WIDTH)
                left_ref[c, 4 * i + j] = part[rows, lanes]


def first_kernel(
    where_ref, mine_ref, other_ref,
    left_ref, sums_ref, gram_ref, stat_ref, flip_hbm, total_hbm, flip_ref, spread_ref, total_ref, rider_ref, cent_ref,
):
    core = where_ref[2]
    at = pl.multiple_of(core * WIDTH, WIDTH)
    off = pl.multiple_of((1 - core) * WIDTH, WIDTH)
    center_pair(mine_ref, other_ref, at, off, cent_ref, stat_ref)
    rider_ref[...] = jnp.zeros((8, WIDTH), F32)
    rider_ref[0:1, :] = stat_ref[0, 2:3, 0:WIDTH]
    rider_ref[1:2, :] = stat_ref[0, 2:3, WIDTH:PAIR]
    rider_ref[2:3, :] = jnp.full((1, WIDTH), where_ref[20], jnp.int32).astype(F32)
    flip_ref[...] = cent_ref[:, pl.ds(at, WIDTH)].T
    flipped = flip_ref[...]
    flip_hbm[...] = flipped
    gram = jnp.dot(flipped, cent_ref[...], preferred_element_type=F32)
    gram_ref[0] = gram
    total = jnp.dot(flipped, jnp.ones((ROWS, WIDTH), BF16), preferred_element_type=F32)
    total_ref[...] = total
    total_hbm[...] = total
    spread_ref[...] = gram - wide(total) * (stat_ref[0, 1:2, :] / ROWS)
    left_part(where_ref, flipped, cent_ref, left_ref, sums_ref)


def near_kernel(
    where_ref, first_ref, second_ref, flip_ref, total_ref,
    left_ref, sums_ref, gram_ref, stat_ref, spread_ref, cent_ref,
):
    center_pair(first_ref, second_ref, 0, WIDTH, cent_ref, stat_ref)
    flipped = flip_ref[...]
    gram = jnp.dot(flipped, cent_ref[...], preferred_element_type=F32)
    gram_ref[0] = gram
    spread_ref[...] = gram - wide(total_ref[...]) * (stat_ref[0, 1:2, :] / ROWS)
    left_part(where_ref, flipped, cent_ref, left_ref, sums_ref)


def side_kernel(where_ref, first_ref, second_ref, flip_ref, gram_ref, stat_ref, cent_ref):
    center_pair(first_ref, second_ref, 0, WIDTH, cent_ref, stat_ref)
    gram_ref[0] = jnp.dot(flip_ref[...], cent_ref[...], preferred_element_type=F32)


def far_kernel(
    where_ref, first_ref, second_ref, flip_ref, total_ref, spread0_ref, spread1_ref, rider_ref,
    gram_ref, stat_ref, out_ref, cent_ref, held_ref,
):
    rider = rider_ref[0:4, :]
    for q in range(BLOCKS):
        spread, lane = ((spread0_ref, spread1_ref)[q // 16], WIDTH * (q // 8 % 2))
        row = 16 * (q % 8)
        out_ref[q, 0:16, :] = spread[row : row + 16, lane : lane + WIDTH]
        out_ref[q, 20:24, :] = rider
    center_pair(first_ref, second_ref, 0, WIDTH, cent_ref, stat_ref)
    gram = jnp.dot(flip_ref[...], cent_ref[...], preferred_element_type=F32)
    gram_ref[0] = gram
    spread = gram - wide(total_ref[...]) * (stat_ref[0, 1:2, :] / ROWS)
    held_ref[...] = jnp.where(where_ref[3] == 0, spread[:, 0:WIDTH], spread[:, WIDTH:PAIR])
    for q in range(BLOCKS):
        out_ref[q, 16:20, :] = held_ref[4 * q : 4 * q + 4, :]


def rest_kernel(where_ref, cent_ref, flip_ref, left_ref, sums_ref):
    left_part(where_ref, flip_ref[...], cent_ref, left_ref, sums_ref)


ALL = [
    array(CHIPS, 8, PAIR),
    array(CHIPS, WIDTH, PAIR),
    array(CHIPS, 8, PAIR),
]


STORE = array(96, 8, WIDTH, WIDTH)
SHARD_PAIR = (2, SPLITS, WIDTH, WIDTH)


def call(
    kernel, name, inputs, outputs, *, store=None, puts=(), fetched=(), stored=(), kept=(),
    pair=0, span=1, scratch=(), us=3, grant=24,
):
    kept = (*([store] if store is not None else []), *kept)
    count, made, first = len(inputs), len(outputs), 1 if puts else 0
    sliced = [out in ALL for out in outputs]
    sizes = [(span, *out.shape[1:]) if cut else out.shape for out, cut in zip(outputs, sliced)]
    buffers = [pltpu.VMEM(inputs[i].shape, inputs[i].dtype) for i in fetched]
    buffers += [pltpu.VMEM(shape, F32) for shape, _ in puts]
    buffers += [pltpu.VMEM(sizes[i], outputs[i].dtype) for i in stored]

    def body(*refs):
        ins, refs = list(refs[:count]), refs[count + len(kept) :]
        slots, outs, refs = refs[:first], list(refs[first : first + made]), refs[first + made :]
        own, buffer, sem = refs[: len(scratch)], refs[len(scratch) : -1], refs[-1]
        copies = []
        for c, i in enumerate(fetched):
            copies.append(pltpu.make_async_copy(ins[i], buffer[c], sem.at[c]))
            ins[i] = buffer[c]
        for copy in copies:
            copy.start()
        for copy in copies:
            copy.wait()
        copies, mine = [], []
        for c, (_, place) in enumerate(puts, len(fetched)):
            copies.append(pltpu.make_async_copy(buffer[c], slots[0].at[place], sem.at[c]))
            mine.append(buffer[c])
        for c, i in enumerate(stored, len(fetched) + len(puts)):
            target = outs[i].at[pl.ds(pair, span)] if sliced[i] else outs[i]
            copies.append(pltpu.make_async_copy(buffer[c], target, sem.at[c]))
            outs[i] = buffer[c]
        kernel(*ins, *mine, *outs, *own)
        for copy in copies:
            copy.start()
        for copy in copies:
            copy.wait()

    ins = [SM if value.dtype == jnp.int32 else whole(*value.shape) for value in inputs]
    for i in fetched:
        ins[i] = HBM
    outs = [HBM if i in stored else whole(*out.shape) for i, out in enumerate(outputs)]
    aliased = range(first if store is None else 0, first + len(kept))
    return pl.pallas_call(
        body,
        out_shape=[STORE] * first + outputs,
        grid=(1,),
        in_specs=ins + [HBM] * len(kept),
        out_specs=[HBM] * first + outs,
        input_output_aliases={count + i: out for i, out in zip(range(len(kept)), aliased)},
        scratch_shapes=[pltpu.VMEM(shape, dtype) for shape, dtype in scratch]
        + buffers
        + [pltpu.SemaphoreType.DMA((max(len(buffers), 1),))],
        compiler_params=params(grant),
        cost_estimate=cost(us),
        name=name,
    )(*inputs, *kept)


def scan_kernel(arrived_ref, both_ref, means_ref, flags_ref):
    for b in range(BLOCKS):
        rider = arrived_ref[b, 16:24, :]
        means_ref[0, b : b + 1, :] = rider[4:5, :]
        means_ref[1, b : b + 1, :] = rider[5:6, :]
        flags_ref[b : b + 1, :] = rider[6:7, :]
    scan(arrived_ref, flags_ref, both_ref, 0, 16, 0)
    scan(arrived_ref, flags_ref, both_ref, 16, 4, 32)


def scan(arrived_ref, flags_ref, both_ref, row, size, at):
    zero = jnp.zeros((size, WIDTH), F32)
    running = zero
    for b in range(BLOCKS):
        begins = flags_ref[b : b + 1, :] > 0.5
        running = jnp.where(begins, zero, running)
        both_ref[b, at : at + size, :] = running
        running = running + arrived_ref[b, row : row + size, :]
    running = zero
    for b in reversed(range(BLOCKS)):
        begins = flags_ref[b : b + 1, :] > 0.5
        both_ref[b, at + size : at + 2 * size, :] = running
        running = jnp.where(begins, zero, running + arrived_ref[b, row : row + size, :])


def prep_kernel(
    where_ref, sums_ref, gram_ref, stat_ref, own_means_ref, ahead_ref, behind_ref, far_ref, flags_ref,
    turned_ref, cols_ref, coef_ref, before_ref, after_ref, vectors,
):
    here = where_ref[0]
    core = where_ref[2]
    away = 1 - core
    flags = flags_ref[...]
    spot = lax.broadcasted_iota(jnp.int32, (BLOCKS, WIDTH), 0)
    low = lax.broadcasted_iota(jnp.int32, (BLOCKS, BLOCKS), 1)
    high = lax.broadcasted_iota(jnp.int32, (BLOCKS, BLOCKS), 0)
    upto = jnp.dot((low <= high).astype(F32), flags, preferred_element_type=F32)
    mine = jnp.sum(jnp.where(spot <= here, flags, 0.0), axis=0, keepdims=True)
    same = jnp.abs(upto - mine) < 0.5
    masks = [
        jnp.where(same & (spot < here), 1.0, 0.0),
        jnp.where(same & (spot > here), 1.0, 0.0),
    ]
    totals = [jnp.sum(mask, axis=0, keepdims=True) for mask in masks]
    count_p, count_s = totals[0] * ROWS, totals[1] * ROWS

    def pooled(means, side):
        mask = masks[side]
        mean = jnp.sum(means * mask, axis=0, keepdims=True) / jnp.maximum(totals[side], 1.0)
        return mean, (means - mean) * mask

    def pick(value):
        return jnp.where(core == 0, value[:, 0:WIDTH], value[:, WIDTH:PAIR])

    row_means = own_means_ref[core]
    row_p, row_part_p = pooled(row_means, 0)
    row_s, row_part_s = pooled(row_means, 1)
    row_stat = pick(stat_ref[0])
    row_sums = pick(sums_ref[0])

    index = lax.broadcasted_iota(jnp.int32, (SPLITS, WIDTH), 0)
    k = jnp.zeros((SPLITS, WIDTH), jnp.int32)
    for j in range(SPLITS):
        k = jnp.where(index == j, where_ref[12 + j], k)
    k = k.astype(F32)
    rest = ROWS - k
    row_right = row_stat[1:2] - row_sums
    row_d = row_stat[0:1] + row_sums / k - row_p
    row_e = row_s - (row_stat[0:1] + row_right / rest)
    n_left, n_right = count_p + k, rest + count_s
    n = n_left + n_right
    weight = n_left * n_right / (n * n)
    a, b = weight / n_left, weight / n_right
    coef_ref[0:8, :] = a
    coef_ref[8:16, :] = b
    vectors[0:8, :] = -a * row_sums / k
    vectors[8:16, :] = a * (count_p * k / n_left) * row_d
    vectors[16:24, :] = b * row_right / rest
    vectors[24:32, :] = -b * (rest * count_s / n_right) * row_e
    total = count_p + ROWS
    n = total + count_s
    row_d = row_stat[2:3] - row_p
    row_e = row_s - (row_p + row_d * (ROWS / total))
    coef_ref[16:24, :] = jnp.broadcast_to(1.0 / n, (8, WIDTH))
    vectors[32:WIDTH, :] = jnp.zeros((WIDTH - 32, WIDTH), F32)
    vectors[32:33, :] = row_stat[1:2] / -ROWS / n
    vectors[33:34, :] = (count_p * ROWS / total) / n * row_d
    vectors[34:35, :] = (total * count_s / n) / n * row_e
    turned_ref[...] = vectors[...].T

    columns = (
        (own_means_ref[0], own_means_ref[1]),
        (ahead_ref[core], behind_ref[away]),
        (far_ref[core], far_ref[away]),
        (ahead_ref[away], behind_ref[core]),
    )
    for u in range(8):
        r, lanes = u // 2, slice(WIDTH * (u % 2), WIDTH * (u % 2) + WIDTH)
        means = columns[r][u % 2]
        col_p, col_part_p = pooled(means, 0)
        col_s, col_part_s = pooled(means, 1)
        stat = stat_ref[r, :, lanes]
        col_left = sums_ref[r, :, lanes]
        col_right = stat[1:2] - col_left
        cols_ref[u, 0:8, :] = col_left
        cols_ref[u, 8:16, :] = stat[0:1] + col_left / k - col_p
        cols_ref[u, 16:24, :] = col_right
        cols_ref[u, 24:32, :] = col_s - (stat[0:1] + col_right / rest)
        col_d = stat[2:3] - col_p
        cols_ref[u, 32:40, :] = jnp.zeros((8, WIDTH), F32)
        cols_ref[u, 32:33, :] = stat[1:2]
        cols_ref[u, 33:34, :] = col_d
        cols_ref[u, 34:35, :] = col_s - (col_p + col_d * (ROWS / total))

        def between(row_part, col_part):
            return ROWS * lax.dot_general(
                row_part, col_part, TRANSPOSED, precision=HIGH, preferred_element_type=F32
            )

        before_ref[u] = between(row_part_p, col_part_p)
        after_ref[u] = gram_ref[r, :, lanes] + between(row_part_s, col_part_s)


def load_near(ref, p_ref, s_ref):
    for g in range(8):
        p_ref[16 * g : 16 * g + 16, :] = ref[g, 0:16, :]
        s_ref[16 * g : 16 * g + 16, :] = ref[g, 16:32, :]


def load_far(ref, p_ref, s_ref):
    for q in range(BLOCKS):
        p_ref[4 * q : 4 * q + 4, :] = ref[q, 0:4, :]
        s_ref[4 * q : 4 * q + 4, :] = ref[q, 4:8, :]


def shard_lanes(where_ref, u):
    return pl.ds(pl.multiple_of(where_ref[4 + u] * WIDTH, WIDTH), WIDTH)


def most_kernel(
    where_ref, back_ref, store_hbm, most_ref, seg_ref, coef_ref,
    left_ref, prefix_ref, suffix_ref, cols_ref, turned_ref, p_ref, s_ref, sem,
):
    loads = [
        pltpu.make_async_copy(source, target, sem.at[c])
        for c, (source, target) in enumerate(
            (
                (store_hbm.at[8], prefix_ref),
                (store_hbm.at[9], suffix_ref),
                (store_hbm.at[10, :, pl.ds(0, 40)], cols_ref),
                (store_hbm.at[11, 0], turned_ref),
                (store_hbm.at[11, 1, pl.ds(0, 24)], coef_ref),
                (store_hbm.at[pl.ds(0, 8)], left_ref),
            )
        )
    ]
    for load in loads:
        load.start()
    held = where_ref[3]
    for load in loads[:5]:
        load.wait()

    def add(u):
        prefix_ref[u] = prefix_ref[u] + p_ref[...]
        suffix_ref[u] = suffix_ref[u] + s_ref[...]

    for u in range(4):
        load_near(back_ref.at[pl.ds(8 * u, 8)], p_ref, s_ref)
        add(u)
    load_far(back_ref.at[:, pl.ds(32, 8)], p_ref, s_ref)
    add(4 + held)

    def spread_out(rows):
        return [jnp.broadcast_to(turned_ref[:, i : i + 1], (WIDTH, WIDTH)) for i in rows]

    turned = spread_out(range(32, 35))
    for u in range(8):
        value = (prefix_ref[u] + suffix_ref[u]) * coef_ref[16:17, :]
        for i in range(3):
            value = value + turned[i] * cols_ref[u, 32 + i : 33 + i, :]
        seg_ref[:, shard_lanes(where_ref, u)] = value
    loads[5].wait()
    for j in range(SPLITS):
        turned = spread_out(range(j, 32, 8))
        a, b = coef_ref[j : j + 1, :], coef_ref[8 + j : 9 + j, :]
        for u in range(8):
            value = (a + b) * left_ref[u, j] + a * prefix_ref[u] - b * suffix_ref[u]
            for i in range(4):
                value = value + turned[i] * cols_ref[u, 8 * i + j : 8 * i + j + 1, :]
            most_ref[j, :, shard_lanes(where_ref, u)] = value


def last_kernel(
    where_ref, most_ref, most_seg_ref, coef_ref, opposite_ref, next_ref, before_ref, cusum_hbm, seg_hbm,
    cusum_ref, seg_ref, prefix_ref, suffix_ref, p_ref, s_ref, sem,
):
    shards = (5 - where_ref[3], 6, 7)
    for v, (ref, load) in enumerate(
        ((opposite_ref, load_far), (next_ref, load_near), (before_ref, load_near))
    ):
        load(ref, p_ref, s_ref)
        prefix_ref[v] = p_ref[...].T
        suffix_ref[v] = s_ref[...].T
    seg_ref[0] = most_seg_ref[...]
    for v, u in enumerate(shards):
        lanes = shard_lanes(where_ref, u)
        added = (prefix_ref[v] + suffix_ref[v]) * coef_ref[16:17, :]
        seg_ref[0, :, lanes] = most_seg_ref[:, lanes] + added
    stores = [pltpu.make_async_copy(seg_ref, seg_hbm, sem.at[SPLITS])]
    stores[0].start()
    for j in range(SPLITS):
        a, b = coef_ref[j : j + 1, :], coef_ref[8 + j : 9 + j, :]
        cusum_ref[0, j] = most_ref[j]
        for v, u in enumerate(shards):
            lanes = shard_lanes(where_ref, u)
            cusum_ref[0, j, :, lanes] = most_ref[j, :, lanes] + a * prefix_ref[v] - b * suffix_ref[v]
        store = pltpu.make_async_copy(
            cusum_ref.at[:, pl.ds(j, 1)], cusum_hbm.at[:, pl.ds(j, 1)], sem.at[j]
        )
        store.start()
        stores.append(store)
    for store in stores:
        store.wait()


OUTPUTS = [array(1, SPLITS, WIDTH, CHIPS * PAIR), array(1, WIDTH, CHIPS * PAIR)]
MOST = [array(SPLITS, WIDTH, CHIPS * PAIR), array(WIDTH, CHIPS * PAIR), array(24, WIDTH)]


def most_outputs(where, back, store):
    square = array(8, WIDTH, WIDTH)
    buffers = [array(8, SPLITS, WIDTH, WIDTH), square, square, array(8, 40, WIDTH)]
    buffers += [array(WIDTH, WIDTH)] * 3
    return pl.pallas_call(
        most_kernel,
        out_shape=MOST,
        grid=(1,),
        in_specs=[SM, whole(*back.shape), HBM],
        out_specs=[whole(*value.shape) for value in MOST],
        scratch_shapes=[pltpu.VMEM(value.shape, F32) for value in buffers]
        + [pltpu.SemaphoreType.DMA((6,))],
        compiler_params=params(24),
        cost_estimate=cost(5),
        name="most_outputs",
    )(where, back, store)


def last_outputs(where, most, opposite, following, before):
    inputs = [*most, opposite, following, before]
    buffers = [*OUTPUTS, array(3, WIDTH, WIDTH), array(3, WIDTH, WIDTH)]
    buffers += [array(WIDTH, WIDTH)] * 2
    return pl.pallas_call(
        last_kernel,
        out_shape=OUTPUTS,
        grid=(1,),
        in_specs=[SM] + [whole(*value.shape) for value in inputs],
        out_specs=[HBM, HBM],
        scratch_shapes=[pltpu.VMEM(value.shape, F32) for value in buffers]
        + [pltpu.SemaphoreType.DMA((SPLITS + 1,))],
        compiler_params=params(24),
        cost_estimate=cost(3),
        name="last_outputs",
    )(where, *inputs)


def window_kernel(
    where_ref, mine_ref, other_ref, gram_ref, stat_ref, total_ref,
    out_ref, cent_ref, flip_ref, sum_ref,
):
    halves = (
        (mine_ref, 0), (other_ref, 0), (mine_ref, HALO), (other_ref, 3 * HALO),
        (mine_ref, 2 * HALO), (other_ref, 2 * HALO), (other_ref, HALO), (mine_ref, 3 * HALO),
    )
    live = jnp.where(where_ref[0] > 0, 1.0, 0.0).astype(F32)
    core = where_ref[2]
    at = pl.multiple_of(core * WIDTH, WIDTH)
    off = pl.multiple_of((1 - core) * WIDTH, WIDTH)
    count = ROWS + live * HALO
    scale = wide(1.0 / jnp.full((1, WIDTH), count, F32))
    unbias = wide(1.0 / jnp.full((1, WIDTH), count - 1.0, F32))
    step = 256
    for r in range(CHIPS):
        lanes = (at, off) if r == 0 else (0, WIDTH)
        for (raw, row), lane in zip(halves[2 * r : 2 * r + 2], lanes):
            mean = stat_ref[r, 0:1, pl.ds(lane, WIDTH)]

            def shift(i, _, raw=raw, row=row, lane=lane, mean=mean):
                piece = (raw[pl.ds(row + i * step, step), :].astype(F32) - mean) * live
                cent_ref[pl.ds(i * step, step), pl.ds(lane, WIDTH)] = piece.astype(BF16)
                return 0

            lax.fori_loop(0, HALO // step, shift, 0, unroll=2)
        if r == 0:
            flip_ref[...] = cent_ref[:, pl.ds(at, WIDTH)].T
            flipped = flip_ref[...]
            row_sum = jnp.dot(flipped, jnp.ones((HALO, WIDTH), BF16), preferred_element_type=F32)
            sum_ref[...] = row_sum + total_ref[...]
        cent = cent_ref[...]
        halo = jnp.dot(flip_ref[...], cent, preferred_element_type=F32)
        col_sum = jnp.dot(jnp.ones((16, HALO), BF16), cent, preferred_element_type=F32)[0:1]
        col_sum = col_sum + stat_ref[r, 1:2, :]
        value = (halo + gram_ref[r] - wide(sum_ref[...]) * (col_sum * scale)) * unbias
        for c in range(2):
            lane = pl.multiple_of(where_ref[4 + 2 * r + c] * WIDTH, WIDTH)
            out_ref[0, :, pl.ds(lane, WIDTH)] = value[:, c * WIDTH : (c + 1) * WIDTH]


def late_kernel(
    where_ref, mine_ref, other_ref, total_ref, sums_ref, gram_ref, stat_ref, own_ref, ahead_ref, behind_ref, far_ref, flags_ref,
    turned_ref, cols_ref, coef_ref, before_ref, after_ref, window_ref, vectors, cent_ref, flip_ref, sum_ref,
):
    prep_kernel(
        where_ref, sums_ref, gram_ref, stat_ref, own_ref, ahead_ref, behind_ref, far_ref, flags_ref,
        turned_ref, cols_ref, coef_ref, before_ref, after_ref, vectors,
    )
    window_kernel(
        where_ref, mine_ref, other_ref, gram_ref, stat_ref, total_ref, window_ref, cent_ref, flip_ref, sum_ref
    )


def late_terms(where, mine, other, total, sums, gram, stat, means, flags, store):
    square = (8, WIDTH, WIDTH)
    return call(
        late_kernel,
        "late_terms",
        [where, mine, other, total, sums, gram, stat, *means, flags],
        [array(1, WIDTH, CHIPS * PAIR)],
        store=store,
        puts=(
            ((WIDTH, WIDTH), (11, 0)),
            ((8, 40, WIDTH), (10, slice(None), pl.ds(0, 40))),
            ((24, WIDTH), (11, 1, pl.ds(0, 24))),
            (square, 8),
            (square, 9),
        ),
        fetched=(3, 4, 5, 6, 7, 11),
        stored=(0,),
        scratch=[
            ((WIDTH, WIDTH), F32),
            ((HALO, PAIR), BF16),
            ((WIDTH, HALO), BF16),
            ((WIDTH, WIDTH), F32),
        ],
        us=0.1,
    )


def to_chan(value, target):
    count = lax.axis_size("chan")
    return lax.ppermute(value, "chan", [(s, target(s) % count) for s in range(count)])


def exchange(value):
    return lax.all_to_all(value, "tm", 0, 0, tiled=True)


def after(value, *others):
    return lax.optimization_barrier((value, *others))[0]


def local(samples, candidates, segment_start):
    here, index = lax.axis_index("tm"), lax.axis_index("chan")
    chip, core = index // 2, index % 2
    nearby = [2 * chip, 2 * chip + 1]
    for step, side in ((1, core), (3, 1 - core), (2, core), (2, 1 - core), (1, 1 - core), (3, core)):
        nearby.append(2 * ((chip + step) % CHIPS) + side)
    held = jnp.where(chip < CHIPS // 2, 0, 1)
    where = jnp.stack([here, chip, core, held] + nearby).astype(jnp.int32)
    where = jnp.concatenate([where, candidates[0], segment_start])

    behind = to_chan(samples, lambda s: s + 2)
    ahead = to_chan(samples, lambda s: s - 2)
    other = to_chan(samples, lambda s: s ^ 1)
    prior = lax.ppermute(samples[ROWS - HALO :], "tm", [(b, b + 1) for b in range(BLOCKS - 1)])
    flip_shape, square = array(WIDTH, ROWS, dtype=BF16), array(WIDTH, WIDTH)
    store, sums, gram, stat, late_flipped, late_total, flipped, spread0, total, rider = call(
        first_kernel,
        "first_pair",
        [where, samples, other],
        ALL + [flip_shape, square, flip_shape, array(WIDTH, PAIR), square, array(8, WIDTH)],
        puts=((SHARD_PAIR, pl.ds(0, 2)),),
        fetched=(1,),
        stored=(0, 1, 2, 3, 4),
        scratch=[((ROWS, PAIR), BF16)],
    )
    behind, ahead, prior, flipped = lax.optimization_barrier((behind, ahead, prior, flipped))
    half = ROWS // 2
    far_low = to_chan(behind[:half], lambda s: s + 2)
    far_high = to_chan(ahead[half:], lambda s: s - 2)
    behind_other = to_chan(behind, lambda s: s ^ 1)
    ahead_other = to_chan(ahead, lambda s: s ^ 1)
    store, sums, gram, stat, spread1 = call(
        near_kernel,
        "near_pair",
        [where, ahead, behind_other, flipped, total],
        ALL + [array(WIDTH, PAIR)],
        store=store,
        puts=((SHARD_PAIR, pl.ds(2, 2)),),
        stored=(0, 1, 2),
        kept=(sums, gram, stat),
        pair=1,
        scratch=[((ROWS, PAIR), BF16)],
    )
    cent_shape = array(ROWS, PAIR, dtype=BF16)
    gram, stat, side = call(
        side_kernel,
        "side_pair",
        [where, ahead_other, behind, flipped],
        ALL[1:] + [cent_shape],
        stored=(0, 1),
        kept=(gram, stat),
        pair=3,
        us=0.1,
    )
    far_low, far_high, stat = lax.optimization_barrier((far_low, far_high, stat))
    far = jnp.concatenate([far_low, far_high], axis=0)
    far_other = to_chan(far, lambda s: s ^ 1)
    gram, stat, pieces, cent = call(
        far_kernel,
        "far_pair",
        [where, far, far_other, flipped, total, spread0, spread1, rider],
        ALL[1:] + [array(BLOCKS, 24, WIDTH), cent_shape],
        stored=(0, 1, 3),
        kept=(gram, stat),
        pair=2,
        scratch=[((WIDTH, WIDTH), F32)],
        us=0.1,
    )
    arrived = exchange(pieces)

    store, sums = call(
        rest_kernel,
        "rest_left",
        [where, after(side, cent), late_flipped],
        ALL[:1],
        store=store,
        puts=((SHARD_PAIR, pl.ds(6, 2)),),
        fetched=(2,),
        stored=(0,),
        kept=(sums,),
        pair=3,
        us=4,
    )
    prior = after(prior, sums)
    prior_behind = to_chan(prior, lambda s: s + 2)
    prior_ahead = to_chan(prior, lambda s: s - 2)
    store, sums = call(
        rest_kernel,
        "rest_left",
        [where, cent, late_flipped],
        ALL[:1],
        store=store,
        puts=((SHARD_PAIR, pl.ds(4, 2)),),
        fetched=(1, 2),
        stored=(0,),
        kept=(sums,),
        pair=2,
        us=2,
    )
    arrived, prior_behind, prior_ahead, sums = lax.optimization_barrier(
        (arrived, prior_behind, prior_ahead, sums)
    )
    half = HALO // 2
    prior_low = to_chan(prior_behind[:half], lambda s: s + 2)
    prior_high = to_chan(prior_ahead[half:], lambda s: s - 2)
    prior = jnp.concatenate([prior, prior_ahead, prior_low, prior_high, prior_behind], axis=0)
    prior_other = to_chan(prior, lambda s: s ^ 1)
    scanned, own_means, flags = call(
        scan_kernel,
        "scan_pieces",
        [arrived],
        [array(BLOCKS, 40, WIDTH), array(2, BLOCKS, WIDTH), array(BLOCKS, WIDTH)],
        stored=(0, 1, 2),
        us=1,
    )
    back = exchange(scanned)
    ahead_means = to_chan(own_means, lambda s: s - 2)
    behind_means = to_chan(own_means, lambda s: s + 2)
    far_means = to_chan(own_means, lambda s: s + 4)
    means = (own_means, ahead_means, behind_means, far_means)
    store, window_cov = late_terms(
        where, prior, prior_other, late_total, sums, gram, stat, means, flags, store
    )
    back, store, window_cov = lax.optimization_barrier((back, store, window_cov))
    before = to_chan(back[16:24, 0:32], lambda s: s + 2)
    following = to_chan(back[24:32, 0:32], lambda s: (s - 2) ^ 1)
    opposite = to_chan(back[:, 32:40], lambda s: s + 4 if s < 4 else (s - 4) ^ 1)
    most = most_outputs(where, back, store)
    cusum, segment_cov = last_outputs(where, most, opposite, following, before)
    return window_cov, segment_cov, cusum


def solution(mesh):
    placed = (P("tm", "chan"), P("tm", None), P("tm"))
    return jax.shard_map(
        local,
        mesh=mesh,
        in_specs=placed,
        out_specs=(P("tm", "chan", None), P("tm", "chan", None), P("tm", None, "chan", None)),
        check_vma=False,
    )
```

```python
import jax
import jax.numpy as jnp
from jax import lax
from jax.experimental import pallas as pl
from jax.experimental.pallas import tpu as pltpu
from jax.sharding import PartitionSpec as P

F32, BF16 = jnp.float32, jnp.bfloat16
ROWS, HALO, WIDTH, BLOCKS, SPLITS, CHIPS = 2048, 1024, 128, 32, 8, 4
PAIR = 2 * WIDTH
HIGH = lax.Precision.HIGHEST
TRANSPOSED = (((0,), (0,)), ((), ()))
SM = pl.BlockSpec(memory_space=pltpu.SMEM)
HBM = pl.BlockSpec(memory_space=pltpu.HBM)
MIB = 2**20


def whole(*shape):
    return pl.BlockSpec(shape, lambda *_: (0,) * len(shape))


def array(*shape, dtype=F32):
    return jax.ShapeDtypeStruct(shape, dtype)


def params(grant):
    return pltpu.CompilerParams(
        vmem_limit_bytes=grant * MIB, dimension_semantics=("arbitrary",)
    )


def cost(microseconds):
    return pl.CostEstimate(
        flops=int(microseconds * 1e9), bytes_accessed=MIB, transcendentals=0
    )


def center_shard(raw_ref, out_ref, at):
    step = 256

    def add(i, total):
        piece = raw_ref[pl.ds(i * step, step), :].astype(F32)
        return total + jnp.sum(piece.reshape(step // 8, 8, WIDTH), axis=0)

    total = lax.fori_loop(0, ROWS // step, add, jnp.zeros((8, WIDTH), F32), unroll=2)
    mean = jnp.sum(total, axis=0, keepdims=True) / ROWS

    def shift(i, _):
        piece = raw_ref[pl.ds(i * step, step), :].astype(F32) - mean
        out_ref[pl.ds(i * step, step), pl.ds(at, WIDTH)] = piece.astype(BF16)
        return 0

    lax.fori_loop(0, ROWS // step, shift, 0, unroll=2)
    return mean


def center_pair(first_ref, second_ref, at, off, cent_ref, stat_ref):
    stat_ref[0] = jnp.zeros((8, PAIR), F32)
    stat_ref[0, 0:1, pl.ds(at, WIDTH)] = center_shard(first_ref, cent_ref, at)
    stat_ref[0, 0:1, pl.ds(off, WIDTH)] = center_shard(second_ref, cent_ref, off)
    total = jnp.dot(jnp.ones((16, ROWS), BF16), cent_ref[...], preferred_element_type=F32)[0:1]
    stat_ref[0, 1:2, :] = total
    stat_ref[0, 2:3, :] = stat_ref[0, 0:1, :] + total / ROWS


def turned_dot(left, right):
    return lax.dot_general(left, right, TRANSPOSED, preferred_element_type=F32)


def wide(value):
    return jnp.concatenate([value, value], axis=1)


def left_part(where_ref, flipped, cent_ref, left_ref, sums_ref, block=0):
    index = lax.broadcasted_iota(jnp.int32, (16, ROWS), 0)
    place = lax.broadcasted_iota(jnp.int32, (16, ROWS), 1)
    limit = jnp.zeros((16, ROWS), jnp.int32)
    for j in range(SPLITS):
        limit = jnp.where(index == j, where_ref[12 + j], limit)
    masks = jnp.where(place < limit, 1.0, 0.0).astype(BF16)
    cent = cent_ref[...]
    sums_ref[block] = jnp.dot(masks, cent, preferred_element_type=F32)[0:8]
    for i in range(SPLITS // 4):
        kept = jnp.concatenate([flipped * masks[j : j + 1, :] for j in range(4 * i, 4 * i + 4)], axis=0)
        part = jnp.dot(kept, cent, preferred_element_type=F32)
        for j in range(4):
            for c in range(2):
                rows, lanes = slice(j * WIDTH, (j + 1) * WIDTH), slice(c * WIDTH, (c + 1) * WIDTH)
                left_ref[c, 4 * i + j] = part[rows, lanes]


def first_kernel(
    where_ref, mine_ref, other_ref,
    left_ref, sums_ref, gram_ref, stat_ref, flip_hbm, total_hbm, flip_ref, spread_ref, total_ref, rider_ref, cent_ref,
):
    core = where_ref[2]
    at = pl.multiple_of(core * WIDTH, WIDTH)
    off = pl.multiple_of((1 - core) * WIDTH, WIDTH)
    center_pair(mine_ref, other_ref, at, off, cent_ref, stat_ref)
    rider_ref[...] = jnp.zeros((8, WIDTH), F32)
    rider_ref[0:1, :] = stat_ref[0, 2:3, 0:WIDTH]
    rider_ref[1:2, :] = stat_ref[0, 2:3, WIDTH:PAIR]
    rider_ref[2:3, :] = jnp.full((1, WIDTH), where_ref[20], jnp.int32).astype(F32)
    flip_ref[...] = cent_ref[:, pl.ds(at, WIDTH)].T
    flipped = flip_ref[...]
    flip_hbm[...] = flipped
    gram = jnp.dot(flipped, cent_ref[...], preferred_element_type=F32)
    gram_ref[0] = gram
    total = jnp.dot(flipped, jnp.ones((ROWS, WIDTH), BF16), preferred_element_type=F32)
    total_ref[...] = total
    total_hbm[...] = total
    spread_ref[...] = gram - wide(total) * (stat_ref[0, 1:2, :] / ROWS)
    left_part(where_ref, flipped, cent_ref, left_ref, sums_ref)


def near_kernel(
    where_ref, first_ref, second_ref, flip_ref, total_ref,
    left_ref, sums_ref, gram_ref, stat_ref, spread_ref, cent_ref,
):
    center_pair(first_ref, second_ref, 0, WIDTH, cent_ref, stat_ref)
    flipped = flip_ref[...]
    gram = jnp.dot(flipped, cent_ref[...], preferred_element_type=F32)
    gram_ref[0] = gram
    spread_ref[...] = gram - wide(total_ref[...]) * (stat_ref[0, 1:2, :] / ROWS)
    left_part(where_ref, flipped, cent_ref, left_ref, sums_ref)


def side_kernel(
    where_ref, first_ref, second_ref, flip_ref, left_ref, sums_ref, gram_ref, stat_ref, cent_ref
):
    center_pair(first_ref, second_ref, 0, WIDTH, cent_ref, stat_ref)
    flipped = flip_ref[...]
    gram_ref[0] = jnp.dot(flipped, cent_ref[...], preferred_element_type=F32)
    left_part(where_ref, flipped, cent_ref, left_ref, sums_ref)


def far_kernel(
    where_ref, first_ref, second_ref, flip_ref, total_ref, spread0_ref, spread1_ref, rider_ref,
    gram_ref, stat_ref, out_ref, held_ref, cent_ref,
):
    rider = rider_ref[0:4, :]
    for q in range(BLOCKS):
        spread, lane = ((spread0_ref, spread1_ref)[q // 16], WIDTH * (q // 8 % 2))
        row = 16 * (q % 8)
        out_ref[q, 0:16, :] = spread[row : row + 16, lane : lane + WIDTH]
        out_ref[q, 20:24, :] = rider
    center_pair(first_ref, second_ref, 0, WIDTH, cent_ref, stat_ref)
    gram = jnp.dot(flip_ref[...], cent_ref[...], preferred_element_type=F32)
    gram_ref[0] = gram
    spread = gram - wide(total_ref[...]) * (stat_ref[0, 1:2, :] / ROWS)
    held_ref[...] = jnp.where(where_ref[3] == 0, spread[:, 0:WIDTH], spread[:, WIDTH:PAIR])
    for q in range(BLOCKS):
        out_ref[q, 16:20, :] = held_ref[4 * q : 4 * q + 4, :]


def rest_kernel(where_ref, first_ref, second_ref, flip_ref, left_ref, sums_ref, cent_ref, stat_ref):
    center_pair(first_ref, second_ref, 0, WIDTH, cent_ref, stat_ref)
    left_part(where_ref, flip_ref[...], cent_ref, left_ref, sums_ref)


ALL = [
    array(CHIPS, 8, PAIR),
    array(CHIPS, WIDTH, PAIR),
    array(CHIPS, 8, PAIR),
]


STORE = array(96, 8, WIDTH, WIDTH)
SHARD_PAIR = (2, SPLITS, WIDTH, WIDTH)


def call(
    kernel, name, inputs, outputs, *, store=None, puts=(), fetched=(), stored=(), kept=(),
    pair=0, span=1, scratch=(), us=3, grant=24,
):
    kept = (*([store] if store is not None else []), *kept)
    count, made, first = len(inputs), len(outputs), 1 if puts else 0
    sliced = [out in ALL for out in outputs]
    sizes = [(span, *out.shape[1:]) if cut else out.shape for out, cut in zip(outputs, sliced)]
    buffers = [pltpu.VMEM(inputs[i].shape, inputs[i].dtype) for i in fetched]
    buffers += [pltpu.VMEM(shape, F32) for shape, _ in puts]
    buffers += [pltpu.VMEM(sizes[i], outputs[i].dtype) for i in stored]

    def body(*refs):
        ins, refs = list(refs[:count]), refs[count + len(kept) :]
        slots, outs, refs = refs[:first], list(refs[first : first + made]), refs[first + made :]
        own, buffer, sem = refs[: len(scratch)], refs[len(scratch) : -1], refs[-1]
        copies = []
        for c, i in enumerate(fetched):
            copies.append(pltpu.make_async_copy(ins[i], buffer[c], sem.at[c]))
            ins[i] = buffer[c]
        for copy in copies:
            copy.start()
        for copy in copies:
            copy.wait()
        copies, mine = [], []
        for c, (_, place) in enumerate(puts, len(fetched)):
            copies.append(pltpu.make_async_copy(buffer[c], slots[0].at[place], sem.at[c]))
            mine.append(buffer[c])
        for c, i in enumerate(stored, len(fetched) + len(puts)):
            target = outs[i].at[pl.ds(pair, span)] if sliced[i] else outs[i]
            copies.append(pltpu.make_async_copy(buffer[c], target, sem.at[c]))
            outs[i] = buffer[c]
        kernel(*ins, *mine, *outs, *own)
        for copy in copies:
            copy.start()
        for copy in copies:
            copy.wait()

    ins = [SM if value.dtype == jnp.int32 else whole(*value.shape) for value in inputs]
    for i in fetched:
        ins[i] = HBM
    outs = [HBM if i in stored else whole(*out.shape) for i, out in enumerate(outputs)]
    aliased = range(first if store is None else 0, first + len(kept))
    return pl.pallas_call(
        body,
        out_shape=[STORE] * first + outputs,
        grid=(1,),
        in_specs=ins + [HBM] * len(kept),
        out_specs=[HBM] * first + outs,
        input_output_aliases={count + i: out for i, out in zip(range(len(kept)), aliased)},
        scratch_shapes=[pltpu.VMEM(shape, dtype) for shape, dtype in scratch]
        + buffers
        + [pltpu.SemaphoreType.DMA((max(len(buffers), 1),))],
        compiler_params=params(grant),
        cost_estimate=cost(us),
        name=name,
    )(*inputs, *kept)


def scan_kernel(arrived_ref, both_ref, means_ref, flags_ref):
    for b in range(BLOCKS):
        rider = arrived_ref[b, 16:24, :]
        means_ref[0, b : b + 1, :] = rider[4:5, :]
        means_ref[1, b : b + 1, :] = rider[5:6, :]
        flags_ref[b : b + 1, :] = rider[6:7, :]
    scan(arrived_ref, flags_ref, both_ref, 0, 16, 0)
    scan(arrived_ref, flags_ref, both_ref, 16, 4, 32)


def scan(arrived_ref, flags_ref, both_ref, row, size, at):
    zero = jnp.zeros((size, WIDTH), F32)
    running = zero
    for b in range(BLOCKS):
        begins = flags_ref[b : b + 1, :] > 0.5
        running = jnp.where(begins, zero, running)
        both_ref[b, at : at + size, :] = running
        running = running + arrived_ref[b, row : row + size, :]
    running = zero
    for b in reversed(range(BLOCKS)):
        begins = flags_ref[b : b + 1, :] > 0.5
        both_ref[b, at + size : at + 2 * size, :] = running
        running = jnp.where(begins, zero, running + arrived_ref[b, row : row + size, :])


def prep_kernel(
    where_ref, sums_ref, gram_ref, stat_ref, own_means_ref, ahead_ref, behind_ref, far_ref, flags_ref,
    turned_ref, cols_ref, coef_ref, before_ref, after_ref, vectors,
):
    here = where_ref[0]
    core = where_ref[2]
    away = 1 - core
    flags = flags_ref[...]
    spot = lax.broadcasted_iota(jnp.int32, (BLOCKS, WIDTH), 0)
    low = lax.broadcasted_iota(jnp.int32, (BLOCKS, BLOCKS), 1)
    high = lax.broadcasted_iota(jnp.int32, (BLOCKS, BLOCKS), 0)
    upto = jnp.dot((low <= high).astype(F32), flags, preferred_element_type=F32)
    mine = jnp.sum(jnp.where(spot <= here, flags, 0.0), axis=0, keepdims=True)
    same = jnp.abs(upto - mine) < 0.5
    masks = [
        jnp.where(same & (spot < here), 1.0, 0.0),
        jnp.where(same & (spot > here), 1.0, 0.0),
    ]
    totals = [jnp.sum(mask, axis=0, keepdims=True) for mask in masks]
    count_p, count_s = totals[0] * ROWS, totals[1] * ROWS

    def pooled(means, side):
        mask = masks[side]
        mean = jnp.sum(means * mask, axis=0, keepdims=True) / jnp.maximum(totals[side], 1.0)
        return mean, (means - mean) * mask

    def pick(value):
        return jnp.where(core == 0, value[:, 0:WIDTH], value[:, WIDTH:PAIR])

    row_means = own_means_ref[core]
    row_p, row_part_p = pooled(row_means, 0)
    row_s, row_part_s = pooled(row_means, 1)
    row_stat = pick(stat_ref[0])
    row_sums = pick(sums_ref[0])

    index = lax.broadcasted_iota(jnp.int32, (SPLITS, WIDTH), 0)
    k = jnp.zeros((SPLITS, WIDTH), jnp.int32)
    for j in range(SPLITS):
        k = jnp.where(index == j, where_ref[12 + j], k)
    k = k.astype(F32)
    rest = ROWS - k
    row_right = row_stat[1:2] - row_sums
    row_d = row_stat[0:1] + row_sums / k - row_p
    row_e = row_s - (row_stat[0:1] + row_right / rest)
    n_left, n_right = count_p + k, rest + count_s
    n = n_left + n_right
    weight = n_left * n_right / (n * n)
    a, b = weight / n_left, weight / n_right
    coef_ref[0:8, :] = a
    coef_ref[8:16, :] = b
    vectors[0:8, :] = -a * row_sums / k
    vectors[8:16, :] = a * (count_p * k / n_left) * row_d
    vectors[16:24, :] = b * row_right / rest
    vectors[24:32, :] = -b * (rest * count_s / n_right) * row_e
    total = count_p + ROWS
    n = total + count_s
    row_d = row_stat[2:3] - row_p
    row_e = row_s - (row_p + row_d * (ROWS / total))
    coef_ref[16:24, :] = jnp.broadcast_to(1.0 / n, (8, WIDTH))
    vectors[32:WIDTH, :] = jnp.zeros((WIDTH - 32, WIDTH), F32)
    vectors[32:33, :] = row_stat[1:2] / -ROWS / n
    vectors[33:34, :] = (count_p * ROWS / total) / n * row_d
    vectors[34:35, :] = (total * count_s / n) / n * row_e
    turned_ref[...] = vectors[...].T

    columns = (
        (own_means_ref[0], own_means_ref[1]),
        (ahead_ref[core], behind_ref[away]),
        (far_ref[core], far_ref[away]),
        (ahead_ref[away], behind_ref[core]),
    )
    for u in range(8):
        r, lanes = u // 2, slice(WIDTH * (u % 2), WIDTH * (u % 2) + WIDTH)
        means = columns[r][u % 2]
        col_p, col_part_p = pooled(means, 0)
        col_s, col_part_s = pooled(means, 1)
        stat = stat_ref[r, :, lanes]
        col_left = sums_ref[r, :, lanes]
        col_right = stat[1:2] - col_left
        cols_ref[u, 0:8, :] = col_left
        cols_ref[u, 8:16, :] = stat[0:1] + col_left / k - col_p
        cols_ref[u, 16:24, :] = col_right
        cols_ref[u, 24:32, :] = col_s - (stat[0:1] + col_right / rest)
        col_d = stat[2:3] - col_p
        cols_ref[u, 32:40, :] = jnp.zeros((8, WIDTH), F32)
        cols_ref[u, 32:33, :] = stat[1:2]
        cols_ref[u, 33:34, :] = col_d
        cols_ref[u, 34:35, :] = col_s - (col_p + col_d * (ROWS / total))

        def between(row_part, col_part):
            return ROWS * lax.dot_general(
                row_part, col_part, TRANSPOSED, precision=HIGH, preferred_element_type=F32
            )

        before_ref[u] = between(row_part_p, col_part_p)
        after_ref[u] = gram_ref[r, :, lanes] + between(row_part_s, col_part_s)


def load_near(ref, p_ref, s_ref):
    for g in range(8):
        p_ref[16 * g : 16 * g + 16, :] = ref[g, 0:16, :]
        s_ref[16 * g : 16 * g + 16, :] = ref[g, 16:32, :]


def load_far(ref, p_ref, s_ref):
    for q in range(BLOCKS):
        p_ref[4 * q : 4 * q + 4, :] = ref[q, 0:4, :]
        s_ref[4 * q : 4 * q + 4, :] = ref[q, 4:8, :]


def shard_lanes(where_ref, u):
    return pl.ds(pl.multiple_of(where_ref[4 + u] * WIDTH, WIDTH), WIDTH)


def most_kernel(
    where_ref, back_ref, store_hbm, most_ref, seg_ref, coef_ref,
    left_ref, prefix_ref, suffix_ref, cols_ref, turned_ref, p_ref, s_ref, sem,
):
    loads = [
        pltpu.make_async_copy(source, target, sem.at[c])
        for c, (source, target) in enumerate(
            (
                (store_hbm.at[8], prefix_ref),
                (store_hbm.at[9], suffix_ref),
                (store_hbm.at[10, :, pl.ds(0, 40)], cols_ref),
                (store_hbm.at[11, 0], turned_ref),
                (store_hbm.at[11, 1, pl.ds(0, 24)], coef_ref),
                *(
                    (store_hbm.at[pl.ds(0, 8), j], left_ref.at[:, j])
                    for j in range(SPLITS)
                ),
            )
        )
    ]
    for load in loads:
        load.start()
    held = where_ref[3]
    for load in loads[:5]:
        load.wait()

    def add(u):
        prefix_ref[u] = prefix_ref[u] + p_ref[...]
        suffix_ref[u] = suffix_ref[u] + s_ref[...]

    for u in range(4):
        load_near(back_ref.at[pl.ds(8 * u, 8)], p_ref, s_ref)
        add(u)
    load_far(back_ref.at[:, pl.ds(32, 8)], p_ref, s_ref)
    add(4 + held)

    def spread_out(rows):
        return [jnp.broadcast_to(turned_ref[:, i : i + 1], (WIDTH, WIDTH)) for i in rows]

    turned = spread_out(range(32, 35))
    for u in range(8):
        value = (prefix_ref[u] + suffix_ref[u]) * coef_ref[16:17, :]
        for i in range(3):
            value = value + turned[i] * cols_ref[u, 32 + i : 33 + i, :]
        seg_ref[:, shard_lanes(where_ref, u)] = value
    for j in range(SPLITS):
        loads[5 + j].wait()
        turned = spread_out(range(j, 32, 8))
        a, b = coef_ref[j : j + 1, :], coef_ref[8 + j : 9 + j, :]
        for u in range(8):
            value = (a + b) * left_ref[u, j] + a * prefix_ref[u] - b * suffix_ref[u]
            for i in range(4):
                value = value + turned[i] * cols_ref[u, 8 * i + j : 8 * i + j + 1, :]
            most_ref[j, :, shard_lanes(where_ref, u)] = value


def last_kernel(
    where_ref, most_ref, most_seg_ref, coef_ref, opposite_ref, next_ref, before_ref, cusum_hbm, seg_hbm,
    cusum_ref, seg_ref, prefix_ref, suffix_ref, p_ref, s_ref, sem,
):
    shards = (5 - where_ref[3], 6, 7)
    for v, (ref, load) in enumerate(
        ((opposite_ref, load_far), (next_ref, load_near), (before_ref, load_near))
    ):
        load(ref, p_ref, s_ref)
        prefix_ref[v] = p_ref[...].T
        suffix_ref[v] = s_ref[...].T
    seg_ref[0] = most_seg_ref[...]
    for v, u in enumerate(shards):
        lanes = shard_lanes(where_ref, u)
        added = (prefix_ref[v] + suffix_ref[v]) * coef_ref[16:17, :]
        seg_ref[0, :, lanes] = most_seg_ref[:, lanes] + added
    stores = [pltpu.make_async_copy(seg_ref, seg_hbm, sem.at[SPLITS])]
    stores[0].start()
    for j in range(SPLITS):
        a, b = coef_ref[j : j + 1, :], coef_ref[8 + j : 9 + j, :]
        cusum_ref[0, j] = most_ref[j]
        for v, u in enumerate(shards):
            lanes = shard_lanes(where_ref, u)
            cusum_ref[0, j, :, lanes] = most_ref[j, :, lanes] + a * prefix_ref[v] - b * suffix_ref[v]
        store = pltpu.make_async_copy(
            cusum_ref.at[:, pl.ds(j, 1)], cusum_hbm.at[:, pl.ds(j, 1)], sem.at[j]
        )
        store.start()
        stores.append(store)
    for store in stores:
        store.wait()


OUTPUTS = [array(1, SPLITS, WIDTH, CHIPS * PAIR), array(1, WIDTH, CHIPS * PAIR)]
MOST = [array(SPLITS, WIDTH, CHIPS * PAIR), array(WIDTH, CHIPS * PAIR), array(24, WIDTH)]


def most_outputs(where, back, store):
    square = array(8, WIDTH, WIDTH)
    buffers = [array(8, SPLITS, WIDTH, WIDTH), square, square, array(8, 40, WIDTH)]
    buffers += [array(WIDTH, WIDTH)] * 3
    return pl.pallas_call(
        most_kernel,
        out_shape=MOST,
        grid=(1,),
        in_specs=[SM, whole(*back.shape), HBM],
        out_specs=[whole(*value.shape) for value in MOST],
        scratch_shapes=[pltpu.VMEM(value.shape, F32) for value in buffers]
        + [pltpu.SemaphoreType.DMA((5 + SPLITS,))],
        compiler_params=params(24),
        cost_estimate=cost(5),
        name="most_outputs",
    )(where, back, store)


def last_outputs(where, most, opposite, following, before):
    inputs = [*most, opposite, following, before]
    buffers = [*OUTPUTS, array(3, WIDTH, WIDTH), array(3, WIDTH, WIDTH)]
    buffers += [array(WIDTH, WIDTH)] * 2
    return pl.pallas_call(
        last_kernel,
        out_shape=OUTPUTS,
        grid=(1,),
        in_specs=[SM] + [whole(*value.shape) for value in inputs],
        out_specs=[HBM, HBM],
        scratch_shapes=[pltpu.VMEM(value.shape, F32) for value in buffers]
        + [pltpu.SemaphoreType.DMA((SPLITS + 1,))],
        compiler_params=params(24),
        cost_estimate=cost(3),
        name="last_outputs",
    )(where, *inputs)


def window_kernel(
    where_ref, mine_ref, other_ref, gram_ref, stat_ref, total_ref,
    out_ref, cent_ref, flip_ref, sum_ref,
):
    halves = (
        (mine_ref, 0), (other_ref, 0), (mine_ref, HALO), (other_ref, 3 * HALO),
        (mine_ref, 2 * HALO), (other_ref, 2 * HALO), (other_ref, HALO), (mine_ref, 3 * HALO),
    )
    live = jnp.where(where_ref[0] > 0, 1.0, 0.0).astype(F32)
    core = where_ref[2]
    at = pl.multiple_of(core * WIDTH, WIDTH)
    off = pl.multiple_of((1 - core) * WIDTH, WIDTH)
    count = ROWS + live * HALO
    scale = wide(1.0 / jnp.full((1, WIDTH), count, F32))
    unbias = wide(1.0 / jnp.full((1, WIDTH), count - 1.0, F32))
    step = 256
    for r in range(CHIPS):
        lanes = (at, off) if r == 0 else (0, WIDTH)
        for (raw, row), lane in zip(halves[2 * r : 2 * r + 2], lanes):
            mean = stat_ref[r, 0:1, pl.ds(lane, WIDTH)]

            def shift(i, _, raw=raw, row=row, lane=lane, mean=mean):
                piece = (raw[pl.ds(row + i * step, step), :].astype(F32) - mean) * live
                cent_ref[pl.ds(i * step, step), pl.ds(lane, WIDTH)] = piece.astype(BF16)
                return 0

            lax.fori_loop(0, HALO // step, shift, 0, unroll=2)
        if r == 0:
            flip_ref[...] = cent_ref[:, pl.ds(at, WIDTH)].T
            flipped = flip_ref[...]
            row_sum = jnp.dot(flipped, jnp.ones((HALO, WIDTH), BF16), preferred_element_type=F32)
            sum_ref[...] = row_sum + total_ref[...]
        cent = cent_ref[...]
        halo = jnp.dot(flip_ref[...], cent, preferred_element_type=F32)
        col_sum = jnp.dot(jnp.ones((16, HALO), BF16), cent, preferred_element_type=F32)[0:1]
        col_sum = col_sum + stat_ref[r, 1:2, :]
        value = (halo + gram_ref[r] - wide(sum_ref[...]) * (col_sum * scale)) * unbias
        for c in range(2):
            lane = pl.multiple_of(where_ref[4 + 2 * r + c] * WIDTH, WIDTH)
            out_ref[0, :, pl.ds(lane, WIDTH)] = value[:, c * WIDTH : (c + 1) * WIDTH]


def late_kernel(
    where_ref, mine_ref, other_ref, total_ref, sums_ref, gram_ref, stat_ref, own_ref, ahead_ref, behind_ref, far_ref, flags_ref,
    turned_ref, cols_ref, coef_ref, before_ref, after_ref, window_ref, vectors, cent_ref, flip_ref, sum_ref,
):
    prep_kernel(
        where_ref, sums_ref, gram_ref, stat_ref, own_ref, ahead_ref, behind_ref, far_ref, flags_ref,
        turned_ref, cols_ref, coef_ref, before_ref, after_ref, vectors,
    )
    window_kernel(
        where_ref, mine_ref, other_ref, gram_ref, stat_ref, total_ref, window_ref, cent_ref, flip_ref, sum_ref
    )


def late_terms(where, mine, other, total, sums, gram, stat, means, flags, store):
    square = (8, WIDTH, WIDTH)
    return call(
        late_kernel,
        "late_terms",
        [where, mine, other, total, sums, gram, stat, *means, flags],
        [array(1, WIDTH, CHIPS * PAIR)],
        store=store,
        puts=(
            ((WIDTH, WIDTH), (11, 0)),
            ((8, 40, WIDTH), (10, slice(None), pl.ds(0, 40))),
            ((24, WIDTH), (11, 1, pl.ds(0, 24))),
            (square, 8),
            (square, 9),
        ),
        fetched=(3, 4, 5, 6, 7, 11),
        stored=(0,),
        scratch=[
            ((WIDTH, WIDTH), F32),
            ((HALO, PAIR), BF16),
            ((WIDTH, HALO), BF16),
            ((WIDTH, WIDTH), F32),
        ],
        us=0.1,
    )


def to_chan(value, target):
    count = lax.axis_size("chan")
    return lax.ppermute(value, "chan", [(s, target(s) % count) for s in range(count)])


def exchange(value):
    return lax.all_to_all(value, "tm", 0, 0, tiled=True)


def after(value, *others):
    return lax.optimization_barrier((value, *others))[0]


def local(samples, candidates, segment_start):
    here, index = lax.axis_index("tm"), lax.axis_index("chan")
    chip, core = index // 2, index % 2
    nearby = [2 * chip, 2 * chip + 1]
    for step, side in ((1, core), (3, 1 - core), (2, core), (2, 1 - core), (1, 1 - core), (3, core)):
        nearby.append(2 * ((chip + step) % CHIPS) + side)
    held = jnp.where(chip < CHIPS // 2, 0, 1)
    where = jnp.stack([here, chip, core, held] + nearby).astype(jnp.int32)
    where = jnp.concatenate([where, candidates[0], segment_start])

    behind = to_chan(samples, lambda s: s + 2)
    ahead = to_chan(samples, lambda s: s - 2)
    other = to_chan(samples, lambda s: s ^ 1)
    prior = lax.ppermute(samples[ROWS - HALO :], "tm", [(b, b + 1) for b in range(BLOCKS - 1)])
    flip_shape, square = array(WIDTH, ROWS, dtype=BF16), array(WIDTH, WIDTH)
    store, sums, gram, stat, late_flipped, late_total, flipped, spread0, total, rider = call(
        first_kernel,
        "first_pair",
        [where, samples, other],
        ALL + [flip_shape, square, flip_shape, array(WIDTH, PAIR), square, array(8, WIDTH)],
        puts=((SHARD_PAIR, pl.ds(0, 2)),),
        fetched=(1,),
        stored=(0, 1, 2, 3, 4),
        scratch=[((ROWS, PAIR), BF16)],
    )
    behind, ahead, prior, flipped = lax.optimization_barrier((behind, ahead, prior, flipped))
    half = ROWS // 2
    far_low = to_chan(behind[:half], lambda s: s + 2)
    far_high = to_chan(ahead[half:], lambda s: s - 2)
    behind_other = to_chan(behind, lambda s: s ^ 1)
    ahead_other = to_chan(ahead, lambda s: s ^ 1)
    store, sums, gram, stat, spread1 = call(
        near_kernel,
        "near_pair",
        [where, ahead, behind_other, flipped, total],
        ALL + [array(WIDTH, PAIR)],
        store=store,
        puts=((SHARD_PAIR, pl.ds(2, 2)),),
        stored=(0, 1, 2),
        kept=(sums, gram, stat),
        pair=1,
        scratch=[((ROWS, PAIR), BF16)],
    )
    store, sums, gram, stat = call(
        side_kernel,
        "side_pair",
        [where, ahead_other, behind, flipped],
        ALL,
        store=store,
        puts=((SHARD_PAIR, pl.ds(6, 2)),),
        stored=(0, 1, 2),
        kept=(sums, gram, stat),
        pair=3,
        scratch=[((ROWS, PAIR), BF16)],
        us=2,
    )
    far_low, far_high, stat = lax.optimization_barrier((far_low, far_high, stat))
    far = jnp.concatenate([far_low, far_high], axis=0)
    far_other = to_chan(far, lambda s: s ^ 1)
    gram, stat, pieces = call(
        far_kernel,
        "far_pair",
        [where, far, far_other, flipped, total, spread0, spread1, rider],
        ALL[1:] + [array(BLOCKS, 24, WIDTH)],
        stored=(0, 1),
        kept=(gram, stat),
        pair=2,
        scratch=[((WIDTH, WIDTH), F32), ((ROWS, PAIR), BF16)],
        us=0.1,
    )
    arrived = exchange(pieces)

    store, sums = call(
        rest_kernel,
        "rest_left",
        [where, after(far, pieces), far_other, late_flipped],
        ALL[:1],
        store=store,
        puts=((SHARD_PAIR, pl.ds(4, 2)),),
        fetched=(3,),
        stored=(0,),
        kept=(sums,),
        pair=2,
        scratch=[((ROWS, PAIR), BF16), ((1, 8, PAIR), F32)],
        us=4,
    )
    prior = after(prior, sums)
    prior_ahead = to_chan(prior, lambda s: s - 2)
    prior_behind = to_chan(prior, lambda s: s + 2)
    prior_far = to_chan(prior, lambda s: s + 4)
    arrived, prior_ahead = lax.optimization_barrier((arrived, prior_ahead))
    prior = jnp.concatenate([prior, prior_ahead, prior_far, prior_behind], axis=0)
    prior_other = to_chan(prior, lambda s: s ^ 1)
    scanned, own_means, flags = call(
        scan_kernel,
        "scan_pieces",
        [arrived],
        [array(BLOCKS, 40, WIDTH), array(2, BLOCKS, WIDTH), array(BLOCKS, WIDTH)],
        stored=(0, 1, 2),
        us=1,
    )
    back = exchange(scanned)
    ahead_means = to_chan(own_means, lambda s: s - 2)
    behind_means = to_chan(own_means, lambda s: s + 2)
    far_means = to_chan(own_means, lambda s: s + 4)
    means = (own_means, ahead_means, behind_means, far_means)
    store, window_cov = late_terms(
        where, prior, prior_other, late_total, sums, gram, stat, means, flags, store
    )
    back, store, window_cov = lax.optimization_barrier((back, store, window_cov))
    before = to_chan(back[16:24, 0:32], lambda s: s + 2)
    following = to_chan(back[24:32, 0:32], lambda s: (s - 2) ^ 1)
    opposite = to_chan(back[:, 32:40], lambda s: s + 4 if s < 4 else (s - 4) ^ 1)
    most = most_outputs(where, back, store)
    cusum, segment_cov = last_outputs(where, most, opposite, following, before)
    return window_cov, segment_cov, cusum


def solution(mesh):
    placed = (P("tm", "chan"), P("tm", None), P("tm"))
    return jax.shard_map(
        local,
        mesh=mesh,
        in_specs=placed,
        out_specs=(P("tm", "chan", None), P("tm", "chan", None), P("tm", None, "chan", None)),
        check_vma=False,
    )
```

```python
import jax
import jax.numpy as jnp
from jax import lax
from jax.experimental import pallas as pl
from jax.experimental.pallas import tpu as pltpu
from jax.sharding import PartitionSpec as P

F32, BF16 = jnp.float32, jnp.bfloat16
ROWS, HALO, WIDTH, BLOCKS, SPLITS, CHIPS = 2048, 1024, 128, 32, 8, 4
PAIR = 2 * WIDTH
HIGH = lax.Precision.HIGHEST
TRANSPOSED = (((0,), (0,)), ((), ()))
SM = pl.BlockSpec(memory_space=pltpu.SMEM)
HBM = pl.BlockSpec(memory_space=pltpu.HBM)
MIB = 2**20


def whole(*shape):
    return pl.BlockSpec(shape, lambda *_: (0,) * len(shape))


def array(*shape, dtype=F32):
    return jax.ShapeDtypeStruct(shape, dtype)


def params(grant):
    return pltpu.CompilerParams(
        vmem_limit_bytes=grant * MIB, dimension_semantics=("arbitrary",)
    )


def cost(microseconds):
    return pl.CostEstimate(
        flops=int(microseconds * 1e9), bytes_accessed=MIB, transcendentals=0
    )


def center_shard(raw_ref, out_ref, at):
    step = 256

    def add(i, total):
        piece = raw_ref[pl.ds(i * step, step), :].astype(F32)
        return total + jnp.sum(piece.reshape(step // 8, 8, WIDTH), axis=0)

    total = lax.fori_loop(0, ROWS // step, add, jnp.zeros((8, WIDTH), F32), unroll=2)
    mean = jnp.sum(total, axis=0, keepdims=True) / ROWS

    def shift(i, _):
        piece = raw_ref[pl.ds(i * step, step), :].astype(F32) - mean
        out_ref[pl.ds(i * step, step), pl.ds(at, WIDTH)] = piece.astype(BF16)
        return 0

    lax.fori_loop(0, ROWS // step, shift, 0, unroll=2)
    return mean


def center_pair(first_ref, second_ref, at, off, cent_ref, stat_ref):
    stat_ref[0] = jnp.zeros((8, PAIR), F32)
    stat_ref[0, 0:1, pl.ds(at, WIDTH)] = center_shard(first_ref, cent_ref, at)
    stat_ref[0, 0:1, pl.ds(off, WIDTH)] = center_shard(second_ref, cent_ref, off)
    total = jnp.dot(jnp.ones((16, ROWS), BF16), cent_ref[...], preferred_element_type=F32)[0:1]
    stat_ref[0, 1:2, :] = total
    stat_ref[0, 2:3, :] = stat_ref[0, 0:1, :] + total / ROWS


def turned_dot(left, right):
    return lax.dot_general(left, right, TRANSPOSED, preferred_element_type=F32)


def wide(value):
    return jnp.concatenate([value, value], axis=1)


def left_part(where_ref, flipped, cent_ref, left_ref, sums_ref, block=0):
    index = lax.broadcasted_iota(jnp.int32, (16, ROWS), 0)
    place = lax.broadcasted_iota(jnp.int32, (16, ROWS), 1)
    limit = jnp.zeros((16, ROWS), jnp.int32)
    for j in range(SPLITS):
        limit = jnp.where(index == j, where_ref[12 + j], limit)
    masks = jnp.where(place < limit, 1.0, 0.0).astype(BF16)
    cent = cent_ref[...]
    sums_ref[block] = jnp.dot(masks, cent, preferred_element_type=F32)[0:8]
    for i in range(SPLITS // 4):
        kept = jnp.concatenate([flipped * masks[j : j + 1, :] for j in range(4 * i, 4 * i + 4)], axis=0)
        part = jnp.dot(kept, cent, preferred_element_type=F32)
        for j in range(4):
            for c in range(2):
                rows, lanes = slice(j * WIDTH, (j + 1) * WIDTH), slice(c * WIDTH, (c + 1) * WIDTH)
                left_ref[c, 4 * i + j] = part[rows, lanes]


def first_kernel(
    where_ref, mine_ref, other_ref,
    left_ref, sums_ref, gram_ref, stat_ref, flip_hbm, total_hbm, flip_ref, spread_ref, total_ref, rider_ref, cent_ref,
):
    core = where_ref[2]
    at = pl.multiple_of(core * WIDTH, WIDTH)
    off = pl.multiple_of((1 - core) * WIDTH, WIDTH)
    center_pair(mine_ref, other_ref, at, off, cent_ref, stat_ref)
    rider_ref[...] = jnp.zeros((8, WIDTH), F32)
    rider_ref[0:1, :] = stat_ref[0, 2:3, 0:WIDTH]
    rider_ref[1:2, :] = stat_ref[0, 2:3, WIDTH:PAIR]
    rider_ref[2:3, :] = jnp.full((1, WIDTH), where_ref[20], jnp.int32).astype(F32)
    flip_ref[...] = cent_ref[:, pl.ds(at, WIDTH)].T
    flipped = flip_ref[...]
    flip_hbm[...] = flipped
    gram = jnp.dot(flipped, cent_ref[...], preferred_element_type=F32)
    gram_ref[0] = gram
    total = jnp.dot(flipped, jnp.ones((ROWS, WIDTH), BF16), preferred_element_type=F32)
    total_ref[...] = total
    total_hbm[...] = total
    spread_ref[...] = gram - wide(total) * (stat_ref[0, 1:2, :] / ROWS)
    left_part(where_ref, flipped, cent_ref, left_ref, sums_ref)


def near_kernel(
    where_ref, first_ref, second_ref, flip_ref, total_ref,
    left_ref, sums_ref, gram_ref, stat_ref, spread_ref, cent_ref,
):
    center_pair(first_ref, second_ref, 0, WIDTH, cent_ref, stat_ref)
    flipped = flip_ref[...]
    gram = jnp.dot(flipped, cent_ref[...], preferred_element_type=F32)
    gram_ref[0] = gram
    spread_ref[...] = gram - wide(total_ref[...]) * (stat_ref[0, 1:2, :] / ROWS)
    left_part(where_ref, flipped, cent_ref, left_ref, sums_ref)


def side_kernel(
    where_ref, first_ref, second_ref, flip_ref, left_ref, sums_ref, gram_ref, stat_ref, cent_ref
):
    center_pair(first_ref, second_ref, 0, WIDTH, cent_ref, stat_ref)
    flipped = flip_ref[...]
    gram_ref[0] = jnp.dot(flipped, cent_ref[...], preferred_element_type=F32)
    left_part(where_ref, flipped, cent_ref, left_ref, sums_ref)


def far_kernel(
    where_ref, first_ref, second_ref, flip_ref, total_ref, spread0_ref, spread1_ref, rider_ref,
    gram_ref, stat_ref, out_ref, held_ref, cent_ref,
):
    rider = rider_ref[0:4, :]
    for q in range(BLOCKS):
        spread, lane = ((spread0_ref, spread1_ref)[q // 16], WIDTH * (q // 8 % 2))
        row = 16 * (q % 8)
        out_ref[q, 0:16, :] = spread[row : row + 16, lane : lane + WIDTH]
        out_ref[q, 20:24, :] = rider
    center_pair(first_ref, second_ref, 0, WIDTH, cent_ref, stat_ref)
    gram = jnp.dot(flip_ref[...], cent_ref[...], preferred_element_type=F32)
    gram_ref[0] = gram
    spread = gram - wide(total_ref[...]) * (stat_ref[0, 1:2, :] / ROWS)
    held_ref[...] = jnp.where(where_ref[3] == 0, spread[:, 0:WIDTH], spread[:, WIDTH:PAIR])
    for q in range(BLOCKS):
        out_ref[q, 16:20, :] = held_ref[4 * q : 4 * q + 4, :]


def rest_kernel(where_ref, first_ref, second_ref, flip_ref, left_ref, sums_ref, cent_ref, stat_ref):
    center_pair(first_ref, second_ref, 0, WIDTH, cent_ref, stat_ref)
    left_part(where_ref, flip_ref[...], cent_ref, left_ref, sums_ref)


ALL = [
    array(CHIPS, 8, PAIR),
    array(CHIPS, WIDTH, PAIR),
    array(CHIPS, 8, PAIR),
]


STORE = array(96, 8, WIDTH, WIDTH)
SHARD_PAIR = (2, SPLITS, WIDTH, WIDTH)


def call(
    kernel, name, inputs, outputs, *, store=None, puts=(), fetched=(), stored=(), kept=(),
    pair=0, span=1, scratch=(), us=3, grant=24,
):
    kept = (*([store] if store is not None else []), *kept)
    count, made, first = len(inputs), len(outputs), 1 if puts else 0
    sliced = [out in ALL for out in outputs]
    sizes = [(span, *out.shape[1:]) if cut else out.shape for out, cut in zip(outputs, sliced)]
    buffers = [pltpu.VMEM(inputs[i].shape, inputs[i].dtype) for i in fetched]
    buffers += [pltpu.VMEM(shape, F32) for shape, _ in puts]
    buffers += [pltpu.VMEM(sizes[i], outputs[i].dtype) for i in stored]

    def body(*refs):
        ins, refs = list(refs[:count]), refs[count + len(kept) :]
        slots, outs, refs = refs[:first], list(refs[first : first + made]), refs[first + made :]
        own, buffer, sem = refs[: len(scratch)], refs[len(scratch) : -1], refs[-1]
        copies = []
        for c, i in enumerate(fetched):
            copies.append(pltpu.make_async_copy(ins[i], buffer[c], sem.at[c]))
            ins[i] = buffer[c]
        for copy in copies:
            copy.start()
        for copy in copies:
            copy.wait()
        copies, mine = [], []
        for c, (_, place) in enumerate(puts, len(fetched)):
            copies.append(pltpu.make_async_copy(buffer[c], slots[0].at[place], sem.at[c]))
            mine.append(buffer[c])
        for c, i in enumerate(stored, len(fetched) + len(puts)):
            target = outs[i].at[pl.ds(pair, span)] if sliced[i] else outs[i]
            copies.append(pltpu.make_async_copy(buffer[c], target, sem.at[c]))
            outs[i] = buffer[c]
        kernel(*ins, *mine, *outs, *own)
        for copy in copies:
            copy.start()
        for copy in copies:
            copy.wait()

    ins = [SM if value.dtype == jnp.int32 else whole(*value.shape) for value in inputs]
    for i in fetched:
        ins[i] = HBM
    outs = [HBM if i in stored else whole(*out.shape) for i, out in enumerate(outputs)]
    aliased = range(first if store is None else 0, first + len(kept))
    return pl.pallas_call(
        body,
        out_shape=[STORE] * first + outputs,
        grid=(1,),
        in_specs=ins + [HBM] * len(kept),
        out_specs=[HBM] * first + outs,
        input_output_aliases={count + i: out for i, out in zip(range(len(kept)), aliased)},
        scratch_shapes=[pltpu.VMEM(shape, dtype) for shape, dtype in scratch]
        + buffers
        + [pltpu.SemaphoreType.DMA((max(len(buffers), 1),))],
        compiler_params=params(grant),
        cost_estimate=cost(us),
        name=name,
    )(*inputs, *kept)


def scan_kernel(arrived_ref, both_ref, means_ref, flags_ref):
    for b in range(BLOCKS):
        rider = arrived_ref[b, 16:24, :]
        means_ref[0, b : b + 1, :] = rider[4:5, :]
        means_ref[1, b : b + 1, :] = rider[5:6, :]
        flags_ref[b : b + 1, :] = rider[6:7, :]
    scan(arrived_ref, flags_ref, both_ref, 0, 16, 0)
    scan(arrived_ref, flags_ref, both_ref, 16, 4, 32)


def scan(arrived_ref, flags_ref, both_ref, row, size, at):
    zero = jnp.zeros((size, WIDTH), F32)
    running = zero
    for b in range(BLOCKS):
        begins = flags_ref[b : b + 1, :] > 0.5
        running = jnp.where(begins, zero, running)
        both_ref[b, at : at + size, :] = running
        running = running + arrived_ref[b, row : row + size, :]
    running = zero
    for b in reversed(range(BLOCKS)):
        begins = flags_ref[b : b + 1, :] > 0.5
        both_ref[b, at + size : at + 2 * size, :] = running
        running = jnp.where(begins, zero, running + arrived_ref[b, row : row + size, :])


def prep_kernel(
    where_ref, sums_ref, gram_ref, stat_ref, own_means_ref, ahead_ref, behind_ref, far_ref, flags_ref,
    turned_ref, cols_ref, coef_ref, before_ref, after_ref, vectors,
):
    here = where_ref[0]
    core = where_ref[2]
    away = 1 - core
    flags = flags_ref[...]
    spot = lax.broadcasted_iota(jnp.int32, (BLOCKS, WIDTH), 0)
    low = lax.broadcasted_iota(jnp.int32, (BLOCKS, BLOCKS), 1)
    high = lax.broadcasted_iota(jnp.int32, (BLOCKS, BLOCKS), 0)
    upto = jnp.dot((low <= high).astype(F32), flags, preferred_element_type=F32)
    mine = jnp.sum(jnp.where(spot <= here, flags, 0.0), axis=0, keepdims=True)
    same = jnp.abs(upto - mine) < 0.5
    masks = [
        jnp.where(same & (spot < here), 1.0, 0.0),
        jnp.where(same & (spot > here), 1.0, 0.0),
    ]
    totals = [jnp.sum(mask, axis=0, keepdims=True) for mask in masks]
    count_p, count_s = totals[0] * ROWS, totals[1] * ROWS

    def pooled(means, side):
        mask = masks[side]
        mean = jnp.sum(means * mask, axis=0, keepdims=True) / jnp.maximum(totals[side], 1.0)
        return mean, (means - mean) * mask

    def pick(value):
        return jnp.where(core == 0, value[:, 0:WIDTH], value[:, WIDTH:PAIR])

    row_means = own_means_ref[core]
    row_p, row_part_p = pooled(row_means, 0)
    row_s, row_part_s = pooled(row_means, 1)
    row_stat = pick(stat_ref[0])
    row_sums = pick(sums_ref[0])

    index = lax.broadcasted_iota(jnp.int32, (SPLITS, WIDTH), 0)
    k = jnp.zeros((SPLITS, WIDTH), jnp.int32)
    for j in range(SPLITS):
        k = jnp.where(index == j, where_ref[12 + j], k)
    k = k.astype(F32)
    rest = ROWS - k
    row_right = row_stat[1:2] - row_sums
    row_d = row_stat[0:1] + row_sums / k - row_p
    row_e = row_s - (row_stat[0:1] + row_right / rest)
    n_left, n_right = count_p + k, rest + count_s
    n = n_left + n_right
    weight = n_left * n_right / (n * n)
    a, b = weight / n_left, weight / n_right
    coef_ref[0:8, :] = a
    coef_ref[8:16, :] = b
    vectors[0:8, :] = -a * row_sums / k
    vectors[8:16, :] = a * (count_p * k / n_left) * row_d
    vectors[16:24, :] = b * row_right / rest
    vectors[24:32, :] = -b * (rest * count_s / n_right) * row_e
    total = count_p + ROWS
    n = total + count_s
    row_d = row_stat[2:3] - row_p
    row_e = row_s - (row_p + row_d * (ROWS / total))
    coef_ref[16:24, :] = jnp.broadcast_to(1.0 / n, (8, WIDTH))
    vectors[32:WIDTH, :] = jnp.zeros((WIDTH - 32, WIDTH), F32)
    vectors[32:33, :] = row_stat[1:2] / -ROWS / n
    vectors[33:34, :] = (count_p * ROWS / total) / n * row_d
    vectors[34:35, :] = (total * count_s / n) / n * row_e
    turned_ref[...] = vectors[...].T

    columns = (
        (own_means_ref[0], own_means_ref[1]),
        (ahead_ref[core], behind_ref[away]),
        (far_ref[core], far_ref[away]),
        (ahead_ref[away], behind_ref[core]),
    )
    for u in range(8):
        r, lanes = u // 2, slice(WIDTH * (u % 2), WIDTH * (u % 2) + WIDTH)
        means = columns[r][u % 2]
        col_p, col_part_p = pooled(means, 0)
        col_s, col_part_s = pooled(means, 1)
        stat = stat_ref[r, :, lanes]
        col_left = sums_ref[r, :, lanes]
        col_right = stat[1:2] - col_left
        cols_ref[u, 0:8, :] = col_left
        cols_ref[u, 8:16, :] = stat[0:1] + col_left / k - col_p
        cols_ref[u, 16:24, :] = col_right
        cols_ref[u, 24:32, :] = col_s - (stat[0:1] + col_right / rest)
        col_d = stat[2:3] - col_p
        cols_ref[u, 32:40, :] = jnp.zeros((8, WIDTH), F32)
        cols_ref[u, 32:33, :] = stat[1:2]
        cols_ref[u, 33:34, :] = col_d
        cols_ref[u, 34:35, :] = col_s - (col_p + col_d * (ROWS / total))

        def between(row_part, col_part):
            return ROWS * lax.dot_general(
                row_part, col_part, TRANSPOSED, precision=HIGH, preferred_element_type=F32
            )

        before_ref[u] = between(row_part_p, col_part_p)
        after_ref[u] = gram_ref[r, :, lanes] + between(row_part_s, col_part_s)


def load_near(ref, p_ref, s_ref):
    for g in range(8):
        p_ref[16 * g : 16 * g + 16, :] = ref[g, 0:16, :]
        s_ref[16 * g : 16 * g + 16, :] = ref[g, 16:32, :]


def load_far(ref, p_ref, s_ref):
    for q in range(BLOCKS):
        p_ref[4 * q : 4 * q + 4, :] = ref[q, 0:4, :]
        s_ref[4 * q : 4 * q + 4, :] = ref[q, 4:8, :]


def shard_lanes(where_ref, u):
    return pl.ds(pl.multiple_of(where_ref[4 + u] * WIDTH, WIDTH), WIDTH)


def most_kernel(
    where_ref, back_ref, store_hbm, most_ref, seg_ref, coef_ref,
    left_ref, prefix_ref, suffix_ref, cols_ref, turned_ref, p_ref, s_ref, sem,
):
    loads = [
        pltpu.make_async_copy(source, target, sem.at[c])
        for c, (source, target) in enumerate(
            (
                (store_hbm.at[8], prefix_ref),
                (store_hbm.at[9], suffix_ref),
                (store_hbm.at[10, :, pl.ds(0, 40)], cols_ref),
                (store_hbm.at[11, 0], turned_ref),
                (store_hbm.at[11, 1, pl.ds(0, 24)], coef_ref),
                *(
                    (store_hbm.at[pl.ds(0, 8), j], left_ref.at[:, j])
                    for j in range(SPLITS)
                ),
            )
        )
    ]
    for load in loads:
        load.start()
    held = where_ref[3]
    for load in loads[:5]:
        load.wait()

    def add(u):
        prefix_ref[u] = prefix_ref[u] + p_ref[...]
        suffix_ref[u] = suffix_ref[u] + s_ref[...]

    for u in range(4):
        load_near(back_ref.at[pl.ds(8 * u, 8)], p_ref, s_ref)
        add(u)
    load_far(back_ref.at[:, pl.ds(32, 8)], p_ref, s_ref)
    add(4 + held)

    def spread_out(rows):
        return [jnp.broadcast_to(turned_ref[:, i : i + 1], (WIDTH, WIDTH)) for i in rows]

    turned = spread_out(range(32, 35))
    for u in range(8):
        value = (prefix_ref[u] + suffix_ref[u]) * coef_ref[16:17, :]
        for i in range(3):
            value = value + turned[i] * cols_ref[u, 32 + i : 33 + i, :]
        seg_ref[:, shard_lanes(where_ref, u)] = value
    for j in range(SPLITS):
        loads[5 + j].wait()
        turned = spread_out(range(j, 32, 8))
        a, b = coef_ref[j : j + 1, :], coef_ref[8 + j : 9 + j, :]
        for u in range(8):
            value = (a + b) * left_ref[u, j] + a * prefix_ref[u] - b * suffix_ref[u]
            for i in range(4):
                value = value + turned[i] * cols_ref[u, 8 * i + j : 8 * i + j + 1, :]
            most_ref[j, :, shard_lanes(where_ref, u)] = value


def last_kernel(
    where_ref, most_ref, most_seg_ref, coef_ref, opposite_ref, next_ref, before_ref, cusum_hbm, seg_hbm,
    cusum_ref, seg_ref, prefix_ref, suffix_ref, p_ref, s_ref, sem,
):
    shards = (5 - where_ref[3], 6, 7)
    for v, (ref, load) in enumerate(
        ((opposite_ref, load_far), (next_ref, load_near), (before_ref, load_near))
    ):
        load(ref, p_ref, s_ref)
        prefix_ref[v] = p_ref[...].T
        suffix_ref[v] = s_ref[...].T
    seg_ref[0] = most_seg_ref[...]
    for v, u in enumerate(shards):
        lanes = shard_lanes(where_ref, u)
        added = (prefix_ref[v] + suffix_ref[v]) * coef_ref[16:17, :]
        seg_ref[0, :, lanes] = most_seg_ref[:, lanes] + added
    stores = [pltpu.make_async_copy(seg_ref, seg_hbm, sem.at[SPLITS])]
    stores[0].start()
    for j in range(SPLITS):
        a, b = coef_ref[j : j + 1, :], coef_ref[8 + j : 9 + j, :]
        cusum_ref[0, j] = most_ref[j]
        for v, u in enumerate(shards):
            lanes = shard_lanes(where_ref, u)
            cusum_ref[0, j, :, lanes] = most_ref[j, :, lanes] + a * prefix_ref[v] - b * suffix_ref[v]
        store = pltpu.make_async_copy(
            cusum_ref.at[:, pl.ds(j, 1)], cusum_hbm.at[:, pl.ds(j, 1)], sem.at[j]
        )
        store.start()
        stores.append(store)
    for store in stores:
        store.wait()


OUTPUTS = [array(1, SPLITS, WIDTH, CHIPS * PAIR), array(1, WIDTH, CHIPS * PAIR)]
MOST = [array(SPLITS, WIDTH, CHIPS * PAIR), array(WIDTH, CHIPS * PAIR), array(24, WIDTH)]


def most_outputs(where, back, store):
    square = array(8, WIDTH, WIDTH)
    buffers = [array(8, SPLITS, WIDTH, WIDTH), square, square, array(8, 40, WIDTH)]
    buffers += [array(WIDTH, WIDTH)] * 3
    return pl.pallas_call(
        most_kernel,
        out_shape=MOST,
        grid=(1,),
        in_specs=[SM, whole(*back.shape), HBM],
        out_specs=[whole(*value.shape) for value in MOST],
        scratch_shapes=[pltpu.VMEM(value.shape, F32) for value in buffers]
        + [pltpu.SemaphoreType.DMA((5 + SPLITS,))],
        compiler_params=params(24),
        cost_estimate=cost(5),
        name="most_outputs",
    )(where, back, store)


def last_outputs(where, most, opposite, following, before):
    inputs = [*most, opposite, following, before]
    buffers = [*OUTPUTS, array(3, WIDTH, WIDTH), array(3, WIDTH, WIDTH)]
    buffers += [array(WIDTH, WIDTH)] * 2
    return pl.pallas_call(
        last_kernel,
        out_shape=OUTPUTS,
        grid=(1,),
        in_specs=[SM] + [whole(*value.shape) for value in inputs],
        out_specs=[HBM, HBM],
        scratch_shapes=[pltpu.VMEM(value.shape, F32) for value in buffers]
        + [pltpu.SemaphoreType.DMA((SPLITS + 1,))],
        compiler_params=params(24),
        cost_estimate=cost(3),
        name="last_outputs",
    )(where, *inputs)


def window_kernel(
    where_ref, halves, gram_ref, stat_ref, total_ref, out_ref, cent_ref, flip_ref, sum_ref,
):
    live = jnp.where(where_ref[0] > 0, 1.0, 0.0).astype(F32)
    core = where_ref[2]
    at = pl.multiple_of(core * WIDTH, WIDTH)
    off = pl.multiple_of((1 - core) * WIDTH, WIDTH)
    count = ROWS + live * HALO
    scale = wide(1.0 / jnp.full((1, WIDTH), count, F32))
    unbias = wide(1.0 / jnp.full((1, WIDTH), count - 1.0, F32))
    step = 256
    for r in range(CHIPS):
        lanes = (at, off) if r == 0 else (0, WIDTH)
        for raw, lane in zip(halves[2 * r : 2 * r + 2], lanes):
            mean = stat_ref[r, 0:1, pl.ds(lane, WIDTH)]

            def shift(i, _, raw=raw, lane=lane, mean=mean):
                piece = (raw[pl.ds(i * step, step), :].astype(F32) - mean) * live
                cent_ref[pl.ds(i * step, step), pl.ds(lane, WIDTH)] = piece.astype(BF16)
                return 0

            lax.fori_loop(0, HALO // step, shift, 0, unroll=2)
        if r == 0:
            flip_ref[...] = cent_ref[:, pl.ds(at, WIDTH)].T
            flipped = flip_ref[...]
            row_sum = jnp.dot(flipped, jnp.ones((HALO, WIDTH), BF16), preferred_element_type=F32)
            sum_ref[...] = row_sum + total_ref[...]
        cent = cent_ref[...]
        halo = jnp.dot(flip_ref[...], cent, preferred_element_type=F32)
        col_sum = jnp.dot(jnp.ones((16, HALO), BF16), cent, preferred_element_type=F32)[0:1]
        col_sum = col_sum + stat_ref[r, 1:2, :]
        value = (halo + gram_ref[r] - wide(sum_ref[...]) * (col_sum * scale)) * unbias
        for c in range(2):
            lane = pl.multiple_of(where_ref[4 + 2 * r + c] * WIDTH, WIDTH)
            out_ref[0, :, pl.ds(lane, WIDTH)] = value[:, c * WIDTH : (c + 1) * WIDTH]


def late_kernel(
    where_ref, h0, h1, h2, h3, h4, h5, h6, h7, total_ref, sums_ref, gram_ref, stat_ref,
    own_ref, ahead_ref, behind_ref, far_ref, flags_ref,
    turned_ref, cols_ref, coef_ref, before_ref, after_ref, window_ref, vectors, cent_ref, flip_ref, sum_ref,
):
    prep_kernel(
        where_ref, sums_ref, gram_ref, stat_ref, own_ref, ahead_ref, behind_ref, far_ref, flags_ref,
        turned_ref, cols_ref, coef_ref, before_ref, after_ref, vectors,
    )
    window_kernel(
        where_ref, (h0, h1, h2, h3, h4, h5, h6, h7), gram_ref, stat_ref, total_ref,
        window_ref, cent_ref, flip_ref, sum_ref,
    )


def late_terms(where, halves, total, sums, gram, stat, means, flags, store):
    square = (8, WIDTH, WIDTH)
    return call(
        late_kernel,
        "late_terms",
        [where, *halves, total, sums, gram, stat, *means, flags],
        [array(1, WIDTH, CHIPS * PAIR)],
        store=store,
        puts=(
            ((WIDTH, WIDTH), (11, 0)),
            ((8, 40, WIDTH), (10, slice(None), pl.ds(0, 40))),
            ((24, WIDTH), (11, 1, pl.ds(0, 24))),
            (square, 8),
            (square, 9),
        ),
        fetched=(9, 10, 11, 12, 13, 17),
        stored=(0,),
        scratch=[
            ((WIDTH, WIDTH), F32),
            ((HALO, PAIR), BF16),
            ((WIDTH, HALO), BF16),
            ((WIDTH, WIDTH), F32),
        ],
        us=0.1,
    )


def to_chan(value, target):
    count = lax.axis_size("chan")
    return lax.ppermute(value, "chan", [(s, target(s) % count) for s in range(count)])


def exchange(value):
    return lax.all_to_all(value, "tm", 0, 0, tiled=True)


def after(value, *others):
    return lax.optimization_barrier((value, *others))[0]


def local(samples, candidates, segment_start):
    here, index = lax.axis_index("tm"), lax.axis_index("chan")
    chip, core = index // 2, index % 2
    nearby = [2 * chip, 2 * chip + 1]
    for step, side in ((1, core), (3, 1 - core), (2, core), (2, 1 - core), (1, 1 - core), (3, core)):
        nearby.append(2 * ((chip + step) % CHIPS) + side)
    held = jnp.where(chip < CHIPS // 2, 0, 1)
    where = jnp.stack([here, chip, core, held] + nearby).astype(jnp.int32)
    where = jnp.concatenate([where, candidates[0], segment_start])

    behind = to_chan(samples, lambda s: s + 2)
    ahead = to_chan(samples, lambda s: s - 2)
    other = to_chan(samples, lambda s: s ^ 1)
    prior = lax.ppermute(samples[ROWS - HALO :], "tm", [(b, b + 1) for b in range(BLOCKS - 1)])
    flip_shape, square = array(WIDTH, ROWS, dtype=BF16), array(WIDTH, WIDTH)
    store, sums, gram, stat, late_flipped, late_total, flipped, spread0, total, rider = call(
        first_kernel,
        "first_pair",
        [where, samples, other],
        ALL + [flip_shape, square, flip_shape, array(WIDTH, PAIR), square, array(8, WIDTH)],
        puts=((SHARD_PAIR, pl.ds(0, 2)),),
        fetched=(1,),
        stored=(0, 1, 2, 3, 4),
        scratch=[((ROWS, PAIR), BF16)],
    )
    behind, ahead, prior, flipped = lax.optimization_barrier((behind, ahead, prior, flipped))
    half = ROWS // 2
    far_low = to_chan(behind[:half], lambda s: s + 2)
    far_high = to_chan(ahead[half:], lambda s: s - 2)
    behind_other = to_chan(behind, lambda s: s ^ 1)
    ahead_other = to_chan(ahead, lambda s: s ^ 1)
    store, sums, gram, stat, spread1 = call(
        near_kernel,
        "near_pair",
        [where, ahead, behind_other, flipped, total],
        ALL + [array(WIDTH, PAIR)],
        store=store,
        puts=((SHARD_PAIR, pl.ds(2, 2)),),
        stored=(0, 1, 2),
        kept=(sums, gram, stat),
        pair=1,
        scratch=[((ROWS, PAIR), BF16)],
    )
    store, sums, gram, stat = call(
        side_kernel,
        "side_pair",
        [where, ahead_other, behind, flipped],
        ALL,
        store=store,
        puts=((SHARD_PAIR, pl.ds(6, 2)),),
        stored=(0, 1, 2),
        kept=(sums, gram, stat),
        pair=3,
        scratch=[((ROWS, PAIR), BF16)],
        us=2,
    )
    far_low, far_high, stat = lax.optimization_barrier((far_low, far_high, stat))
    far = jnp.concatenate([far_low, far_high], axis=0)
    far_other = to_chan(far, lambda s: s ^ 1)
    gram, stat, pieces = call(
        far_kernel,
        "far_pair",
        [where, far, far_other, flipped, total, spread0, spread1, rider],
        ALL[1:] + [array(BLOCKS, 24, WIDTH)],
        stored=(0, 1),
        kept=(gram, stat),
        pair=2,
        scratch=[((WIDTH, WIDTH), F32), ((ROWS, PAIR), BF16)],
        us=0.1,
    )
    arrived = exchange(pieces)

    store, sums = call(
        rest_kernel,
        "rest_left",
        [where, after(far, pieces), far_other, late_flipped],
        ALL[:1],
        store=store,
        puts=((SHARD_PAIR, pl.ds(4, 2)),),
        fetched=(3,),
        stored=(0,),
        kept=(sums,),
        pair=2,
        scratch=[((ROWS, PAIR), BF16), ((1, 8, PAIR), F32)],
        us=4,
    )
    prior = after(prior, sums)
    prior_ahead = to_chan(prior, lambda s: s - 2)
    prior_behind = to_chan(prior, lambda s: s + 2)
    prior_far = to_chan(prior, lambda s: s + 4)
    arrived = after(arrived, sums)
    scanned, own_means, flags = call(
        scan_kernel,
        "scan_pieces",
        [arrived],
        [array(BLOCKS, 40, WIDTH), array(2, BLOCKS, WIDTH), array(BLOCKS, WIDTH)],
        stored=(0, 1, 2),
        us=1,
    )
    back = exchange(scanned)
    ahead_means = to_chan(own_means, lambda s: s - 2)
    behind_means = to_chan(own_means, lambda s: s + 2)
    far_means = to_chan(own_means, lambda s: s + 4)
    means = (own_means, ahead_means, behind_means, far_means)
    halo = (prior, prior_ahead, prior_far, prior_behind)
    halo, means = lax.optimization_barrier((halo, means))
    mine, other = halo, [to_chan(value, lambda s: s ^ 1) for value in halo]
    halves = (mine[0], other[0], mine[1], other[3], mine[2], other[2], other[1], mine[3])
    store, window_cov = late_terms(
        where, halves, late_total, sums, gram, stat, means, flags, store
    )
    back, store, window_cov = lax.optimization_barrier((back, store, window_cov))
    before = to_chan(back[16:24, 0:32], lambda s: s + 2)
    following = to_chan(back[24:32, 0:32], lambda s: (s - 2) ^ 1)
    opposite = to_chan(back[:, 32:40], lambda s: s + 4 if s < 4 else (s - 4) ^ 1)
    most = most_outputs(where, back, store)
    cusum, segment_cov = last_outputs(where, most, opposite, following, before)
    return window_cov, segment_cov, cusum


def solution(mesh):
    placed = (P("tm", "chan"), P("tm", None), P("tm"))
    return jax.shard_map(
        local,
        mesh=mesh,
        in_specs=placed,
        out_specs=(P("tm", "chan", None), P("tm", "chan", None), P("tm", None, "chan", None)),
        check_vma=False,
    )
```

```python
import jax
import jax.numpy as jnp
from jax import lax
from jax.experimental import pallas as pl
from jax.experimental.pallas import tpu as pltpu
from jax.sharding import PartitionSpec as P

F32, BF16 = jnp.float32, jnp.bfloat16
ROWS, HALO, WIDTH, BLOCKS, SPLITS, CHIPS = 2048, 1024, 128, 32, 8, 4
PAIR = 2 * WIDTH
HIGH = lax.Precision.HIGHEST
TRANSPOSED = (((0,), (0,)), ((), ()))
SM = pl.BlockSpec(memory_space=pltpu.SMEM)
HBM = pl.BlockSpec(memory_space=pltpu.HBM)
MIB = 2**20


def whole(*shape):
    return pl.BlockSpec(shape, lambda *_: (0,) * len(shape))


def array(*shape, dtype=F32):
    return jax.ShapeDtypeStruct(shape, dtype)


def params(grant):
    return pltpu.CompilerParams(
        vmem_limit_bytes=grant * MIB, dimension_semantics=("arbitrary",)
    )


def cost(microseconds):
    return pl.CostEstimate(
        flops=int(microseconds * 1e9), bytes_accessed=MIB, transcendentals=0
    )


def center_shard(raw_ref, out_ref, at):
    step = 256

    def add(i, total):
        piece = raw_ref[pl.ds(i * step, step), :].astype(F32)
        return total + jnp.sum(piece.reshape(step // 8, 8, WIDTH), axis=0)

    total = lax.fori_loop(0, ROWS // step, add, jnp.zeros((8, WIDTH), F32), unroll=2)
    mean = jnp.sum(total, axis=0, keepdims=True) / ROWS

    def shift(i, _):
        piece = raw_ref[pl.ds(i * step, step), :].astype(F32) - mean
        out_ref[pl.ds(i * step, step), pl.ds(at, WIDTH)] = piece.astype(BF16)
        return 0

    lax.fori_loop(0, ROWS // step, shift, 0, unroll=2)
    return mean


def center_pair(first_ref, second_ref, at, off, cent_ref, stat_ref):
    stat_ref[0] = jnp.zeros((8, PAIR), F32)
    stat_ref[0, 0:1, pl.ds(at, WIDTH)] = center_shard(first_ref, cent_ref, at)
    stat_ref[0, 0:1, pl.ds(off, WIDTH)] = center_shard(second_ref, cent_ref, off)
    total = jnp.dot(jnp.ones((16, ROWS), BF16), cent_ref[...], preferred_element_type=F32)[0:1]
    stat_ref[0, 1:2, :] = total
    stat_ref[0, 2:3, :] = stat_ref[0, 0:1, :] + total / ROWS


def turned_dot(left, right):
    return lax.dot_general(left, right, TRANSPOSED, preferred_element_type=F32)


def wide(value):
    return jnp.concatenate([value, value], axis=1)


def left_part(where_ref, flipped, cent_ref, left_ref, sums_ref, block=0):
    index = lax.broadcasted_iota(jnp.int32, (16, ROWS), 0)
    place = lax.broadcasted_iota(jnp.int32, (16, ROWS), 1)
    limit = jnp.zeros((16, ROWS), jnp.int32)
    for j in range(SPLITS):
        limit = jnp.where(index == j, where_ref[12 + j], limit)
    masks = jnp.where(place < limit, 1.0, 0.0).astype(BF16)
    cent = cent_ref[...]
    sums_ref[block] = jnp.dot(masks, cent, preferred_element_type=F32)[0:8]
    for i in range(SPLITS // 4):
        kept = jnp.concatenate([flipped * masks[j : j + 1, :] for j in range(4 * i, 4 * i + 4)], axis=0)
        part = jnp.dot(kept, cent, preferred_element_type=F32)
        for j in range(4):
            for c in range(2):
                rows, lanes = slice(j * WIDTH, (j + 1) * WIDTH), slice(c * WIDTH, (c + 1) * WIDTH)
                left_ref[c, 4 * i + j] = part[rows, lanes]


def first_kernel(
    where_ref, mine_ref, other_ref,
    left_ref, sums_ref, gram_ref, stat_ref, flip_hbm, total_hbm, flip_ref, spread_ref, total_ref, rider_ref, cent_ref,
):
    core = where_ref[2]
    at = pl.multiple_of(core * WIDTH, WIDTH)
    off = pl.multiple_of((1 - core) * WIDTH, WIDTH)
    center_pair(mine_ref, other_ref, at, off, cent_ref, stat_ref)
    rider_ref[...] = jnp.zeros((8, WIDTH), F32)
    rider_ref[0:1, :] = stat_ref[0, 2:3, 0:WIDTH]
    rider_ref[1:2, :] = stat_ref[0, 2:3, WIDTH:PAIR]
    rider_ref[2:3, :] = jnp.full((1, WIDTH), where_ref[20], jnp.int32).astype(F32)
    flip_ref[...] = cent_ref[:, pl.ds(at, WIDTH)].T
    flipped = flip_ref[...]
    flip_hbm[...] = flipped
    gram = jnp.dot(flipped, cent_ref[...], preferred_element_type=F32)
    gram_ref[0] = gram
    total = jnp.dot(flipped, jnp.ones((ROWS, WIDTH), BF16), preferred_element_type=F32)
    total_ref[...] = total
    total_hbm[...] = total
    spread_ref[...] = gram - wide(total) * (stat_ref[0, 1:2, :] / ROWS)
    left_part(where_ref, flipped, cent_ref, left_ref, sums_ref)


def near_kernel(
    where_ref, first_ref, second_ref, flip_ref, total_ref,
    left_ref, sums_ref, gram_ref, stat_ref, spread_ref, cent_ref,
):
    center_pair(first_ref, second_ref, 0, WIDTH, cent_ref, stat_ref)
    flipped = flip_ref[...]
    gram = jnp.dot(flipped, cent_ref[...], preferred_element_type=F32)
    gram_ref[0] = gram
    spread_ref[...] = gram - wide(total_ref[...]) * (stat_ref[0, 1:2, :] / ROWS)
    left_part(where_ref, flipped, cent_ref, left_ref, sums_ref)


def side_kernel(
    where_ref, first_ref, second_ref, flip_ref, left_ref, sums_ref, gram_ref, stat_ref, cent_ref
):
    center_pair(first_ref, second_ref, 0, WIDTH, cent_ref, stat_ref)
    flipped = flip_ref[...]
    gram_ref[0] = jnp.dot(flipped, cent_ref[...], preferred_element_type=F32)
    left_part(where_ref, flipped, cent_ref, left_ref, sums_ref)


def far_kernel(
    where_ref, first_ref, second_ref, flip_ref, total_ref, spread0_ref, spread1_ref, rider_ref,
    gram_ref, stat_ref, out_ref, held_ref, cent_ref,
):
    rider = rider_ref[0:4, :]
    for q in range(BLOCKS):
        spread, lane = ((spread0_ref, spread1_ref)[q // 16], WIDTH * (q // 8 % 2))
        row = 16 * (q % 8)
        out_ref[q, 0:16, :] = spread[row : row + 16, lane : lane + WIDTH]
        out_ref[q, 20:24, :] = rider
    center_pair(first_ref, second_ref, 0, WIDTH, cent_ref, stat_ref)
    gram = jnp.dot(flip_ref[...], cent_ref[...], preferred_element_type=F32)
    gram_ref[0] = gram
    spread = gram - wide(total_ref[...]) * (stat_ref[0, 1:2, :] / ROWS)
    held_ref[...] = jnp.where(where_ref[3] == 0, spread[:, 0:WIDTH], spread[:, WIDTH:PAIR])
    for q in range(BLOCKS):
        out_ref[q, 16:20, :] = held_ref[4 * q : 4 * q + 4, :]


def rest_kernel(where_ref, first_ref, second_ref, flip_ref, left_ref, sums_ref, cent_ref, stat_ref):
    center_pair(first_ref, second_ref, 0, WIDTH, cent_ref, stat_ref)
    left_part(where_ref, flip_ref[...], cent_ref, left_ref, sums_ref)


def token_kernel(pieces_ref, out_ref):
    out_ref[...] = jnp.zeros((8, WIDTH), F32)


def token(pieces):
    return pl.pallas_call(
        token_kernel,
        out_shape=array(8, WIDTH),
        grid=(1,),
        in_specs=[HBM],
        out_specs=whole(8, WIDTH),
        compiler_params=params(16),
        cost_estimate=cost(4),
        name="token",
    )(pieces)


ALL = [
    array(CHIPS, 8, PAIR),
    array(CHIPS, WIDTH, PAIR),
    array(CHIPS, 8, PAIR),
]


STORE = array(96, 8, WIDTH, WIDTH)
SHARD_PAIR = (2, SPLITS, WIDTH, WIDTH)


def call(
    kernel, name, inputs, outputs, *, store=None, puts=(), fetched=(), stored=(), kept=(),
    pair=0, span=1, scratch=(), us=3, grant=24,
):
    kept = (*([store] if store is not None else []), *kept)
    count, made, first = len(inputs), len(outputs), 1 if puts else 0
    sliced = [out in ALL for out in outputs]
    sizes = [(span, *out.shape[1:]) if cut else out.shape for out, cut in zip(outputs, sliced)]
    buffers = [pltpu.VMEM(inputs[i].shape, inputs[i].dtype) for i in fetched]
    buffers += [pltpu.VMEM(shape, F32) for shape, _ in puts]
    buffers += [pltpu.VMEM(sizes[i], outputs[i].dtype) for i in stored]

    def body(*refs):
        ins, refs = list(refs[:count]), refs[count + len(kept) :]
        slots, outs, refs = refs[:first], list(refs[first : first + made]), refs[first + made :]
        own, buffer, sem = refs[: len(scratch)], refs[len(scratch) : -1], refs[-1]
        copies = []
        for c, i in enumerate(fetched):
            copies.append(pltpu.make_async_copy(ins[i], buffer[c], sem.at[c]))
            ins[i] = buffer[c]
        for copy in copies:
            copy.start()
        for copy in copies:
            copy.wait()
        copies, mine = [], []
        for c, (_, place) in enumerate(puts, len(fetched)):
            copies.append(pltpu.make_async_copy(buffer[c], slots[0].at[place], sem.at[c]))
            mine.append(buffer[c])
        for c, i in enumerate(stored, len(fetched) + len(puts)):
            target = outs[i].at[pl.ds(pair, span)] if sliced[i] else outs[i]
            copies.append(pltpu.make_async_copy(buffer[c], target, sem.at[c]))
            outs[i] = buffer[c]
        kernel(*ins, *mine, *outs, *own)
        for copy in copies:
            copy.start()
        for copy in copies:
            copy.wait()

    ins = [SM if value.dtype == jnp.int32 else whole(*value.shape) for value in inputs]
    for i in fetched:
        ins[i] = HBM
    outs = [HBM if i in stored else whole(*out.shape) for i, out in enumerate(outputs)]
    aliased = range(first if store is None else 0, first + len(kept))
    return pl.pallas_call(
        body,
        out_shape=[STORE] * first + outputs,
        grid=(1,),
        in_specs=ins + [HBM] * len(kept),
        out_specs=[HBM] * first + outs,
        input_output_aliases={count + i: out for i, out in zip(range(len(kept)), aliased)},
        scratch_shapes=[pltpu.VMEM(shape, dtype) for shape, dtype in scratch]
        + buffers
        + [pltpu.SemaphoreType.DMA((max(len(buffers), 1),))],
        compiler_params=params(grant),
        cost_estimate=cost(us),
        name=name,
    )(*inputs, *kept)


def scan_kernel(arrived_ref, both_ref, means_ref, flags_ref):
    for b in range(BLOCKS):
        rider = arrived_ref[b, 16:24, :]
        means_ref[0, b : b + 1, :] = rider[4:5, :]
        means_ref[1, b : b + 1, :] = rider[5:6, :]
        flags_ref[b : b + 1, :] = rider[6:7, :]
    scan(arrived_ref, flags_ref, both_ref, 0, 16, 0)
    scan(arrived_ref, flags_ref, both_ref, 16, 4, 32)


def scan(arrived_ref, flags_ref, both_ref, row, size, at):
    zero = jnp.zeros((size, WIDTH), F32)
    running = zero
    for b in range(BLOCKS):
        begins = flags_ref[b : b + 1, :] > 0.5
        running = jnp.where(begins, zero, running)
        both_ref[b, at : at + size, :] = running
        running = running + arrived_ref[b, row : row + size, :]
    running = zero
    for b in reversed(range(BLOCKS)):
        begins = flags_ref[b : b + 1, :] > 0.5
        both_ref[b, at + size : at + 2 * size, :] = running
        running = jnp.where(begins, zero, running + arrived_ref[b, row : row + size, :])


def prep_kernel(
    where_ref, sums_ref, gram_ref, stat_ref, own_means_ref, ahead_ref, behind_ref, far_ref, flags_ref,
    turned_ref, cols_ref, coef_ref, before_ref, after_ref, vectors,
):
    here = where_ref[0]
    core = where_ref[2]
    away = 1 - core
    flags = flags_ref[...]
    spot = lax.broadcasted_iota(jnp.int32, (BLOCKS, WIDTH), 0)
    low = lax.broadcasted_iota(jnp.int32, (BLOCKS, BLOCKS), 1)
    high = lax.broadcasted_iota(jnp.int32, (BLOCKS, BLOCKS), 0)
    upto = jnp.dot((low <= high).astype(F32), flags, preferred_element_type=F32)
    mine = jnp.sum(jnp.where(spot <= here, flags, 0.0), axis=0, keepdims=True)
    same = jnp.abs(upto - mine) < 0.5
    masks = [
        jnp.where(same & (spot < here), 1.0, 0.0),
        jnp.where(same & (spot > here), 1.0, 0.0),
    ]
    totals = [jnp.sum(mask, axis=0, keepdims=True) for mask in masks]
    count_p, count_s = totals[0] * ROWS, totals[1] * ROWS

    def pooled(means, side):
        mask = masks[side]
        mean = jnp.sum(means * mask, axis=0, keepdims=True) / jnp.maximum(totals[side], 1.0)
        return mean, (means - mean) * mask

    def pick(value):
        return jnp.where(core == 0, value[:, 0:WIDTH], value[:, WIDTH:PAIR])

    row_means = own_means_ref[core]
    row_p, row_part_p = pooled(row_means, 0)
    row_s, row_part_s = pooled(row_means, 1)
    row_stat = pick(stat_ref[0])
    row_sums = pick(sums_ref[0])

    index = lax.broadcasted_iota(jnp.int32, (SPLITS, WIDTH), 0)
    k = jnp.zeros((SPLITS, WIDTH), jnp.int32)
    for j in range(SPLITS):
        k = jnp.where(index == j, where_ref[12 + j], k)
    k = k.astype(F32)
    rest = ROWS - k
    row_right = row_stat[1:2] - row_sums
    row_d = row_stat[0:1] + row_sums / k - row_p
    row_e = row_s - (row_stat[0:1] + row_right / rest)
    n_left, n_right = count_p + k, rest + count_s
    n = n_left + n_right
    weight = n_left * n_right / (n * n)
    a, b = weight / n_left, weight / n_right
    coef_ref[0:8, :] = a
    coef_ref[8:16, :] = b
    vectors[0:8, :] = -a * row_sums / k
    vectors[8:16, :] = a * (count_p * k / n_left) * row_d
    vectors[16:24, :] = b * row_right / rest
    vectors[24:32, :] = -b * (rest * count_s / n_right) * row_e
    total = count_p + ROWS
    n = total + count_s
    row_d = row_stat[2:3] - row_p
    row_e = row_s - (row_p + row_d * (ROWS / total))
    coef_ref[16:24, :] = jnp.broadcast_to(1.0 / n, (8, WIDTH))
    vectors[32:WIDTH, :] = jnp.zeros((WIDTH - 32, WIDTH), F32)
    vectors[32:33, :] = row_stat[1:2] / -ROWS / n
    vectors[33:34, :] = (count_p * ROWS / total) / n * row_d
    vectors[34:35, :] = (total * count_s / n) / n * row_e
    turned_ref[...] = vectors[...].T

    columns = (
        (own_means_ref[0], own_means_ref[1]),
        (ahead_ref[core], behind_ref[away]),
        (far_ref[core], far_ref[away]),
        (ahead_ref[away], behind_ref[core]),
    )
    for u in range(8):
        r, lanes = u // 2, slice(WIDTH * (u % 2), WIDTH * (u % 2) + WIDTH)
        means = columns[r][u % 2]
        col_p, col_part_p = pooled(means, 0)
        col_s, col_part_s = pooled(means, 1)
        stat = stat_ref[r, :, lanes]
        col_left = sums_ref[r, :, lanes]
        col_right = stat[1:2] - col_left
        cols_ref[u, 0:8, :] = col_left
        cols_ref[u, 8:16, :] = stat[0:1] + col_left / k - col_p
        cols_ref[u, 16:24, :] = col_right
        cols_ref[u, 24:32, :] = col_s - (stat[0:1] + col_right / rest)
        col_d = stat[2:3] - col_p
        cols_ref[u, 32:40, :] = jnp.zeros((8, WIDTH), F32)
        cols_ref[u, 32:33, :] = stat[1:2]
        cols_ref[u, 33:34, :] = col_d
        cols_ref[u, 34:35, :] = col_s - (col_p + col_d * (ROWS / total))

        def between(row_part, col_part):
            return ROWS * lax.dot_general(
                row_part, col_part, TRANSPOSED, precision=HIGH, preferred_element_type=F32
            )

        before_ref[u] = between(row_part_p, col_part_p)
        after_ref[u] = gram_ref[r, :, lanes] + between(row_part_s, col_part_s)


def load_near(ref, p_ref, s_ref):
    for g in range(8):
        p_ref[16 * g : 16 * g + 16, :] = ref[g, 0:16, :]
        s_ref[16 * g : 16 * g + 16, :] = ref[g, 16:32, :]


def load_far(ref, p_ref, s_ref):
    for q in range(BLOCKS):
        p_ref[4 * q : 4 * q + 4, :] = ref[q, 0:4, :]
        s_ref[4 * q : 4 * q + 4, :] = ref[q, 4:8, :]


def shard_lanes(where_ref, u):
    return pl.ds(pl.multiple_of(where_ref[4 + u] * WIDTH, WIDTH), WIDTH)


def most_kernel(
    where_ref, back_ref, store_hbm, most_ref, seg_ref, coef_ref,
    left_ref, prefix_ref, suffix_ref, cols_ref, turned_ref, p_ref, s_ref, sem,
):
    loads = [
        pltpu.make_async_copy(source, target, sem.at[c])
        for c, (source, target) in enumerate(
            (
                (store_hbm.at[8], prefix_ref),
                (store_hbm.at[9], suffix_ref),
                (store_hbm.at[10, :, pl.ds(0, 40)], cols_ref),
                (store_hbm.at[11, 0], turned_ref),
                (store_hbm.at[11, 1, pl.ds(0, 24)], coef_ref),
                *(
                    (store_hbm.at[pl.ds(0, 8), j], left_ref.at[:, j])
                    for j in range(SPLITS)
                ),
            )
        )
    ]
    for load in loads:
        load.start()
    held = where_ref[3]
    for load in loads[:5]:
        load.wait()

    def add(u):
        prefix_ref[u] = prefix_ref[u] + p_ref[...]
        suffix_ref[u] = suffix_ref[u] + s_ref[...]

    for u in range(4):
        load_near(back_ref.at[pl.ds(8 * u, 8)], p_ref, s_ref)
        add(u)
    load_far(back_ref.at[:, pl.ds(32, 8)], p_ref, s_ref)
    add(4 + held)

    def spread_out(rows):
        return [jnp.broadcast_to(turned_ref[:, i : i + 1], (WIDTH, WIDTH)) for i in rows]

    turned = spread_out(range(32, 35))
    for u in range(8):
        value = (prefix_ref[u] + suffix_ref[u]) * coef_ref[16:17, :]
        for i in range(3):
            value = value + turned[i] * cols_ref[u, 32 + i : 33 + i, :]
        seg_ref[:, shard_lanes(where_ref, u)] = value
    for j in range(SPLITS):
        loads[5 + j].wait()
        turned = spread_out(range(j, 32, 8))
        a, b = coef_ref[j : j + 1, :], coef_ref[8 + j : 9 + j, :]
        for u in range(8):
            value = (a + b) * left_ref[u, j] + a * prefix_ref[u] - b * suffix_ref[u]
            for i in range(4):
                value = value + turned[i] * cols_ref[u, 8 * i + j : 8 * i + j + 1, :]
            most_ref[j, :, shard_lanes(where_ref, u)] = value


def last_kernel(
    where_ref, most_ref, most_seg_ref, coef_ref, opposite_ref, next_ref, before_ref, cusum_hbm, seg_hbm,
    cusum_ref, seg_ref, prefix_ref, suffix_ref, p_ref, s_ref, sem,
):
    shards = (5 - where_ref[3], 6, 7)
    for v, (ref, load) in enumerate(
        ((opposite_ref, load_far), (next_ref, load_near), (before_ref, load_near))
    ):
        load(ref, p_ref, s_ref)
        prefix_ref[v] = p_ref[...].T
        suffix_ref[v] = s_ref[...].T
    seg_ref[0] = most_seg_ref[...]
    for v, u in enumerate(shards):
        lanes = shard_lanes(where_ref, u)
        added = (prefix_ref[v] + suffix_ref[v]) * coef_ref[16:17, :]
        seg_ref[0, :, lanes] = most_seg_ref[:, lanes] + added
    stores = [pltpu.make_async_copy(seg_ref, seg_hbm, sem.at[SPLITS])]
    stores[0].start()
    for j in range(SPLITS):
        a, b = coef_ref[j : j + 1, :], coef_ref[8 + j : 9 + j, :]
        cusum_ref[0, j] = most_ref[j]
        for v, u in enumerate(shards):
            lanes = shard_lanes(where_ref, u)
            cusum_ref[0, j, :, lanes] = most_ref[j, :, lanes] + a * prefix_ref[v] - b * suffix_ref[v]
        store = pltpu.make_async_copy(
            cusum_ref.at[:, pl.ds(j, 1)], cusum_hbm.at[:, pl.ds(j, 1)], sem.at[j]
        )
        store.start()
        stores.append(store)
    for store in stores:
        store.wait()


OUTPUTS = [array(1, SPLITS, WIDTH, CHIPS * PAIR), array(1, WIDTH, CHIPS * PAIR)]
MOST = [array(SPLITS, WIDTH, CHIPS * PAIR), array(WIDTH, CHIPS * PAIR), array(24, WIDTH)]


def most_outputs(where, back, store):
    square = array(8, WIDTH, WIDTH)
    buffers = [array(8, SPLITS, WIDTH, WIDTH), square, square, array(8, 40, WIDTH)]
    buffers += [array(WIDTH, WIDTH)] * 3
    return pl.pallas_call(
        most_kernel,
        out_shape=MOST,
        grid=(1,),
        in_specs=[SM, whole(*back.shape), HBM],
        out_specs=[whole(*value.shape) for value in MOST],
        scratch_shapes=[pltpu.VMEM(value.shape, F32) for value in buffers]
        + [pltpu.SemaphoreType.DMA((5 + SPLITS,))],
        compiler_params=params(24),
        cost_estimate=cost(5),
        name="most_outputs",
    )(where, back, store)


def last_outputs(where, most, opposite, following, before):
    inputs = [*most, opposite, following, before]
    buffers = [*OUTPUTS, array(3, WIDTH, WIDTH), array(3, WIDTH, WIDTH)]
    buffers += [array(WIDTH, WIDTH)] * 2
    return pl.pallas_call(
        last_kernel,
        out_shape=OUTPUTS,
        grid=(1,),
        in_specs=[SM] + [whole(*value.shape) for value in inputs],
        out_specs=[HBM, HBM],
        scratch_shapes=[pltpu.VMEM(value.shape, F32) for value in buffers]
        + [pltpu.SemaphoreType.DMA((SPLITS + 1,))],
        compiler_params=params(24),
        cost_estimate=cost(3),
        name="last_outputs",
    )(where, *inputs)


def window_kernel(
    where_ref, halves, gram_ref, stat_ref, total_ref, out_ref, cent_ref, flip_ref, sum_ref,
):
    live = jnp.where(where_ref[0] > 0, 1.0, 0.0).astype(F32)
    core = where_ref[2]
    at = pl.multiple_of(core * WIDTH, WIDTH)
    off = pl.multiple_of((1 - core) * WIDTH, WIDTH)
    count = ROWS + live * HALO
    scale = wide(1.0 / jnp.full((1, WIDTH), count, F32))
    unbias = wide(1.0 / jnp.full((1, WIDTH), count - 1.0, F32))
    step = 256
    for r in range(CHIPS):
        lanes = (at, off) if r == 0 else (0, WIDTH)
        for raw, lane in zip(halves[2 * r : 2 * r + 2], lanes):
            mean = stat_ref[r, 0:1, pl.ds(lane, WIDTH)]

            def shift(i, _, raw=raw, lane=lane, mean=mean):
                piece = (raw[pl.ds(i * step, step), :].astype(F32) - mean) * live
                cent_ref[pl.ds(i * step, step), pl.ds(lane, WIDTH)] = piece.astype(BF16)
                return 0

            lax.fori_loop(0, HALO // step, shift, 0, unroll=2)
        if r == 0:
            flip_ref[...] = cent_ref[:, pl.ds(at, WIDTH)].T
            flipped = flip_ref[...]
            row_sum = jnp.dot(flipped, jnp.ones((HALO, WIDTH), BF16), preferred_element_type=F32)
            sum_ref[...] = row_sum + total_ref[...]
        cent = cent_ref[...]
        halo = jnp.dot(flip_ref[...], cent, preferred_element_type=F32)
        col_sum = jnp.dot(jnp.ones((16, HALO), BF16), cent, preferred_element_type=F32)[0:1]
        col_sum = col_sum + stat_ref[r, 1:2, :]
        value = (halo + gram_ref[r] - wide(sum_ref[...]) * (col_sum * scale)) * unbias
        for c in range(2):
            lane = pl.multiple_of(where_ref[4 + 2 * r + c] * WIDTH, WIDTH)
            out_ref[0, :, pl.ds(lane, WIDTH)] = value[:, c * WIDTH : (c + 1) * WIDTH]


def late_kernel(
    where_ref, h0, h1, h2, h3, h4, h5, h6, h7, total_ref, sums_ref, gram_ref, stat_ref,
    own_ref, ahead_ref, behind_ref, far_ref, flags_ref,
    turned_ref, cols_ref, coef_ref, before_ref, after_ref, window_ref, vectors, cent_ref, flip_ref, sum_ref,
):
    prep_kernel(
        where_ref, sums_ref, gram_ref, stat_ref, own_ref, ahead_ref, behind_ref, far_ref, flags_ref,
        turned_ref, cols_ref, coef_ref, before_ref, after_ref, vectors,
    )
    window_kernel(
        where_ref, (h0, h1, h2, h3, h4, h5, h6, h7), gram_ref, stat_ref, total_ref,
        window_ref, cent_ref, flip_ref, sum_ref,
    )


def late_terms(where, halves, total, sums, gram, stat, means, flags, store):
    square = (8, WIDTH, WIDTH)
    return call(
        late_kernel,
        "late_terms",
        [where, *halves, total, sums, gram, stat, *means, flags],
        [array(1, WIDTH, CHIPS * PAIR)],
        store=store,
        puts=(
            ((WIDTH, WIDTH), (11, 0)),
            ((8, 40, WIDTH), (10, slice(None), pl.ds(0, 40))),
            ((24, WIDTH), (11, 1, pl.ds(0, 24))),
            (square, 8),
            (square, 9),
        ),
        fetched=(9, 10, 11, 12, 13, 17),
        stored=(0,),
        scratch=[
            ((WIDTH, WIDTH), F32),
            ((HALO, PAIR), BF16),
            ((WIDTH, HALO), BF16),
            ((WIDTH, WIDTH), F32),
        ],
        us=0.1,
    )


def to_chan(value, target):
    count = lax.axis_size("chan")
    return lax.ppermute(value, "chan", [(s, target(s) % count) for s in range(count)])


def exchange(value):
    return lax.all_to_all(value, "tm", 0, 0, tiled=True)


def after(value, *others):
    return lax.optimization_barrier((value, *others))[0]


def local(samples, candidates, segment_start):
    here, index = lax.axis_index("tm"), lax.axis_index("chan")
    chip, core = index // 2, index % 2
    nearby = [2 * chip, 2 * chip + 1]
    for step, side in ((1, core), (3, 1 - core), (2, core), (2, 1 - core), (1, 1 - core), (3, core)):
        nearby.append(2 * ((chip + step) % CHIPS) + side)
    held = jnp.where(chip < CHIPS // 2, 0, 1)
    where = jnp.stack([here, chip, core, held] + nearby).astype(jnp.int32)
    where = jnp.concatenate([where, candidates[0], segment_start])

    behind = to_chan(samples, lambda s: s + 2)
    ahead = to_chan(samples, lambda s: s - 2)
    other = to_chan(samples, lambda s: s ^ 1)
    prior = lax.ppermute(samples[ROWS - HALO :], "tm", [(b, b + 1) for b in range(BLOCKS - 1)])
    flip_shape, square = array(WIDTH, ROWS, dtype=BF16), array(WIDTH, WIDTH)
    store, sums, gram, stat, late_flipped, late_total, flipped, spread0, total, rider = call(
        first_kernel,
        "first_pair",
        [where, samples, other],
        ALL + [flip_shape, square, flip_shape, array(WIDTH, PAIR), square, array(8, WIDTH)],
        puts=((SHARD_PAIR, pl.ds(0, 2)),),
        fetched=(1,),
        stored=(0, 1, 2, 3, 4),
        scratch=[((ROWS, PAIR), BF16)],
    )
    behind, ahead, prior, flipped = lax.optimization_barrier((behind, ahead, prior, flipped))
    half = ROWS // 2
    far_low = to_chan(behind[:half], lambda s: s + 2)
    far_high = to_chan(ahead[half:], lambda s: s - 2)
    behind_other = to_chan(behind, lambda s: s ^ 1)
    ahead_other = to_chan(ahead, lambda s: s ^ 1)
    store, sums, gram, stat, spread1 = call(
        near_kernel,
        "near_pair",
        [where, ahead, behind_other, flipped, total],
        ALL + [array(WIDTH, PAIR)],
        store=store,
        puts=((SHARD_PAIR, pl.ds(2, 2)),),
        stored=(0, 1, 2),
        kept=(sums, gram, stat),
        pair=1,
        scratch=[((ROWS, PAIR), BF16)],
    )
    store, sums, gram, stat = call(
        side_kernel,
        "side_pair",
        [where, ahead_other, behind, flipped],
        ALL,
        store=store,
        puts=((SHARD_PAIR, pl.ds(6, 2)),),
        stored=(0, 1, 2),
        kept=(sums, gram, stat),
        pair=3,
        scratch=[((ROWS, PAIR), BF16)],
        us=2,
    )
    far_low, far_high, stat = lax.optimization_barrier((far_low, far_high, stat))
    far = jnp.concatenate([far_low, far_high], axis=0)
    far_other = to_chan(far, lambda s: s ^ 1)
    gram, stat, pieces = call(
        far_kernel,
        "far_pair",
        [where, far, far_other, flipped, total, spread0, spread1, rider],
        ALL[1:] + [array(BLOCKS, 24, WIDTH)],
        stored=(0, 1),
        kept=(gram, stat),
        pair=2,
        scratch=[((WIDTH, WIDTH), F32), ((ROWS, PAIR), BF16)],
        us=0.1,
    )
    arrived = exchange(pieces)

    store, sums = call(
        rest_kernel,
        "rest_left",
        [where, after(far, pieces), far_other, late_flipped],
        ALL[:1],
        store=store,
        puts=((SHARD_PAIR, pl.ds(4, 2)),),
        fetched=(3,),
        stored=(0,),
        kept=(sums,),
        pair=2,
        scratch=[((ROWS, PAIR), BF16), ((1, 8, PAIR), F32)],
        us=4,
    )
    prior = after(prior, token(pieces))
    prior_ahead = to_chan(prior, lambda s: s - 2)
    prior_behind = to_chan(prior, lambda s: s + 2)
    prior_far = to_chan(prior, lambda s: s + 4)
    arrived, prior_ahead, sums = lax.optimization_barrier((arrived, prior_ahead, sums))
    scanned, own_means, flags = call(
        scan_kernel,
        "scan_pieces",
        [arrived],
        [array(BLOCKS, 40, WIDTH), array(2, BLOCKS, WIDTH), array(BLOCKS, WIDTH)],
        stored=(0, 1, 2),
        us=1,
    )
    back = exchange(scanned)
    ahead_means = to_chan(own_means, lambda s: s - 2)
    behind_means = to_chan(own_means, lambda s: s + 2)
    far_means = to_chan(own_means, lambda s: s + 4)
    means = (own_means, ahead_means, behind_means, far_means)
    halo = (prior, prior_ahead, prior_far, prior_behind)
    halo, means = lax.optimization_barrier((halo, means))
    mine, other = halo, [to_chan(value, lambda s: s ^ 1) for value in halo]
    halves = (mine[0], other[0], mine[1], other[3], mine[2], other[2], other[1], mine[3])
    store, window_cov = late_terms(
        where, halves, late_total, sums, gram, stat, means, flags, store
    )
    back, store, window_cov = lax.optimization_barrier((back, store, window_cov))
    before = to_chan(back[16:24, 0:32], lambda s: s + 2)
    following = to_chan(back[24:32, 0:32], lambda s: (s - 2) ^ 1)
    opposite = to_chan(back[:, 32:40], lambda s: s + 4 if s < 4 else (s - 4) ^ 1)
    most = most_outputs(where, back, store)
    cusum, segment_cov = last_outputs(where, most, opposite, following, before)
    return window_cov, segment_cov, cusum


def solution(mesh):
    placed = (P("tm", "chan"), P("tm", None), P("tm"))
    return jax.shard_map(
        local,
        mesh=mesh,
        in_specs=placed,
        out_specs=(P("tm", "chan", None), P("tm", "chan", None), P("tm", None, "chan", None)),
        check_vma=False,
    )
```

```python
import jax
import jax.numpy as jnp
from jax import lax
from jax.experimental import pallas as pl
from jax.experimental.pallas import tpu as pltpu
from jax.sharding import PartitionSpec as P

F32, BF16 = jnp.float32, jnp.bfloat16
ROWS, HALO, WIDTH, BLOCKS, SPLITS, CHIPS = 2048, 1024, 128, 32, 8, 4
PAIR = 2 * WIDTH
HIGH = lax.Precision.HIGHEST
TRANSPOSED = (((0,), (0,)), ((), ()))
SM = pl.BlockSpec(memory_space=pltpu.SMEM)
HBM = pl.BlockSpec(memory_space=pltpu.HBM)
MIB = 2**20


def whole(*shape):
    return pl.BlockSpec(shape, lambda *_: (0,) * len(shape))


def array(*shape, dtype=F32):
    return jax.ShapeDtypeStruct(shape, dtype)


def params(grant):
    return pltpu.CompilerParams(
        vmem_limit_bytes=grant * MIB, dimension_semantics=("arbitrary",)
    )


def cost(microseconds):
    return pl.CostEstimate(
        flops=int(microseconds * 1e9), bytes_accessed=MIB, transcendentals=0
    )


def center_shard(raw_ref, out_ref, at):
    step = 256

    def add(i, total):
        piece = raw_ref[pl.ds(i * step, step), :].astype(F32)
        return total + jnp.sum(piece.reshape(step // 8, 8, WIDTH), axis=0)

    total = lax.fori_loop(0, ROWS // step, add, jnp.zeros((8, WIDTH), F32), unroll=2)
    mean = jnp.sum(total, axis=0, keepdims=True) / ROWS

    def shift(i, _):
        piece = raw_ref[pl.ds(i * step, step), :].astype(F32) - mean
        out_ref[pl.ds(i * step, step), pl.ds(at, WIDTH)] = piece.astype(BF16)
        return 0

    lax.fori_loop(0, ROWS // step, shift, 0, unroll=2)
    return mean


def center_pair(first_ref, second_ref, at, off, cent_ref, stat_ref):
    stat_ref[0] = jnp.zeros((8, PAIR), F32)
    stat_ref[0, 0:1, pl.ds(at, WIDTH)] = center_shard(first_ref, cent_ref, at)
    stat_ref[0, 0:1, pl.ds(off, WIDTH)] = center_shard(second_ref, cent_ref, off)
    total = jnp.dot(jnp.ones((16, ROWS), BF16), cent_ref[...], preferred_element_type=F32)[0:1]
    stat_ref[0, 1:2, :] = total
    stat_ref[0, 2:3, :] = stat_ref[0, 0:1, :] + total / ROWS


def turned_dot(left, right):
    return lax.dot_general(left, right, TRANSPOSED, preferred_element_type=F32)


def wide(value):
    return jnp.concatenate([value, value], axis=1)


def left_part(where_ref, flipped, cent_ref, left_ref, sums_ref, block=0):
    index = lax.broadcasted_iota(jnp.int32, (16, ROWS), 0)
    place = lax.broadcasted_iota(jnp.int32, (16, ROWS), 1)
    limit = jnp.zeros((16, ROWS), jnp.int32)
    for j in range(SPLITS):
        limit = jnp.where(index == j, where_ref[12 + j], limit)
    masks = jnp.where(place < limit, 1.0, 0.0).astype(BF16)
    cent = cent_ref[...]
    sums_ref[block] = jnp.dot(masks, cent, preferred_element_type=F32)[0:8]
    for i in range(SPLITS // 4):
        kept = jnp.concatenate([flipped * masks[j : j + 1, :] for j in range(4 * i, 4 * i + 4)], axis=0)
        part = jnp.dot(kept, cent, preferred_element_type=F32)
        for j in range(4):
            for c in range(2):
                rows, lanes = slice(j * WIDTH, (j + 1) * WIDTH), slice(c * WIDTH, (c + 1) * WIDTH)
                left_ref[c, 4 * i + j] = part[rows, lanes]


def first_kernel(
    where_ref, mine_ref, other_ref,
    left_ref, sums_ref, gram_ref, stat_ref, flip_hbm, total_hbm, flip_ref, spread_ref, total_ref, rider_ref, cent_ref,
):
    core = where_ref[2]
    at = pl.multiple_of(core * WIDTH, WIDTH)
    off = pl.multiple_of((1 - core) * WIDTH, WIDTH)
    center_pair(mine_ref, other_ref, at, off, cent_ref, stat_ref)
    rider_ref[...] = jnp.zeros((8, WIDTH), F32)
    rider_ref[0:1, :] = stat_ref[0, 2:3, 0:WIDTH]
    rider_ref[1:2, :] = stat_ref[0, 2:3, WIDTH:PAIR]
    rider_ref[2:3, :] = jnp.full((1, WIDTH), where_ref[20], jnp.int32).astype(F32)
    flip_ref[...] = cent_ref[:, pl.ds(at, WIDTH)].T
    flipped = flip_ref[...]
    flip_hbm[...] = flipped
    gram = jnp.dot(flipped, cent_ref[...], preferred_element_type=F32)
    gram_ref[0] = gram
    total = jnp.dot(flipped, jnp.ones((ROWS, WIDTH), BF16), preferred_element_type=F32)
    total_ref[...] = total
    total_hbm[...] = total
    spread_ref[...] = gram - wide(total) * (stat_ref[0, 1:2, :] / ROWS)
    left_part(where_ref, flipped, cent_ref, left_ref, sums_ref)


def near_kernel(
    where_ref, first_ref, second_ref, flip_ref, total_ref,
    left_ref, sums_ref, gram_ref, stat_ref, spread_ref, cent_ref,
):
    center_pair(first_ref, second_ref, 0, WIDTH, cent_ref, stat_ref)
    flipped = flip_ref[...]
    gram = jnp.dot(flipped, cent_ref[...], preferred_element_type=F32)
    gram_ref[0] = gram
    spread_ref[...] = gram - wide(total_ref[...]) * (stat_ref[0, 1:2, :] / ROWS)
    left_part(where_ref, flipped, cent_ref, left_ref, sums_ref)


def side_kernel(
    where_ref, first_ref, second_ref, flip_ref, left_ref, sums_ref, gram_ref, stat_ref, cent_ref
):
    center_pair(first_ref, second_ref, 0, WIDTH, cent_ref, stat_ref)
    flipped = flip_ref[...]
    gram_ref[0] = jnp.dot(flipped, cent_ref[...], preferred_element_type=F32)
    left_part(where_ref, flipped, cent_ref, left_ref, sums_ref)


def far_kernel(
    where_ref, first_ref, second_ref, flip_ref, total_ref, spread0_ref, spread1_ref, rider_ref,
    gram_ref, stat_ref, out_ref, held_ref, cent_ref,
):
    rider = rider_ref[0:4, :]
    for q in range(BLOCKS):
        spread, lane = ((spread0_ref, spread1_ref)[q // 16], WIDTH * (q // 8 % 2))
        row = 16 * (q % 8)
        out_ref[q, 0:16, :] = spread[row : row + 16, lane : lane + WIDTH]
        out_ref[q, 20:24, :] = rider
    center_pair(first_ref, second_ref, 0, WIDTH, cent_ref, stat_ref)
    gram = jnp.dot(flip_ref[...], cent_ref[...], preferred_element_type=F32)
    gram_ref[0] = gram
    spread = gram - wide(total_ref[...]) * (stat_ref[0, 1:2, :] / ROWS)
    held_ref[...] = jnp.where(where_ref[3] == 0, spread[:, 0:WIDTH], spread[:, WIDTH:PAIR])
    for q in range(BLOCKS):
        out_ref[q, 16:20, :] = held_ref[4 * q : 4 * q + 4, :]


def rest_kernel(where_ref, first_ref, second_ref, flip_ref, left_ref, sums_ref, cent_ref, stat_ref):
    center_pair(first_ref, second_ref, 0, WIDTH, cent_ref, stat_ref)
    left_part(where_ref, flip_ref[...], cent_ref, left_ref, sums_ref)


def token_kernel(pieces_ref, out_ref):
    out_ref[...] = jnp.zeros((8, WIDTH), F32)


def token(pieces):
    return pl.pallas_call(
        token_kernel,
        out_shape=array(8, WIDTH),
        grid=(1,),
        in_specs=[HBM],
        out_specs=whole(8, WIDTH),
        compiler_params=params(16),
        cost_estimate=cost(4),
        name="token",
    )(pieces)


ALL = [
    array(CHIPS, 8, PAIR),
    array(CHIPS, WIDTH, PAIR),
    array(CHIPS, 8, PAIR),
]


STORE = array(96, 8, WIDTH, WIDTH)
SHARD_PAIR = (2, SPLITS, WIDTH, WIDTH)


def call(
    kernel, name, inputs, outputs, *, store=None, puts=(), fetched=(), stored=(), kept=(),
    pair=0, span=1, scratch=(), us=3, grant=24,
):
    kept = (*([store] if store is not None else []), *kept)
    count, made, first = len(inputs), len(outputs), 1 if puts else 0
    sliced = [out in ALL for out in outputs]
    sizes = [(span, *out.shape[1:]) if cut else out.shape for out, cut in zip(outputs, sliced)]
    buffers = [pltpu.VMEM(inputs[i].shape, inputs[i].dtype) for i in fetched]
    buffers += [pltpu.VMEM(shape, F32) for shape, _ in puts]
    buffers += [pltpu.VMEM(sizes[i], outputs[i].dtype) for i in stored]

    def body(*refs):
        ins, refs = list(refs[:count]), refs[count + len(kept) :]
        slots, outs, refs = refs[:first], list(refs[first : first + made]), refs[first + made :]
        own, buffer, sem = refs[: len(scratch)], refs[len(scratch) : -1], refs[-1]
        copies = []
        for c, i in enumerate(fetched):
            copies.append(pltpu.make_async_copy(ins[i], buffer[c], sem.at[c]))
            ins[i] = buffer[c]
        for copy in copies:
            copy.start()
        for copy in copies:
            copy.wait()
        copies, mine = [], []
        for c, (_, place) in enumerate(puts, len(fetched)):
            copies.append(pltpu.make_async_copy(buffer[c], slots[0].at[place], sem.at[c]))
            mine.append(buffer[c])
        for c, i in enumerate(stored, len(fetched) + len(puts)):
            target = outs[i].at[pl.ds(pair, span)] if sliced[i] else outs[i]
            copies.append(pltpu.make_async_copy(buffer[c], target, sem.at[c]))
            outs[i] = buffer[c]
        kernel(*ins, *mine, *outs, *own)
        for copy in copies:
            copy.start()
        for copy in copies:
            copy.wait()

    ins = [SM if value.dtype == jnp.int32 else whole(*value.shape) for value in inputs]
    for i in fetched:
        ins[i] = HBM
    outs = [HBM if i in stored else whole(*out.shape) for i, out in enumerate(outputs)]
    aliased = range(first if store is None else 0, first + len(kept))
    return pl.pallas_call(
        body,
        out_shape=[STORE] * first + outputs,
        grid=(1,),
        in_specs=ins + [HBM] * len(kept),
        out_specs=[HBM] * first + outs,
        input_output_aliases={count + i: out for i, out in zip(range(len(kept)), aliased)},
        scratch_shapes=[pltpu.VMEM(shape, dtype) for shape, dtype in scratch]
        + buffers
        + [pltpu.SemaphoreType.DMA((max(len(buffers), 1),))],
        compiler_params=params(grant),
        cost_estimate=cost(us),
        name=name,
    )(*inputs, *kept)


def scan_kernel(arrived_ref, both_ref, means_ref, flags_ref):
    for b in range(BLOCKS):
        rider = arrived_ref[b, 16:24, :]
        means_ref[0, b : b + 1, :] = rider[4:5, :]
        means_ref[1, b : b + 1, :] = rider[5:6, :]
        flags_ref[b : b + 1, :] = rider[6:7, :]
    scan(arrived_ref, flags_ref, both_ref, 0, 16, 0)
    scan(arrived_ref, flags_ref, both_ref, 16, 4, 32)


def scan(arrived_ref, flags_ref, both_ref, row, size, at):
    zero = jnp.zeros((size, WIDTH), F32)
    running = zero
    for b in range(BLOCKS):
        begins = flags_ref[b : b + 1, :] > 0.5
        running = jnp.where(begins, zero, running)
        both_ref[b, at : at + size, :] = running
        running = running + arrived_ref[b, row : row + size, :]
    running = zero
    for b in reversed(range(BLOCKS)):
        begins = flags_ref[b : b + 1, :] > 0.5
        both_ref[b, at + size : at + 2 * size, :] = running
        running = jnp.where(begins, zero, running + arrived_ref[b, row : row + size, :])


def prep_kernel(
    where_ref, sums_ref, gram_ref, stat_ref, own_means_ref, ahead_ref, behind_ref, far_ref, flags_ref,
    turned_ref, cols_ref, coef_ref, before_ref, after_ref, vectors,
):
    here = where_ref[0]
    core = where_ref[2]
    away = 1 - core
    flags = flags_ref[...]
    spot = lax.broadcasted_iota(jnp.int32, (BLOCKS, WIDTH), 0)
    low = lax.broadcasted_iota(jnp.int32, (BLOCKS, BLOCKS), 1)
    high = lax.broadcasted_iota(jnp.int32, (BLOCKS, BLOCKS), 0)
    upto = jnp.dot((low <= high).astype(F32), flags, preferred_element_type=F32)
    mine = jnp.sum(jnp.where(spot <= here, flags, 0.0), axis=0, keepdims=True)
    same = jnp.abs(upto - mine) < 0.5
    masks = [
        jnp.where(same & (spot < here), 1.0, 0.0),
        jnp.where(same & (spot > here), 1.0, 0.0),
    ]
    totals = [jnp.sum(mask, axis=0, keepdims=True) for mask in masks]
    count_p, count_s = totals[0] * ROWS, totals[1] * ROWS

    def pooled(means, side):
        mask = masks[side]
        mean = jnp.sum(means * mask, axis=0, keepdims=True) / jnp.maximum(totals[side], 1.0)
        return mean, (means - mean) * mask

    def pick(value):
        return jnp.where(core == 0, value[:, 0:WIDTH], value[:, WIDTH:PAIR])

    row_means = own_means_ref[core]
    row_p, row_part_p = pooled(row_means, 0)
    row_s, row_part_s = pooled(row_means, 1)
    row_stat = pick(stat_ref[0])
    row_sums = pick(sums_ref[0])

    index = lax.broadcasted_iota(jnp.int32, (SPLITS, WIDTH), 0)
    k = jnp.zeros((SPLITS, WIDTH), jnp.int32)
    for j in range(SPLITS):
        k = jnp.where(index == j, where_ref[12 + j], k)
    k = k.astype(F32)
    rest = ROWS - k
    row_right = row_stat[1:2] - row_sums
    row_d = row_stat[0:1] + row_sums / k - row_p
    row_e = row_s - (row_stat[0:1] + row_right / rest)
    n_left, n_right = count_p + k, rest + count_s
    n = n_left + n_right
    weight = n_left * n_right / (n * n)
    a, b = weight / n_left, weight / n_right
    coef_ref[0:8, :] = a
    coef_ref[8:16, :] = b
    vectors[0:8, :] = -a * row_sums / k
    vectors[8:16, :] = a * (count_p * k / n_left) * row_d
    vectors[16:24, :] = b * row_right / rest
    vectors[24:32, :] = -b * (rest * count_s / n_right) * row_e
    total = count_p + ROWS
    n = total + count_s
    row_d = row_stat[2:3] - row_p
    row_e = row_s - (row_p + row_d * (ROWS / total))
    coef_ref[16:24, :] = jnp.broadcast_to(1.0 / n, (8, WIDTH))
    vectors[32:WIDTH, :] = jnp.zeros((WIDTH - 32, WIDTH), F32)
    vectors[32:33, :] = row_stat[1:2] / -ROWS / n
    vectors[33:34, :] = (count_p * ROWS / total) / n * row_d
    vectors[34:35, :] = (total * count_s / n) / n * row_e
    turned_ref[...] = vectors[...].T

    columns = (
        (own_means_ref[0], own_means_ref[1]),
        (ahead_ref[core], behind_ref[away]),
        (far_ref[core], far_ref[away]),
        (ahead_ref[away], behind_ref[core]),
    )
    for u in range(8):
        r, lanes = u // 2, slice(WIDTH * (u % 2), WIDTH * (u % 2) + WIDTH)
        means = columns[r][u % 2]
        col_p, col_part_p = pooled(means, 0)
        col_s, col_part_s = pooled(means, 1)
        stat = stat_ref[r, :, lanes]
        col_left = sums_ref[r, :, lanes]
        col_right = stat[1:2] - col_left
        cols_ref[u, 0:8, :] = col_left
        cols_ref[u, 8:16, :] = stat[0:1] + col_left / k - col_p
        cols_ref[u, 16:24, :] = col_right
        cols_ref[u, 24:32, :] = col_s - (stat[0:1] + col_right / rest)
        col_d = stat[2:3] - col_p
        cols_ref[u, 32:40, :] = jnp.zeros((8, WIDTH), F32)
        cols_ref[u, 32:33, :] = stat[1:2]
        cols_ref[u, 33:34, :] = col_d
        cols_ref[u, 34:35, :] = col_s - (col_p + col_d * (ROWS / total))

        def between(row_part, col_part):
            return ROWS * lax.dot_general(
                row_part, col_part, TRANSPOSED, precision=HIGH, preferred_element_type=F32
            )

        before_ref[u] = between(row_part_p, col_part_p)
        after_ref[u] = gram_ref[r, :, lanes] + between(row_part_s, col_part_s)


def load_near(ref, p_ref, s_ref):
    for g in range(8):
        p_ref[16 * g : 16 * g + 16, :] = ref[g, 0:16, :]
        s_ref[16 * g : 16 * g + 16, :] = ref[g, 16:32, :]


def load_far(ref, p_ref, s_ref):
    for q in range(BLOCKS):
        p_ref[4 * q : 4 * q + 4, :] = ref[q, 0:4, :]
        s_ref[4 * q : 4 * q + 4, :] = ref[q, 4:8, :]


def shard_lanes(where_ref, u):
    return pl.ds(pl.multiple_of(where_ref[4 + u] * WIDTH, WIDTH), WIDTH)


def most_kernel(
    where_ref, back_ref, store_hbm, most_ref, seg_ref, coef_ref,
    left_ref, prefix_ref, suffix_ref, cols_ref, turned_ref, p_ref, s_ref, sem,
):
    loads = [
        pltpu.make_async_copy(source, target, sem.at[c])
        for c, (source, target) in enumerate(
            (
                (store_hbm.at[8], prefix_ref),
                (store_hbm.at[9], suffix_ref),
                (store_hbm.at[10, :, pl.ds(0, 40)], cols_ref),
                (store_hbm.at[11, 0], turned_ref),
                (store_hbm.at[11, 1, pl.ds(0, 24)], coef_ref),
                *(
                    (store_hbm.at[pl.ds(0, 8), j], left_ref.at[:, j])
                    for j in range(SPLITS)
                ),
            )
        )
    ]
    for load in loads:
        load.start()
    held = where_ref[3]
    for load in loads[:5]:
        load.wait()

    def add(u):
        prefix_ref[u] = prefix_ref[u] + p_ref[...]
        suffix_ref[u] = suffix_ref[u] + s_ref[...]

    for u in range(4):
        load_near(back_ref.at[pl.ds(8 * u, 8)], p_ref, s_ref)
        add(u)
    load_far(back_ref.at[:, pl.ds(32, 8)], p_ref, s_ref)
    add(4 + held)

    def spread_out(rows):
        return [jnp.broadcast_to(turned_ref[:, i : i + 1], (WIDTH, WIDTH)) for i in rows]

    turned = spread_out(range(32, 35))
    for u in range(8):
        value = (prefix_ref[u] + suffix_ref[u]) * coef_ref[16:17, :]
        for i in range(3):
            value = value + turned[i] * cols_ref[u, 32 + i : 33 + i, :]
        seg_ref[:, shard_lanes(where_ref, u)] = value
    for j in range(SPLITS):
        loads[5 + j].wait()
        turned = spread_out(range(j, 32, 8))
        a, b = coef_ref[j : j + 1, :], coef_ref[8 + j : 9 + j, :]
        for u in range(8):
            value = (a + b) * left_ref[u, j] + a * prefix_ref[u] - b * suffix_ref[u]
            for i in range(4):
                value = value + turned[i] * cols_ref[u, 8 * i + j : 8 * i + j + 1, :]
            most_ref[j, :, shard_lanes(where_ref, u)] = value


def last_kernel(
    where_ref, most_ref, most_seg_ref, coef_ref, opposite_ref, next_ref, before_ref, cusum_hbm, seg_hbm,
    cusum_ref, seg_ref, prefix_ref, suffix_ref, p_ref, s_ref, sem,
):
    shards = (5 - where_ref[3], 6, 7)
    for v, (ref, load) in enumerate(
        ((opposite_ref, load_far), (next_ref, load_near), (before_ref, load_near))
    ):
        load(ref, p_ref, s_ref)
        prefix_ref[v] = p_ref[...].T
        suffix_ref[v] = s_ref[...].T
    seg_ref[0] = most_seg_ref[...]
    for v, u in enumerate(shards):
        lanes = shard_lanes(where_ref, u)
        added = (prefix_ref[v] + suffix_ref[v]) * coef_ref[16:17, :]
        seg_ref[0, :, lanes] = most_seg_ref[:, lanes] + added
    stores = [pltpu.make_async_copy(seg_ref, seg_hbm, sem.at[SPLITS])]
    stores[0].start()
    for j in range(SPLITS):
        a, b = coef_ref[j : j + 1, :], coef_ref[8 + j : 9 + j, :]
        cusum_ref[0, j] = most_ref[j]
        for v, u in enumerate(shards):
            lanes = shard_lanes(where_ref, u)
            cusum_ref[0, j, :, lanes] = most_ref[j, :, lanes] + a * prefix_ref[v] - b * suffix_ref[v]
        store = pltpu.make_async_copy(
            cusum_ref.at[:, pl.ds(j, 1)], cusum_hbm.at[:, pl.ds(j, 1)], sem.at[j]
        )
        store.start()
        stores.append(store)
    for store in stores:
        store.wait()


OUTPUTS = [array(1, SPLITS, WIDTH, CHIPS * PAIR), array(1, WIDTH, CHIPS * PAIR)]
MOST = [array(SPLITS, WIDTH, CHIPS * PAIR), array(WIDTH, CHIPS * PAIR), array(24, WIDTH)]


def most_outputs(where, back, store):
    square = array(8, WIDTH, WIDTH)
    buffers = [array(8, SPLITS, WIDTH, WIDTH), square, square, array(8, 40, WIDTH)]
    buffers += [array(WIDTH, WIDTH)] * 3
    return pl.pallas_call(
        most_kernel,
        out_shape=MOST,
        grid=(1,),
        in_specs=[SM, whole(*back.shape), HBM],
        out_specs=[whole(*value.shape) for value in MOST],
        scratch_shapes=[pltpu.VMEM(value.shape, F32) for value in buffers]
        + [pltpu.SemaphoreType.DMA((5 + SPLITS,))],
        compiler_params=params(24),
        cost_estimate=cost(5),
        name="most_outputs",
    )(where, back, store)


def last_outputs(where, most, opposite, following, before):
    inputs = [*most, opposite, following, before]
    buffers = [*OUTPUTS, array(3, WIDTH, WIDTH), array(3, WIDTH, WIDTH)]
    buffers += [array(WIDTH, WIDTH)] * 2
    return pl.pallas_call(
        last_kernel,
        out_shape=OUTPUTS,
        grid=(1,),
        in_specs=[SM] + [whole(*value.shape) for value in inputs],
        out_specs=[HBM, HBM],
        scratch_shapes=[pltpu.VMEM(value.shape, F32) for value in buffers]
        + [pltpu.SemaphoreType.DMA((SPLITS + 1,))],
        compiler_params=params(24),
        cost_estimate=cost(3),
        name="last_outputs",
    )(where, *inputs)


def window_kernel(
    where_ref, halves, gram_ref, stat_ref, total_ref, out_ref, cent_ref, flip_ref, sum_ref,
):
    live = jnp.where(where_ref[0] > 0, 1.0, 0.0).astype(F32)
    core = where_ref[2]
    at = pl.multiple_of(core * WIDTH, WIDTH)
    off = pl.multiple_of((1 - core) * WIDTH, WIDTH)
    count = ROWS + live * HALO
    scale = wide(1.0 / jnp.full((1, WIDTH), count, F32))
    unbias = wide(1.0 / jnp.full((1, WIDTH), count - 1.0, F32))
    step = 256
    for r in range(CHIPS):
        lanes = (at, off) if r == 0 else (0, WIDTH)
        for raw, lane in zip(halves[2 * r : 2 * r + 2], lanes):
            mean = stat_ref[r, 0:1, pl.ds(lane, WIDTH)]

            def shift(i, _, raw=raw, lane=lane, mean=mean):
                piece = (raw[pl.ds(i * step, step), :].astype(F32) - mean) * live
                cent_ref[pl.ds(i * step, step), pl.ds(lane, WIDTH)] = piece.astype(BF16)
                return 0

            lax.fori_loop(0, HALO // step, shift, 0, unroll=2)
        if r == 0:
            flip_ref[...] = cent_ref[:, pl.ds(at, WIDTH)].T
            flipped = flip_ref[...]
            row_sum = jnp.dot(flipped, jnp.ones((HALO, WIDTH), BF16), preferred_element_type=F32)
            sum_ref[...] = row_sum + total_ref[...]
        cent = cent_ref[...]
        halo = jnp.dot(flip_ref[...], cent, preferred_element_type=F32)
        col_sum = jnp.dot(jnp.ones((16, HALO), BF16), cent, preferred_element_type=F32)[0:1]
        col_sum = col_sum + stat_ref[r, 1:2, :]
        value = (halo + gram_ref[r] - wide(sum_ref[...]) * (col_sum * scale)) * unbias
        for c in range(2):
            lane = pl.multiple_of(where_ref[4 + 2 * r + c] * WIDTH, WIDTH)
            out_ref[0, :, pl.ds(lane, WIDTH)] = value[:, c * WIDTH : (c + 1) * WIDTH]


def late_kernel(
    where_ref, h0, h1, h2, h3, h4, h5, h6, h7, total_ref, sums_ref, gram_ref, stat_ref,
    own_ref, ahead_ref, behind_ref, far_ref, flags_ref,
    turned_ref, cols_ref, coef_ref, before_ref, after_ref, window_ref, vectors, cent_ref, flip_ref, sum_ref,
):
    prep_kernel(
        where_ref, sums_ref, gram_ref, stat_ref, own_ref, ahead_ref, behind_ref, far_ref, flags_ref,
        turned_ref, cols_ref, coef_ref, before_ref, after_ref, vectors,
    )
    window_kernel(
        where_ref, (h0, h1, h2, h3, h4, h5, h6, h7), gram_ref, stat_ref, total_ref,
        window_ref, cent_ref, flip_ref, sum_ref,
    )


def late_terms(where, halves, total, sums, gram, stat, means, flags, store):
    square = (8, WIDTH, WIDTH)
    return call(
        late_kernel,
        "late_terms",
        [where, *halves, total, sums, gram, stat, *means, flags],
        [array(1, WIDTH, CHIPS * PAIR)],
        store=store,
        puts=(
            ((WIDTH, WIDTH), (11, 0)),
            ((8, 40, WIDTH), (10, slice(None), pl.ds(0, 40))),
            ((24, WIDTH), (11, 1, pl.ds(0, 24))),
            (square, 8),
            (square, 9),
        ),
        fetched=(9, 10, 11, 12, 13, 17),
        stored=(0,),
        scratch=[
            ((WIDTH, WIDTH), F32),
            ((HALO, PAIR), BF16),
            ((WIDTH, HALO), BF16),
            ((WIDTH, WIDTH), F32),
        ],
        us=0.1,
    )


def to_chan(value, target):
    count = lax.axis_size("chan")
    return lax.ppermute(value, "chan", [(s, target(s) % count) for s in range(count)])


def exchange(value):
    return lax.all_to_all(value, "tm", 0, 0, tiled=True)


def after(value, *others):
    return lax.optimization_barrier((value, *others))[0]


def local(samples, candidates, segment_start):
    here, index = lax.axis_index("tm"), lax.axis_index("chan")
    chip, core = index // 2, index % 2
    nearby = [2 * chip, 2 * chip + 1]
    for step, side in ((1, core), (3, 1 - core), (2, core), (2, 1 - core), (1, 1 - core), (3, core)):
        nearby.append(2 * ((chip + step) % CHIPS) + side)
    held = jnp.where(chip < CHIPS // 2, 0, 1)
    where = jnp.stack([here, chip, core, held] + nearby).astype(jnp.int32)
    where = jnp.concatenate([where, candidates[0], segment_start])

    behind = to_chan(samples, lambda s: s + 2)
    ahead = to_chan(samples, lambda s: s - 2)
    other = to_chan(samples, lambda s: s ^ 1)
    prior = lax.ppermute(samples[ROWS - HALO :], "tm", [(b, b + 1) for b in range(BLOCKS - 1)])
    flip_shape, square = array(WIDTH, ROWS, dtype=BF16), array(WIDTH, WIDTH)
    store, sums, gram, stat, late_flipped, late_total, flipped, spread0, total, rider = call(
        first_kernel,
        "first_pair",
        [where, samples, other],
        ALL + [flip_shape, square, flip_shape, array(WIDTH, PAIR), square, array(8, WIDTH)],
        puts=((SHARD_PAIR, pl.ds(0, 2)),),
        fetched=(1,),
        stored=(0, 1, 2, 3, 4),
        scratch=[((ROWS, PAIR), BF16)],
    )
    behind, ahead, prior, flipped = lax.optimization_barrier((behind, ahead, prior, flipped))
    half = ROWS // 2
    far_low = to_chan(behind[:half], lambda s: s + 2)
    far_high = to_chan(ahead[half:], lambda s: s - 2)
    behind_other = to_chan(behind, lambda s: s ^ 1)
    ahead_other = to_chan(ahead, lambda s: s ^ 1)
    store, sums, gram, stat, spread1 = call(
        near_kernel,
        "near_pair",
        [where, ahead, behind_other, flipped, total],
        ALL + [array(WIDTH, PAIR)],
        store=store,
        puts=((SHARD_PAIR, pl.ds(2, 2)),),
        stored=(0, 1, 2),
        kept=(sums, gram, stat),
        pair=1,
        scratch=[((ROWS, PAIR), BF16)],
    )
    store, sums, gram, stat = call(
        side_kernel,
        "side_pair",
        [where, ahead_other, behind, flipped],
        ALL,
        store=store,
        puts=((SHARD_PAIR, pl.ds(6, 2)),),
        stored=(0, 1, 2),
        kept=(sums, gram, stat),
        pair=3,
        scratch=[((ROWS, PAIR), BF16)],
        us=2,
    )
    far_low, far_high, stat = lax.optimization_barrier((far_low, far_high, stat))
    far = jnp.concatenate([far_low, far_high], axis=0)
    far_other = to_chan(far, lambda s: s ^ 1)
    gram, stat, pieces = call(
        far_kernel,
        "far_pair",
        [where, far, far_other, flipped, total, spread0, spread1, rider],
        ALL[1:] + [array(BLOCKS, 24, WIDTH)],
        stored=(0, 1),
        kept=(gram, stat),
        pair=2,
        scratch=[((WIDTH, WIDTH), F32), ((ROWS, PAIR), BF16)],
        us=0.1,
    )
    arrived = exchange(pieces)

    store, sums = call(
        rest_kernel,
        "rest_left",
        [where, after(far, pieces), far_other, late_flipped],
        ALL[:1],
        store=store,
        puts=((SHARD_PAIR, pl.ds(4, 2)),),
        fetched=(3,),
        stored=(0,),
        kept=(sums,),
        pair=2,
        scratch=[((ROWS, PAIR), BF16), ((1, 8, PAIR), F32)],
        us=4,
    )
    prior = after(prior, token(pieces))
    prior_ahead = to_chan(prior, lambda s: s - 2)
    prior_behind = to_chan(prior, lambda s: s + 2)
    prior_far = to_chan(prior, lambda s: s + 4)
    arrived, prior_ahead, prior_behind, sums = lax.optimization_barrier(
        (arrived, prior_ahead, prior_behind, sums)
    )
    scanned, own_means, flags = call(
        scan_kernel,
        "scan_pieces",
        [arrived],
        [array(BLOCKS, 40, WIDTH), array(2, BLOCKS, WIDTH), array(BLOCKS, WIDTH)],
        stored=(0, 1, 2),
        us=1,
    )
    back = exchange(scanned)
    own_means, prior_far = lax.optimization_barrier((own_means, prior_far))
    ahead_means = to_chan(own_means, lambda s: s - 2)
    behind_means = to_chan(own_means, lambda s: s + 2)
    far_means = to_chan(own_means, lambda s: s + 4)
    means = (own_means, ahead_means, behind_means, far_means)
    halo = (prior, prior_ahead, prior_far, prior_behind)
    halo, means = lax.optimization_barrier((halo, means))
    mine, other = halo, [to_chan(value, lambda s: s ^ 1) for value in halo]
    halves = (mine[0], other[0], mine[1], other[3], mine[2], other[2], other[1], mine[3])
    store, window_cov = late_terms(
        where, halves, late_total, sums, gram, stat, means, flags, store
    )
    back, store, window_cov = lax.optimization_barrier((back, store, window_cov))
    before = to_chan(back[16:24, 0:32], lambda s: s + 2)
    following = to_chan(back[24:32, 0:32], lambda s: (s - 2) ^ 1)
    opposite = to_chan(back[:, 32:40], lambda s: s + 4 if s < 4 else (s - 4) ^ 1)
    most = most_outputs(where, back, store)
    cusum, segment_cov = last_outputs(where, most, opposite, following, before)
    return window_cov, segment_cov, cusum


def solution(mesh):
    placed = (P("tm", "chan"), P("tm", None), P("tm"))
    return jax.shard_map(
        local,
        mesh=mesh,
        in_specs=placed,
        out_specs=(P("tm", "chan", None), P("tm", "chan", None), P("tm", None, "chan", None)),
        check_vma=False,
    )
```

```python
import jax
import jax.numpy as jnp
from jax import lax
from jax.experimental import pallas as pl
from jax.experimental.pallas import tpu as pltpu
from jax.sharding import PartitionSpec as P

F32, BF16 = jnp.float32, jnp.bfloat16
ROWS, HALO, WIDTH, BLOCKS, SPLITS, CHIPS = 2048, 1024, 128, 32, 8, 4
PAIR = 2 * WIDTH
HIGH = lax.Precision.HIGHEST
TRANSPOSED = (((0,), (0,)), ((), ()))
SM = pl.BlockSpec(memory_space=pltpu.SMEM)
HBM = pl.BlockSpec(memory_space=pltpu.HBM)
MIB = 2**20


def whole(*shape):
    return pl.BlockSpec(shape, lambda *_: (0,) * len(shape))


def array(*shape, dtype=F32):
    return jax.ShapeDtypeStruct(shape, dtype)


def params(grant):
    return pltpu.CompilerParams(
        vmem_limit_bytes=grant * MIB, dimension_semantics=("arbitrary",)
    )


def cost(microseconds):
    return pl.CostEstimate(
        flops=int(microseconds * 1e9), bytes_accessed=MIB, transcendentals=0
    )


def center_shard(raw_ref, out_ref, at):
    step = 256

    def add(i, total):
        piece = raw_ref[pl.ds(i * step, step), :].astype(F32)
        return total + jnp.sum(piece.reshape(step // 8, 8, WIDTH), axis=0)

    total = lax.fori_loop(0, ROWS // step, add, jnp.zeros((8, WIDTH), F32), unroll=2)
    mean = jnp.sum(total, axis=0, keepdims=True) / ROWS

    def shift(i, _):
        piece = raw_ref[pl.ds(i * step, step), :].astype(F32) - mean
        out_ref[pl.ds(i * step, step), pl.ds(at, WIDTH)] = piece.astype(BF16)
        return 0

    lax.fori_loop(0, ROWS // step, shift, 0, unroll=2)
    return mean


def center_pair(first_ref, second_ref, at, off, cent_ref, stat_ref):
    stat_ref[0] = jnp.zeros((8, PAIR), F32)
    stat_ref[0, 0:1, pl.ds(at, WIDTH)] = center_shard(first_ref, cent_ref, at)
    stat_ref[0, 0:1, pl.ds(off, WIDTH)] = center_shard(second_ref, cent_ref, off)
    total = jnp.dot(jnp.ones((16, ROWS), BF16), cent_ref[...], preferred_element_type=F32)[0:1]
    stat_ref[0, 1:2, :] = total
    stat_ref[0, 2:3, :] = stat_ref[0, 0:1, :] + total / ROWS


def turned_dot(left, right):
    return lax.dot_general(left, right, TRANSPOSED, preferred_element_type=F32)


def wide(value):
    return jnp.concatenate([value, value], axis=1)


def left_part(where_ref, flipped, cent_ref, left_ref, sums_ref, block=0):
    index = lax.broadcasted_iota(jnp.int32, (16, ROWS), 0)
    place = lax.broadcasted_iota(jnp.int32, (16, ROWS), 1)
    limit = jnp.zeros((16, ROWS), jnp.int32)
    for j in range(SPLITS):
        limit = jnp.where(index == j, where_ref[12 + j], limit)
    masks = jnp.where(place < limit, 1.0, 0.0).astype(BF16)
    cent = cent_ref[...]
    sums_ref[block] = jnp.dot(masks, cent, preferred_element_type=F32)[0:8]
    for i in range(SPLITS // 4):
        kept = jnp.concatenate([flipped * masks[j : j + 1, :] for j in range(4 * i, 4 * i + 4)], axis=0)
        part = jnp.dot(kept, cent, preferred_element_type=F32)
        for j in range(4):
            for c in range(2):
                rows, lanes = slice(j * WIDTH, (j + 1) * WIDTH), slice(c * WIDTH, (c + 1) * WIDTH)
                left_ref[c, 4 * i + j] = part[rows, lanes]


def first_kernel(
    where_ref, mine_ref, other_ref,
    left_ref, sums_ref, gram_ref, stat_ref, flip_hbm, total_hbm, flip_ref, spread_ref, total_ref, rider_ref, cent_ref,
):
    core = where_ref[2]
    at = pl.multiple_of(core * WIDTH, WIDTH)
    off = pl.multiple_of((1 - core) * WIDTH, WIDTH)
    center_pair(mine_ref, other_ref, at, off, cent_ref, stat_ref)
    rider_ref[...] = jnp.zeros((8, WIDTH), F32)
    rider_ref[0:1, :] = stat_ref[0, 2:3, 0:WIDTH]
    rider_ref[1:2, :] = stat_ref[0, 2:3, WIDTH:PAIR]
    rider_ref[2:3, :] = jnp.full((1, WIDTH), where_ref[20], jnp.int32).astype(F32)
    flip_ref[...] = cent_ref[:, pl.ds(at, WIDTH)].T
    flipped = flip_ref[...]
    flip_hbm[...] = flipped
    gram = jnp.dot(flipped, cent_ref[...], preferred_element_type=F32)
    gram_ref[0] = gram
    total = jnp.dot(flipped, jnp.ones((ROWS, WIDTH), BF16), preferred_element_type=F32)
    total_ref[...] = total
    total_hbm[...] = total
    spread_ref[...] = gram - wide(total) * (stat_ref[0, 1:2, :] / ROWS)
    left_part(where_ref, flipped, cent_ref, left_ref, sums_ref)


def near_kernel(
    where_ref, first_ref, second_ref, flip_ref, total_ref,
    left_ref, sums_ref, gram_ref, stat_ref, spread_ref, cent_ref,
):
    center_pair(first_ref, second_ref, 0, WIDTH, cent_ref, stat_ref)
    flipped = flip_ref[...]
    gram = jnp.dot(flipped, cent_ref[...], preferred_element_type=F32)
    gram_ref[0] = gram
    spread_ref[...] = gram - wide(total_ref[...]) * (stat_ref[0, 1:2, :] / ROWS)
    left_part(where_ref, flipped, cent_ref, left_ref, sums_ref)


def side_kernel(
    where_ref, first_ref, second_ref, flip_ref, left_ref, sums_ref, gram_ref, stat_ref, cent_ref
):
    center_pair(first_ref, second_ref, 0, WIDTH, cent_ref, stat_ref)
    flipped = flip_ref[...]
    gram_ref[0] = jnp.dot(flipped, cent_ref[...], preferred_element_type=F32)
    left_part(where_ref, flipped, cent_ref, left_ref, sums_ref)


def far_kernel(
    where_ref, first_ref, second_ref, flip_ref, total_ref, spread0_ref, spread1_ref, rider_ref,
    gram_ref, stat_ref, out_ref, held_ref, cent_ref,
):
    rider = rider_ref[0:4, :]
    for q in range(BLOCKS):
        spread, lane = ((spread0_ref, spread1_ref)[q // 16], WIDTH * (q // 8 % 2))
        row = 16 * (q % 8)
        out_ref[q, 0:16, :] = spread[row : row + 16, lane : lane + WIDTH]
        out_ref[q, 20:24, :] = rider
    center_pair(first_ref, second_ref, 0, WIDTH, cent_ref, stat_ref)
    gram = jnp.dot(flip_ref[...], cent_ref[...], preferred_element_type=F32)
    gram_ref[0] = gram
    spread = gram - wide(total_ref[...]) * (stat_ref[0, 1:2, :] / ROWS)
    held_ref[...] = jnp.where(where_ref[3] == 0, spread[:, 0:WIDTH], spread[:, WIDTH:PAIR])
    for q in range(BLOCKS):
        out_ref[q, 16:20, :] = held_ref[4 * q : 4 * q + 4, :]


def rest_kernel(where_ref, first_ref, second_ref, flip_ref, left_ref, sums_ref, cent_ref, stat_ref):
    center_pair(first_ref, second_ref, 0, WIDTH, cent_ref, stat_ref)
    left_part(where_ref, flip_ref[...], cent_ref, left_ref, sums_ref)


def token_kernel(pieces_ref, out_ref):
    out_ref[...] = jnp.zeros((8, WIDTH), F32)


def token(pieces):
    return pl.pallas_call(
        token_kernel,
        out_shape=array(8, WIDTH),
        grid=(1,),
        in_specs=[HBM],
        out_specs=whole(8, WIDTH),
        compiler_params=params(16),
        cost_estimate=cost(4),
        name="token",
    )(pieces)


ALL = [
    array(CHIPS, 8, PAIR),
    array(CHIPS, WIDTH, PAIR),
    array(CHIPS, 8, PAIR),
]


STORE = array(96, 8, WIDTH, WIDTH)
SHARD_PAIR = (2, SPLITS, WIDTH, WIDTH)


def call(
    kernel, name, inputs, outputs, *, store=None, puts=(), fetched=(), stored=(), kept=(),
    pair=0, span=1, scratch=(), us=3, grant=24,
):
    kept = (*([store] if store is not None else []), *kept)
    count, made, first = len(inputs), len(outputs), 1 if puts else 0
    sliced = [out in ALL for out in outputs]
    sizes = [(span, *out.shape[1:]) if cut else out.shape for out, cut in zip(outputs, sliced)]
    buffers = [pltpu.VMEM(inputs[i].shape, inputs[i].dtype) for i in fetched]
    buffers += [pltpu.VMEM(shape, F32) for shape, _ in puts]
    buffers += [pltpu.VMEM(sizes[i], outputs[i].dtype) for i in stored]

    def body(*refs):
        ins, refs = list(refs[:count]), refs[count + len(kept) :]
        slots, outs, refs = refs[:first], list(refs[first : first + made]), refs[first + made :]
        own, buffer, sem = refs[: len(scratch)], refs[len(scratch) : -1], refs[-1]
        copies = []
        for c, i in enumerate(fetched):
            copies.append(pltpu.make_async_copy(ins[i], buffer[c], sem.at[c]))
            ins[i] = buffer[c]
        for copy in copies:
            copy.start()
        for copy in copies:
            copy.wait()
        copies, mine = [], []
        for c, (_, place) in enumerate(puts, len(fetched)):
            copies.append(pltpu.make_async_copy(buffer[c], slots[0].at[place], sem.at[c]))
            mine.append(buffer[c])
        for c, i in enumerate(stored, len(fetched) + len(puts)):
            target = outs[i].at[pl.ds(pair, span)] if sliced[i] else outs[i]
            copies.append(pltpu.make_async_copy(buffer[c], target, sem.at[c]))
            outs[i] = buffer[c]
        kernel(*ins, *mine, *outs, *own)
        for copy in copies:
            copy.start()
        for copy in copies:
            copy.wait()

    ins = [SM if value.dtype == jnp.int32 else whole(*value.shape) for value in inputs]
    for i in fetched:
        ins[i] = HBM
    outs = [HBM if i in stored else whole(*out.shape) for i, out in enumerate(outputs)]
    aliased = range(first if store is None else 0, first + len(kept))
    return pl.pallas_call(
        body,
        out_shape=[STORE] * first + outputs,
        grid=(1,),
        in_specs=ins + [HBM] * len(kept),
        out_specs=[HBM] * first + outs,
        input_output_aliases={count + i: out for i, out in zip(range(len(kept)), aliased)},
        scratch_shapes=[pltpu.VMEM(shape, dtype) for shape, dtype in scratch]
        + buffers
        + [pltpu.SemaphoreType.DMA((max(len(buffers), 1),))],
        compiler_params=params(grant),
        cost_estimate=cost(us),
        name=name,
    )(*inputs, *kept)


def scan_kernel(arrived_ref, both_ref, means_ref, flags_ref):
    for b in range(BLOCKS):
        rider = arrived_ref[b, 16:24, :]
        means_ref[0, b : b + 1, :] = rider[4:5, :]
        means_ref[1, b : b + 1, :] = rider[5:6, :]
        flags_ref[b : b + 1, :] = rider[6:7, :]
    scan(arrived_ref, flags_ref, both_ref, 0, 16, 0)
    scan(arrived_ref, flags_ref, both_ref, 16, 4, 32)


def scan(arrived_ref, flags_ref, both_ref, row, size, at):
    zero = jnp.zeros((size, WIDTH), F32)
    running = zero
    for b in range(BLOCKS):
        begins = flags_ref[b : b + 1, :] > 0.5
        running = jnp.where(begins, zero, running)
        both_ref[b, at : at + size, :] = running
        running = running + arrived_ref[b, row : row + size, :]
    running = zero
    for b in reversed(range(BLOCKS)):
        begins = flags_ref[b : b + 1, :] > 0.5
        both_ref[b, at + size : at + 2 * size, :] = running
        running = jnp.where(begins, zero, running + arrived_ref[b, row : row + size, :])


def prep_kernel(
    where_ref, sums_ref, gram_ref, stat_ref, own_means_ref, ahead_ref, behind_ref, far_ref, flags_ref,
    turned_ref, cols_ref, coef_ref, before_ref, after_ref, vectors,
):
    here = where_ref[0]
    core = where_ref[2]
    away = 1 - core
    flags = flags_ref[...]
    spot = lax.broadcasted_iota(jnp.int32, (BLOCKS, WIDTH), 0)
    low = lax.broadcasted_iota(jnp.int32, (BLOCKS, BLOCKS), 1)
    high = lax.broadcasted_iota(jnp.int32, (BLOCKS, BLOCKS), 0)
    upto = jnp.dot((low <= high).astype(F32), flags, preferred_element_type=F32)
    mine = jnp.sum(jnp.where(spot <= here, flags, 0.0), axis=0, keepdims=True)
    same = jnp.abs(upto - mine) < 0.5
    masks = [
        jnp.where(same & (spot < here), 1.0, 0.0),
        jnp.where(same & (spot > here), 1.0, 0.0),
    ]
    totals = [jnp.sum(mask, axis=0, keepdims=True) for mask in masks]
    count_p, count_s = totals[0] * ROWS, totals[1] * ROWS

    def pooled(means, side):
        mask = masks[side]
        mean = jnp.sum(means * mask, axis=0, keepdims=True) / jnp.maximum(totals[side], 1.0)
        return mean, (means - mean) * mask

    def pick(value):
        return jnp.where(core == 0, value[:, 0:WIDTH], value[:, WIDTH:PAIR])

    row_means = own_means_ref[core]
    row_p, row_part_p = pooled(row_means, 0)
    row_s, row_part_s = pooled(row_means, 1)
    row_stat = pick(stat_ref[0])
    row_sums = pick(sums_ref[0])

    index = lax.broadcasted_iota(jnp.int32, (SPLITS, WIDTH), 0)
    k = jnp.zeros((SPLITS, WIDTH), jnp.int32)
    for j in range(SPLITS):
        k = jnp.where(index == j, where_ref[12 + j], k)
    k = k.astype(F32)
    rest = ROWS - k
    row_right = row_stat[1:2] - row_sums
    row_d = row_stat[0:1] + row_sums / k - row_p
    row_e = row_s - (row_stat[0:1] + row_right / rest)
    n_left, n_right = count_p + k, rest + count_s
    n = n_left + n_right
    weight = n_left * n_right / (n * n)
    a, b = weight / n_left, weight / n_right
    coef_ref[0:8, :] = a
    coef_ref[8:16, :] = b
    vectors[0:8, :] = -a * row_sums / k
    vectors[8:16, :] = a * (count_p * k / n_left) * row_d
    vectors[16:24, :] = b * row_right / rest
    vectors[24:32, :] = -b * (rest * count_s / n_right) * row_e
    total = count_p + ROWS
    n = total + count_s
    row_d = row_stat[2:3] - row_p
    row_e = row_s - (row_p + row_d * (ROWS / total))
    coef_ref[16:24, :] = jnp.broadcast_to(1.0 / n, (8, WIDTH))
    vectors[32:WIDTH, :] = jnp.zeros((WIDTH - 32, WIDTH), F32)
    vectors[32:33, :] = row_stat[1:2] / -ROWS / n
    vectors[33:34, :] = (count_p * ROWS / total) / n * row_d
    vectors[34:35, :] = (total * count_s / n) / n * row_e
    turned_ref[...] = vectors[...].T

    columns = (
        (own_means_ref[0], own_means_ref[1]),
        (ahead_ref[core], behind_ref[away]),
        (far_ref[core], far_ref[away]),
        (ahead_ref[away], behind_ref[core]),
    )
    for u in range(8):
        r, lanes = u // 2, slice(WIDTH * (u % 2), WIDTH * (u % 2) + WIDTH)
        means = columns[r][u % 2]
        col_p, col_part_p = pooled(means, 0)
        col_s, col_part_s = pooled(means, 1)
        stat = stat_ref[r, :, lanes]
        col_left = sums_ref[r, :, lanes]
        col_right = stat[1:2] - col_left
        cols_ref[u, 0:8, :] = col_left
        cols_ref[u, 8:16, :] = stat[0:1] + col_left / k - col_p
        cols_ref[u, 16:24, :] = col_right
        cols_ref[u, 24:32, :] = col_s - (stat[0:1] + col_right / rest)
        col_d = stat[2:3] - col_p
        cols_ref[u, 32:40, :] = jnp.zeros((8, WIDTH), F32)
        cols_ref[u, 32:33, :] = stat[1:2]
        cols_ref[u, 33:34, :] = col_d
        cols_ref[u, 34:35, :] = col_s - (col_p + col_d * (ROWS / total))

        def between(row_part, col_part):
            return ROWS * lax.dot_general(
                row_part, col_part, TRANSPOSED, precision=HIGH, preferred_element_type=F32
            )

        before_ref[u] = between(row_part_p, col_part_p)
        after_ref[u] = gram_ref[r, :, lanes] + between(row_part_s, col_part_s)


def load_near(ref, p_ref, s_ref):
    for g in range(8):
        p_ref[16 * g : 16 * g + 16, :] = ref[g, 0:16, :]
        s_ref[16 * g : 16 * g + 16, :] = ref[g, 16:32, :]


def load_far(ref, p_ref, s_ref):
    for q in range(BLOCKS):
        p_ref[4 * q : 4 * q + 4, :] = ref[q, 0:4, :]
        s_ref[4 * q : 4 * q + 4, :] = ref[q, 4:8, :]


def shard_lanes(where_ref, u):
    return pl.ds(pl.multiple_of(where_ref[4 + u] * WIDTH, WIDTH), WIDTH)


def most_kernel(
    where_ref, back_ref, store_hbm, most_ref, seg_ref, coef_ref,
    left_ref, prefix_ref, suffix_ref, cols_ref, turned_ref, p_ref, s_ref, sem,
):
    loads = [
        pltpu.make_async_copy(source, target, sem.at[c])
        for c, (source, target) in enumerate(
            (
                (store_hbm.at[8], prefix_ref),
                (store_hbm.at[9], suffix_ref),
                (store_hbm.at[10, :, pl.ds(0, 40)], cols_ref),
                (store_hbm.at[11, 0], turned_ref),
                (store_hbm.at[11, 1, pl.ds(0, 24)], coef_ref),
                *(
                    (store_hbm.at[pl.ds(0, 8), j], left_ref.at[:, j])
                    for j in range(SPLITS)
                ),
            )
        )
    ]
    for load in loads:
        load.start()
    held = where_ref[3]
    for load in loads[:5]:
        load.wait()

    def add(u):
        prefix_ref[u] = prefix_ref[u] + p_ref[...]
        suffix_ref[u] = suffix_ref[u] + s_ref[...]

    for u in range(4):
        load_near(back_ref.at[pl.ds(8 * u, 8)], p_ref, s_ref)
        add(u)
    load_far(back_ref.at[:, pl.ds(32, 8)], p_ref, s_ref)
    add(4 + held)

    def spread_out(rows):
        return [jnp.broadcast_to(turned_ref[:, i : i + 1], (WIDTH, WIDTH)) for i in rows]

    turned = spread_out(range(32, 35))
    for u in range(8):
        value = (prefix_ref[u] + suffix_ref[u]) * coef_ref[16:17, :]
        for i in range(3):
            value = value + turned[i] * cols_ref[u, 32 + i : 33 + i, :]
        seg_ref[:, shard_lanes(where_ref, u)] = value
    for j in range(SPLITS):
        loads[5 + j].wait()
        turned = spread_out(range(j, 32, 8))
        a, b = coef_ref[j : j + 1, :], coef_ref[8 + j : 9 + j, :]
        for u in range(8):
            value = (a + b) * left_ref[u, j] + a * prefix_ref[u] - b * suffix_ref[u]
            for i in range(4):
                value = value + turned[i] * cols_ref[u, 8 * i + j : 8 * i + j + 1, :]
            most_ref[j, :, shard_lanes(where_ref, u)] = value


def last_kernel(
    where_ref, most_ref, most_seg_ref, coef_ref, opposite_ref, next_ref, before_ref, cusum_hbm, seg_hbm,
    cusum_ref, seg_ref, prefix_ref, suffix_ref, p_ref, s_ref, sem,
):
    shards = (5 - where_ref[3], 6, 7)
    for v, (ref, load) in enumerate(
        ((opposite_ref, load_far), (next_ref, load_near), (before_ref, load_near))
    ):
        load(ref, p_ref, s_ref)
        prefix_ref[v] = p_ref[...].T
        suffix_ref[v] = s_ref[...].T
    seg_ref[0] = most_seg_ref[...]
    for v, u in enumerate(shards):
        lanes = shard_lanes(where_ref, u)
        added = (prefix_ref[v] + suffix_ref[v]) * coef_ref[16:17, :]
        seg_ref[0, :, lanes] = most_seg_ref[:, lanes] + added
    stores = [pltpu.make_async_copy(seg_ref, seg_hbm, sem.at[SPLITS])]
    stores[0].start()
    for j in range(SPLITS):
        a, b = coef_ref[j : j + 1, :], coef_ref[8 + j : 9 + j, :]
        cusum_ref[0, j] = most_ref[j]
        for v, u in enumerate(shards):
            lanes = shard_lanes(where_ref, u)
            cusum_ref[0, j, :, lanes] = most_ref[j, :, lanes] + a * prefix_ref[v] - b * suffix_ref[v]
        store = pltpu.make_async_copy(
            cusum_ref.at[:, pl.ds(j, 1)], cusum_hbm.at[:, pl.ds(j, 1)], sem.at[j]
        )
        store.start()
        stores.append(store)
    for store in stores:
        store.wait()


OUTPUTS = [array(1, SPLITS, WIDTH, CHIPS * PAIR), array(1, WIDTH, CHIPS * PAIR)]
MOST = [array(SPLITS, WIDTH, CHIPS * PAIR), array(WIDTH, CHIPS * PAIR), array(24, WIDTH)]


def most_outputs(where, back, store):
    square = array(8, WIDTH, WIDTH)
    buffers = [array(8, SPLITS, WIDTH, WIDTH), square, square, array(8, 40, WIDTH)]
    buffers += [array(WIDTH, WIDTH)] * 3
    return pl.pallas_call(
        most_kernel,
        out_shape=MOST,
        grid=(1,),
        in_specs=[SM, whole(*back.shape), HBM],
        out_specs=[whole(*value.shape) for value in MOST],
        scratch_shapes=[pltpu.VMEM(value.shape, F32) for value in buffers]
        + [pltpu.SemaphoreType.DMA((5 + SPLITS,))],
        compiler_params=params(24),
        cost_estimate=cost(5),
        name="most_outputs",
    )(where, back, store)


def last_outputs(where, most, opposite, following, before):
    inputs = [*most, opposite, following, before]
    buffers = [*OUTPUTS, array(3, WIDTH, WIDTH), array(3, WIDTH, WIDTH)]
    buffers += [array(WIDTH, WIDTH)] * 2
    return pl.pallas_call(
        last_kernel,
        out_shape=OUTPUTS,
        grid=(1,),
        in_specs=[SM] + [whole(*value.shape) for value in inputs],
        out_specs=[HBM, HBM],
        scratch_shapes=[pltpu.VMEM(value.shape, F32) for value in buffers]
        + [pltpu.SemaphoreType.DMA((SPLITS + 1,))],
        compiler_params=params(24),
        cost_estimate=cost(3),
        name="last_outputs",
    )(where, *inputs)


def window_kernel(
    where_ref, halves, gram_ref, stat_ref, total_ref, out_ref, cent_ref, flip_ref, sum_ref,
):
    live = jnp.where(where_ref[0] > 0, 1.0, 0.0).astype(F32)
    core = where_ref[2]
    at = pl.multiple_of(core * WIDTH, WIDTH)
    off = pl.multiple_of((1 - core) * WIDTH, WIDTH)
    count = ROWS + live * HALO
    scale = wide(1.0 / jnp.full((1, WIDTH), count, F32))
    unbias = wide(1.0 / jnp.full((1, WIDTH), count - 1.0, F32))
    step = 256
    for r in range(CHIPS):
        lanes = (at, off) if r == 0 else (0, WIDTH)
        for raws, lane in zip(halves[2 * r : 2 * r + 2], lanes):
            mean = stat_ref[r, 0:1, pl.ds(lane, WIDTH)]
            for index, raw in enumerate(raws):
                rows = raw.shape[0]

                def shift(i, _, raw=raw, first=index * rows, lane=lane, mean=mean):
                    piece = (raw[pl.ds(i * step, step), :].astype(F32) - mean) * live
                    cent_ref[pl.ds(first + i * step, step), pl.ds(lane, WIDTH)] = piece.astype(BF16)
                    return 0

                lax.fori_loop(0, rows // step, shift, 0, unroll=2)
        if r == 0:
            flip_ref[...] = cent_ref[:, pl.ds(at, WIDTH)].T
            flipped = flip_ref[...]
            row_sum = jnp.dot(flipped, jnp.ones((HALO, WIDTH), BF16), preferred_element_type=F32)
            sum_ref[...] = row_sum + total_ref[...]
        cent = cent_ref[...]
        halo = jnp.dot(flip_ref[...], cent, preferred_element_type=F32)
        col_sum = jnp.dot(jnp.ones((16, HALO), BF16), cent, preferred_element_type=F32)[0:1]
        col_sum = col_sum + stat_ref[r, 1:2, :]
        value = (halo + gram_ref[r] - wide(sum_ref[...]) * (col_sum * scale)) * unbias
        for c in range(2):
            lane = pl.multiple_of(where_ref[4 + 2 * r + c] * WIDTH, WIDTH)
            out_ref[0, :, pl.ds(lane, WIDTH)] = value[:, c * WIDTH : (c + 1) * WIDTH]


def late_kernel(
    where_ref, m0, m1, m2, m3, m4, o0, o1, o2, o3, o4, total_ref, sums_ref, gram_ref, stat_ref,
    own_ref, ahead_ref, behind_ref, far_ref, flags_ref,
    turned_ref, cols_ref, coef_ref, before_ref, after_ref, window_ref, vectors, cent_ref, flip_ref, sum_ref,
):
    prep_kernel(
        where_ref, sums_ref, gram_ref, stat_ref, own_ref, ahead_ref, behind_ref, far_ref, flags_ref,
        turned_ref, cols_ref, coef_ref, before_ref, after_ref, vectors,
    )
    window_kernel(
        where_ref, ((m0,), (o0,), (m1,), (o4,), (m2, m3), (o2, o3), (o1,), (m4,)),
        gram_ref, stat_ref, total_ref,
        window_ref, cent_ref, flip_ref, sum_ref,
    )


def late_terms(where, halves, total, sums, gram, stat, means, flags, store):
    square = (8, WIDTH, WIDTH)
    return call(
        late_kernel,
        "late_terms",
        [where, *halves, total, sums, gram, stat, *means, flags],
        [array(1, WIDTH, CHIPS * PAIR)],
        store=store,
        puts=(
            ((WIDTH, WIDTH), (11, 0)),
            ((8, 40, WIDTH), (10, slice(None), pl.ds(0, 40))),
            ((24, WIDTH), (11, 1, pl.ds(0, 24))),
            (square, 8),
            (square, 9),
        ),
        fetched=(11, 12, 13, 14, 15, 19),
        stored=(0,),
        scratch=[
            ((WIDTH, WIDTH), F32),
            ((HALO, PAIR), BF16),
            ((WIDTH, HALO), BF16),
            ((WIDTH, WIDTH), F32),
        ],
        us=0.1,
    )


def to_chan(value, target):
    count = lax.axis_size("chan")
    return lax.ppermute(value, "chan", [(s, target(s) % count) for s in range(count)])


def exchange(value):
    return lax.all_to_all(value, "tm", 0, 0, tiled=True)


def after(value, *others):
    return lax.optimization_barrier((value, *others))[0]


def local(samples, candidates, segment_start):
    here, index = lax.axis_index("tm"), lax.axis_index("chan")
    chip, core = index // 2, index % 2
    nearby = [2 * chip, 2 * chip + 1]
    for step, side in ((1, core), (3, 1 - core), (2, core), (2, 1 - core), (1, 1 - core), (3, core)):
        nearby.append(2 * ((chip + step) % CHIPS) + side)
    held = jnp.where(chip < CHIPS // 2, 0, 1)
    where = jnp.stack([here, chip, core, held] + nearby).astype(jnp.int32)
    where = jnp.concatenate([where, candidates[0], segment_start])

    behind = to_chan(samples, lambda s: s + 2)
    ahead = to_chan(samples, lambda s: s - 2)
    other = to_chan(samples, lambda s: s ^ 1)
    prior = lax.ppermute(samples[ROWS - HALO :], "tm", [(b, b + 1) for b in range(BLOCKS - 1)])
    flip_shape, square = array(WIDTH, ROWS, dtype=BF16), array(WIDTH, WIDTH)
    store, sums, gram, stat, late_flipped, late_total, flipped, spread0, total, rider = call(
        first_kernel,
        "first_pair",
        [where, samples, other],
        ALL + [flip_shape, square, flip_shape, array(WIDTH, PAIR), square, array(8, WIDTH)],
        puts=((SHARD_PAIR, pl.ds(0, 2)),),
        fetched=(1,),
        stored=(0, 1, 2, 3, 4),
        scratch=[((ROWS, PAIR), BF16)],
    )
    behind, ahead, prior, flipped = lax.optimization_barrier((behind, ahead, prior, flipped))
    half = ROWS // 2
    far_low = to_chan(behind[:half], lambda s: s + 2)
    far_high = to_chan(ahead[half:], lambda s: s - 2)
    behind_other = to_chan(behind, lambda s: s ^ 1)
    ahead_other = to_chan(ahead, lambda s: s ^ 1)
    store, sums, gram, stat, spread1 = call(
        near_kernel,
        "near_pair",
        [where, ahead, behind_other, flipped, total],
        ALL + [array(WIDTH, PAIR)],
        store=store,
        puts=((SHARD_PAIR, pl.ds(2, 2)),),
        stored=(0, 1, 2),
        kept=(sums, gram, stat),
        pair=1,
        scratch=[((ROWS, PAIR), BF16)],
    )
    store, sums, gram, stat = call(
        side_kernel,
        "side_pair",
        [where, ahead_other, behind, flipped],
        ALL,
        store=store,
        puts=((SHARD_PAIR, pl.ds(6, 2)),),
        stored=(0, 1, 2),
        kept=(sums, gram, stat),
        pair=3,
        scratch=[((ROWS, PAIR), BF16)],
        us=2,
    )
    far_low, far_high, stat = lax.optimization_barrier((far_low, far_high, stat))
    far = jnp.concatenate([far_low, far_high], axis=0)
    far_other = to_chan(far, lambda s: s ^ 1)
    gram, stat, pieces = call(
        far_kernel,
        "far_pair",
        [where, far, far_other, flipped, total, spread0, spread1, rider],
        ALL[1:] + [array(BLOCKS, 24, WIDTH)],
        stored=(0, 1),
        kept=(gram, stat),
        pair=2,
        scratch=[((WIDTH, WIDTH), F32), ((ROWS, PAIR), BF16)],
        us=0.1,
    )
    arrived = exchange(pieces)

    store, sums = call(
        rest_kernel,
        "rest_left",
        [where, after(far, pieces), far_other, late_flipped],
        ALL[:1],
        store=store,
        puts=((SHARD_PAIR, pl.ds(4, 2)),),
        fetched=(3,),
        stored=(0,),
        kept=(sums,),
        pair=2,
        scratch=[((ROWS, PAIR), BF16), ((1, 8, PAIR), F32)],
        us=4,
    )
    prior = after(prior, token(pieces))
    prior_ahead = to_chan(prior, lambda s: s - 2)
    prior_behind = to_chan(prior, lambda s: s + 2)
    arrived, prior_ahead, prior_behind, sums = lax.optimization_barrier(
        (arrived, prior_ahead, prior_behind, sums)
    )
    half = HALO // 2
    prior_low = to_chan(prior_behind[:half], lambda s: s + 2)
    prior_high = to_chan(prior_ahead[half:], lambda s: s - 2)
    scanned, own_means, flags = call(
        scan_kernel,
        "scan_pieces",
        [arrived],
        [array(BLOCKS, 40, WIDTH), array(2, BLOCKS, WIDTH), array(BLOCKS, WIDTH)],
        stored=(0, 1, 2),
        us=1,
    )
    scanned, prior_low, prior_high = lax.optimization_barrier((scanned, prior_low, prior_high))
    back = exchange(scanned)
    ahead_means = to_chan(own_means, lambda s: s - 2)
    behind_means = to_chan(own_means, lambda s: s + 2)
    far_means = to_chan(own_means, lambda s: s + 4)
    means = (own_means, ahead_means, behind_means, far_means)
    halo = (prior, prior_ahead, prior_low, prior_high, prior_behind)
    halo, means = lax.optimization_barrier((halo, means))
    mine, other = halo, [to_chan(value, lambda s: s ^ 1) for value in halo]
    halves = (*mine, *other)
    store, window_cov = late_terms(
        where, halves, late_total, sums, gram, stat, means, flags, store
    )
    back, store, window_cov = lax.optimization_barrier((back, store, window_cov))
    before = to_chan(back[16:24, 0:32], lambda s: s + 2)
    following = to_chan(back[24:32, 0:32], lambda s: (s - 2) ^ 1)
    opposite = to_chan(back[:, 32:40], lambda s: s + 4 if s < 4 else (s - 4) ^ 1)
    most = most_outputs(where, back, store)
    cusum, segment_cov = last_outputs(where, most, opposite, following, before)
    return window_cov, segment_cov, cusum


def solution(mesh):
    placed = (P("tm", "chan"), P("tm", None), P("tm"))
    return jax.shard_map(
        local,
        mesh=mesh,
        in_specs=placed,
        out_specs=(P("tm", "chan", None), P("tm", "chan", None), P("tm", None, "chan", None)),
        check_vma=False,
    )
```

```python
import jax
import jax.numpy as jnp
from jax import lax
from jax.experimental import pallas as pl
from jax.experimental.pallas import tpu as pltpu
from jax.sharding import PartitionSpec as P

F32, BF16 = jnp.float32, jnp.bfloat16
ROWS, HALO, WIDTH, BLOCKS, SPLITS, CHIPS = 2048, 1024, 128, 32, 8, 4
PAIR = 2 * WIDTH
HIGH = lax.Precision.HIGHEST
TRANSPOSED = (((0,), (0,)), ((), ()))
SM = pl.BlockSpec(memory_space=pltpu.SMEM)
HBM = pl.BlockSpec(memory_space=pltpu.HBM)
MIB = 2**20


def whole(*shape):
    return pl.BlockSpec(shape, lambda *_: (0,) * len(shape))


def array(*shape, dtype=F32):
    return jax.ShapeDtypeStruct(shape, dtype)


def params(grant):
    return pltpu.CompilerParams(
        vmem_limit_bytes=grant * MIB, dimension_semantics=("arbitrary",)
    )


def cost(microseconds):
    return pl.CostEstimate(
        flops=int(microseconds * 1e9), bytes_accessed=MIB, transcendentals=0
    )


def center_shard(raw_ref, out_ref, at):
    step = 256

    def add(i, total):
        piece = raw_ref[pl.ds(i * step, step), :].astype(F32)
        return total + jnp.sum(piece.reshape(step // 8, 8, WIDTH), axis=0)

    total = lax.fori_loop(0, ROWS // step, add, jnp.zeros((8, WIDTH), F32), unroll=2)
    mean = jnp.sum(total, axis=0, keepdims=True) / ROWS

    def shift(i, _):
        piece = raw_ref[pl.ds(i * step, step), :].astype(F32) - mean
        out_ref[pl.ds(i * step, step), pl.ds(at, WIDTH)] = piece.astype(BF16)
        return 0

    lax.fori_loop(0, ROWS // step, shift, 0, unroll=2)
    return mean


def center_pair(first_ref, second_ref, at, off, cent_ref, stat_ref):
    stat_ref[0] = jnp.zeros((8, PAIR), F32)
    stat_ref[0, 0:1, pl.ds(at, WIDTH)] = center_shard(first_ref, cent_ref, at)
    stat_ref[0, 0:1, pl.ds(off, WIDTH)] = center_shard(second_ref, cent_ref, off)
    total = jnp.dot(jnp.ones((16, ROWS), BF16), cent_ref[...], preferred_element_type=F32)[0:1]
    stat_ref[0, 1:2, :] = total
    stat_ref[0, 2:3, :] = stat_ref[0, 0:1, :] + total / ROWS


def turned_dot(left, right):
    return lax.dot_general(left, right, TRANSPOSED, preferred_element_type=F32)


def wide(value):
    return jnp.concatenate([value, value], axis=1)


def left_part(where_ref, flipped, cent_ref, left_ref, sums_ref, block=0):
    index = lax.broadcasted_iota(jnp.int32, (16, ROWS), 0)
    place = lax.broadcasted_iota(jnp.int32, (16, ROWS), 1)
    limit = jnp.zeros((16, ROWS), jnp.int32)
    for j in range(SPLITS):
        limit = jnp.where(index == j, where_ref[12 + j], limit)
    masks = jnp.where(place < limit, 1.0, 0.0).astype(BF16)
    cent = cent_ref[...]
    sums_ref[block] = jnp.dot(masks, cent, preferred_element_type=F32)[0:8]
    for i in range(SPLITS // 4):
        kept = jnp.concatenate([flipped * masks[j : j + 1, :] for j in range(4 * i, 4 * i + 4)], axis=0)
        part = jnp.dot(kept, cent, preferred_element_type=F32)
        for j in range(4):
            for c in range(2):
                rows, lanes = slice(j * WIDTH, (j + 1) * WIDTH), slice(c * WIDTH, (c + 1) * WIDTH)
                left_ref[c, 4 * i + j] = part[rows, lanes]


def first_kernel(
    where_ref, mine_ref, other_ref,
    left_ref, sums_ref, gram_ref, stat_ref, flip_hbm, total_hbm, flip_ref, spread_ref, total_ref, rider_ref, cent_ref,
):
    core = where_ref[2]
    at = pl.multiple_of(core * WIDTH, WIDTH)
    off = pl.multiple_of((1 - core) * WIDTH, WIDTH)
    center_pair(mine_ref, other_ref, at, off, cent_ref, stat_ref)
    rider_ref[...] = jnp.zeros((8, WIDTH), F32)
    rider_ref[0:1, :] = stat_ref[0, 2:3, 0:WIDTH]
    rider_ref[1:2, :] = stat_ref[0, 2:3, WIDTH:PAIR]
    rider_ref[2:3, :] = jnp.full((1, WIDTH), where_ref[20], jnp.int32).astype(F32)
    flip_ref[...] = cent_ref[:, pl.ds(at, WIDTH)].T
    flipped = flip_ref[...]
    flip_hbm[...] = flipped
    gram = jnp.dot(flipped, cent_ref[...], preferred_element_type=F32)
    gram_ref[0] = gram
    total = jnp.dot(flipped, jnp.ones((ROWS, WIDTH), BF16), preferred_element_type=F32)
    total_ref[...] = total
    total_hbm[...] = total
    spread_ref[...] = gram - wide(total) * (stat_ref[0, 1:2, :] / ROWS)
    left_part(where_ref, flipped, cent_ref, left_ref, sums_ref)


def near_kernel(
    where_ref, first_ref, second_ref, flip_ref, total_ref,
    left_ref, sums_ref, gram_ref, stat_ref, spread_ref, cent_ref,
):
    center_pair(first_ref, second_ref, 0, WIDTH, cent_ref, stat_ref)
    flipped = flip_ref[...]
    gram = jnp.dot(flipped, cent_ref[...], preferred_element_type=F32)
    gram_ref[0] = gram
    spread_ref[...] = gram - wide(total_ref[...]) * (stat_ref[0, 1:2, :] / ROWS)
    left_part(where_ref, flipped, cent_ref, left_ref, sums_ref)


def side_kernel(
    where_ref, first_ref, second_ref, flip_ref, left_ref, sums_ref, gram_ref, stat_ref, cent_ref
):
    center_pair(first_ref, second_ref, 0, WIDTH, cent_ref, stat_ref)
    flipped = flip_ref[...]
    gram_ref[0] = jnp.dot(flipped, cent_ref[...], preferred_element_type=F32)
    left_part(where_ref, flipped, cent_ref, left_ref, sums_ref)


def far_kernel(
    where_ref, first_ref, second_ref, flip_ref, total_ref, spread0_ref, spread1_ref, rider_ref,
    gram_ref, stat_ref, out_ref, held_ref, cent_ref,
):
    rider = rider_ref[0:4, :]
    for q in range(BLOCKS):
        spread, lane = ((spread0_ref, spread1_ref)[q // 16], WIDTH * (q // 8 % 2))
        row = 16 * (q % 8)
        out_ref[q, 0:16, :] = spread[row : row + 16, lane : lane + WIDTH]
        out_ref[q, 20:24, :] = rider
    center_pair(first_ref, second_ref, 0, WIDTH, cent_ref, stat_ref)
    gram = jnp.dot(flip_ref[...], cent_ref[...], preferred_element_type=F32)
    gram_ref[0] = gram
    spread = gram - wide(total_ref[...]) * (stat_ref[0, 1:2, :] / ROWS)
    held_ref[...] = jnp.where(where_ref[3] == 0, spread[:, 0:WIDTH], spread[:, WIDTH:PAIR])
    for q in range(BLOCKS):
        out_ref[q, 16:20, :] = held_ref[4 * q : 4 * q + 4, :]


def rest_kernel(where_ref, first_ref, second_ref, flip_ref, left_ref, sums_ref, cent_ref, stat_ref):
    center_pair(first_ref, second_ref, 0, WIDTH, cent_ref, stat_ref)
    left_part(where_ref, flip_ref[...], cent_ref, left_ref, sums_ref)


def token_kernel(pieces_ref, out_ref):
    out_ref[...] = jnp.zeros((8, WIDTH), F32)


def token(pieces):
    return pl.pallas_call(
        token_kernel,
        out_shape=array(8, WIDTH),
        grid=(1,),
        in_specs=[HBM],
        out_specs=whole(8, WIDTH),
        compiler_params=params(16),
        cost_estimate=cost(4),
        name="token",
    )(pieces)


ALL = [
    array(CHIPS, 8, PAIR),
    array(CHIPS, WIDTH, PAIR),
    array(CHIPS, 8, PAIR),
]


STORE = array(96, 8, WIDTH, WIDTH)
SHARD_PAIR = (2, SPLITS, WIDTH, WIDTH)


def call(
    kernel, name, inputs, outputs, *, store=None, puts=(), fetched=(), stored=(), kept=(),
    pair=0, span=1, scratch=(), us=3, grant=24,
):
    kept = (*([store] if store is not None else []), *kept)
    count, made, first = len(inputs), len(outputs), 1 if puts else 0
    sliced = [out in ALL for out in outputs]
    sizes = [(span, *out.shape[1:]) if cut else out.shape for out, cut in zip(outputs, sliced)]
    buffers = [pltpu.VMEM(inputs[i].shape, inputs[i].dtype) for i in fetched]
    buffers += [pltpu.VMEM(shape, F32) for shape, _ in puts]
    buffers += [pltpu.VMEM(sizes[i], outputs[i].dtype) for i in stored]

    def body(*refs):
        ins, refs = list(refs[:count]), refs[count + len(kept) :]
        slots, outs, refs = refs[:first], list(refs[first : first + made]), refs[first + made :]
        own, buffer, sem = refs[: len(scratch)], refs[len(scratch) : -1], refs[-1]
        copies = []
        for c, i in enumerate(fetched):
            copies.append(pltpu.make_async_copy(ins[i], buffer[c], sem.at[c]))
            ins[i] = buffer[c]
        for copy in copies:
            copy.start()
        for copy in copies:
            copy.wait()
        copies, mine = [], []
        for c, (_, place) in enumerate(puts, len(fetched)):
            copies.append(pltpu.make_async_copy(buffer[c], slots[0].at[place], sem.at[c]))
            mine.append(buffer[c])
        for c, i in enumerate(stored, len(fetched) + len(puts)):
            target = outs[i].at[pl.ds(pair, span)] if sliced[i] else outs[i]
            copies.append(pltpu.make_async_copy(buffer[c], target, sem.at[c]))
            outs[i] = buffer[c]
        kernel(*ins, *mine, *outs, *own)
        for copy in copies:
            copy.start()
        for copy in copies:
            copy.wait()

    ins = [SM if value.dtype == jnp.int32 else whole(*value.shape) for value in inputs]
    for i in fetched:
        ins[i] = HBM
    outs = [HBM if i in stored else whole(*out.shape) for i, out in enumerate(outputs)]
    aliased = range(first if store is None else 0, first + len(kept))
    return pl.pallas_call(
        body,
        out_shape=[STORE] * first + outputs,
        grid=(1,),
        in_specs=ins + [HBM] * len(kept),
        out_specs=[HBM] * first + outs,
        input_output_aliases={count + i: out for i, out in zip(range(len(kept)), aliased)},
        scratch_shapes=[pltpu.VMEM(shape, dtype) for shape, dtype in scratch]
        + buffers
        + [pltpu.SemaphoreType.DMA((max(len(buffers), 1),))],
        compiler_params=params(grant),
        cost_estimate=cost(us),
        name=name,
    )(*inputs, *kept)


def scan_kernel(arrived_ref, both_ref, means_ref, flags_ref):
    for b in range(BLOCKS):
        rider = arrived_ref[b, 16:24, :]
        means_ref[0, b : b + 1, :] = rider[4:5, :]
        means_ref[1, b : b + 1, :] = rider[5:6, :]
        flags_ref[b : b + 1, :] = rider[6:7, :]
    scan(arrived_ref, flags_ref, both_ref, 0, 16, 0)
    scan(arrived_ref, flags_ref, both_ref, 16, 4, 32)


def scan(arrived_ref, flags_ref, both_ref, row, size, at):
    zero = jnp.zeros((size, WIDTH), F32)
    running = zero
    for b in range(BLOCKS):
        begins = flags_ref[b : b + 1, :] > 0.5
        running = jnp.where(begins, zero, running)
        both_ref[b, at : at + size, :] = running
        running = running + arrived_ref[b, row : row + size, :]
    running = zero
    for b in reversed(range(BLOCKS)):
        begins = flags_ref[b : b + 1, :] > 0.5
        both_ref[b, at + size : at + 2 * size, :] = running
        running = jnp.where(begins, zero, running + arrived_ref[b, row : row + size, :])


def prep_kernel(
    where_ref, sums_ref, gram_ref, stat_ref, own_means_ref, ahead_ref, behind_ref, far_ref, flags_ref,
    turned_ref, cols_ref, coef_ref, before_ref, after_ref, vectors,
):
    here = where_ref[0]
    core = where_ref[2]
    away = 1 - core
    flags = flags_ref[...]
    spot = lax.broadcasted_iota(jnp.int32, (BLOCKS, WIDTH), 0)
    low = lax.broadcasted_iota(jnp.int32, (BLOCKS, BLOCKS), 1)
    high = lax.broadcasted_iota(jnp.int32, (BLOCKS, BLOCKS), 0)
    upto = jnp.dot((low <= high).astype(F32), flags, preferred_element_type=F32)
    mine = jnp.sum(jnp.where(spot <= here, flags, 0.0), axis=0, keepdims=True)
    same = jnp.abs(upto - mine) < 0.5
    masks = [
        jnp.where(same & (spot < here), 1.0, 0.0),
        jnp.where(same & (spot > here), 1.0, 0.0),
    ]
    totals = [jnp.sum(mask, axis=0, keepdims=True) for mask in masks]
    count_p, count_s = totals[0] * ROWS, totals[1] * ROWS

    def pooled(means, side):
        mask = masks[side]
        mean = jnp.sum(means * mask, axis=0, keepdims=True) / jnp.maximum(totals[side], 1.0)
        return mean, (means - mean) * mask

    def pick(value):
        return jnp.where(core == 0, value[:, 0:WIDTH], value[:, WIDTH:PAIR])

    row_means = own_means_ref[core]
    row_p, row_part_p = pooled(row_means, 0)
    row_s, row_part_s = pooled(row_means, 1)
    row_stat = pick(stat_ref[0])
    row_sums = pick(sums_ref[0])

    index = lax.broadcasted_iota(jnp.int32, (SPLITS, WIDTH), 0)
    k = jnp.zeros((SPLITS, WIDTH), jnp.int32)
    for j in range(SPLITS):
        k = jnp.where(index == j, where_ref[12 + j], k)
    k = k.astype(F32)
    rest = ROWS - k
    row_right = row_stat[1:2] - row_sums
    row_d = row_stat[0:1] + row_sums / k - row_p
    row_e = row_s - (row_stat[0:1] + row_right / rest)
    n_left, n_right = count_p + k, rest + count_s
    n = n_left + n_right
    weight = n_left * n_right / (n * n)
    a, b = weight / n_left, weight / n_right
    coef_ref[0:8, :] = a
    coef_ref[8:16, :] = b
    vectors[0:8, :] = -a * row_sums / k
    vectors[8:16, :] = a * (count_p * k / n_left) * row_d
    vectors[16:24, :] = b * row_right / rest
    vectors[24:32, :] = -b * (rest * count_s / n_right) * row_e
    total = count_p + ROWS
    n = total + count_s
    row_d = row_stat[2:3] - row_p
    row_e = row_s - (row_p + row_d * (ROWS / total))
    coef_ref[16:24, :] = jnp.broadcast_to(1.0 / n, (8, WIDTH))
    vectors[32:WIDTH, :] = jnp.zeros((WIDTH - 32, WIDTH), F32)
    vectors[32:33, :] = row_stat[1:2] / -ROWS / n
    vectors[33:34, :] = (count_p * ROWS / total) / n * row_d
    vectors[34:35, :] = (total * count_s / n) / n * row_e
    turned_ref[...] = vectors[...].T

    columns = (
        (own_means_ref[0], own_means_ref[1]),
        (ahead_ref[core], behind_ref[away]),
        (far_ref[core], far_ref[away]),
        (ahead_ref[away], behind_ref[core]),
    )
    for u in range(8):
        r, lanes = u // 2, slice(WIDTH * (u % 2), WIDTH * (u % 2) + WIDTH)
        means = columns[r][u % 2]
        col_p, col_part_p = pooled(means, 0)
        col_s, col_part_s = pooled(means, 1)
        stat = stat_ref[r, :, lanes]
        col_left = sums_ref[r, :, lanes]
        col_right = stat[1:2] - col_left
        cols_ref[u, 0:8, :] = col_left
        cols_ref[u, 8:16, :] = stat[0:1] + col_left / k - col_p
        cols_ref[u, 16:24, :] = col_right
        cols_ref[u, 24:32, :] = col_s - (stat[0:1] + col_right / rest)
        col_d = stat[2:3] - col_p
        cols_ref[u, 32:40, :] = jnp.zeros((8, WIDTH), F32)
        cols_ref[u, 32:33, :] = stat[1:2]
        cols_ref[u, 33:34, :] = col_d
        cols_ref[u, 34:35, :] = col_s - (col_p + col_d * (ROWS / total))

        def between(row_part, col_part):
            return ROWS * lax.dot_general(
                row_part, col_part, TRANSPOSED, precision=HIGH, preferred_element_type=F32
            )

        before_ref[u] = between(row_part_p, col_part_p)
        after_ref[u] = gram_ref[r, :, lanes] + between(row_part_s, col_part_s)


def load_near(ref, p_ref, s_ref):
    for g in range(8):
        p_ref[16 * g : 16 * g + 16, :] = ref[g, 0:16, :]
        s_ref[16 * g : 16 * g + 16, :] = ref[g, 16:32, :]


def load_far(ref, p_ref, s_ref):
    for q in range(BLOCKS):
        p_ref[4 * q : 4 * q + 4, :] = ref[q, 0:4, :]
        s_ref[4 * q : 4 * q + 4, :] = ref[q, 4:8, :]


def shard_lanes(where_ref, u):
    return pl.ds(pl.multiple_of(where_ref[4 + u] * WIDTH, WIDTH), WIDTH)


def most_kernel(
    where_ref, back_ref, store_hbm, most_ref, seg_ref, coef_ref,
    left_ref, prefix_ref, suffix_ref, cols_ref, turned_ref, p_ref, s_ref, sem,
):
    loads = [
        pltpu.make_async_copy(source, target, sem.at[c])
        for c, (source, target) in enumerate(
            (
                (store_hbm.at[8], prefix_ref),
                (store_hbm.at[9], suffix_ref),
                (store_hbm.at[10, :, pl.ds(0, 40)], cols_ref),
                (store_hbm.at[11, 0], turned_ref),
                (store_hbm.at[11, 1, pl.ds(0, 24)], coef_ref),
                *(
                    (store_hbm.at[pl.ds(0, 8), j], left_ref.at[:, j])
                    for j in range(SPLITS)
                ),
            )
        )
    ]
    for load in loads:
        load.start()
    held = where_ref[3]
    for load in loads[:5]:
        load.wait()

    def add(u):
        prefix_ref[u] = prefix_ref[u] + p_ref[...]
        suffix_ref[u] = suffix_ref[u] + s_ref[...]

    for u in range(4):
        load_near(back_ref.at[pl.ds(8 * u, 8)], p_ref, s_ref)
        add(u)
    load_far(back_ref.at[:, pl.ds(32, 8)], p_ref, s_ref)
    add(4 + held)

    def spread_out(rows):
        return [jnp.broadcast_to(turned_ref[:, i : i + 1], (WIDTH, WIDTH)) for i in rows]

    turned = spread_out(range(32, 35))
    for u in range(8):
        value = (prefix_ref[u] + suffix_ref[u]) * coef_ref[16:17, :]
        for i in range(3):
            value = value + turned[i] * cols_ref[u, 32 + i : 33 + i, :]
        seg_ref[:, shard_lanes(where_ref, u)] = value
    for j in range(SPLITS):
        loads[5 + j].wait()
        turned = spread_out(range(j, 32, 8))
        a, b = coef_ref[j : j + 1, :], coef_ref[8 + j : 9 + j, :]
        for u in range(8):
            value = (a + b) * left_ref[u, j] + a * prefix_ref[u] - b * suffix_ref[u]
            for i in range(4):
                value = value + turned[i] * cols_ref[u, 8 * i + j : 8 * i + j + 1, :]
            most_ref[j, :, shard_lanes(where_ref, u)] = value


def last_kernel(
    where_ref, most_ref, most_seg_ref, coef_ref, opposite_ref, next_ref, before_ref, cusum_hbm, seg_hbm,
    cusum_ref, seg_ref, prefix_ref, suffix_ref, p_ref, s_ref, sem,
):
    shards = (5 - where_ref[3], 6, 7)
    for v, (ref, load) in enumerate(
        ((opposite_ref, load_far), (next_ref, load_near), (before_ref, load_near))
    ):
        load(ref, p_ref, s_ref)
        prefix_ref[v] = p_ref[...].T
        suffix_ref[v] = s_ref[...].T
    seg_ref[0] = most_seg_ref[...]
    for v, u in enumerate(shards):
        lanes = shard_lanes(where_ref, u)
        added = (prefix_ref[v] + suffix_ref[v]) * coef_ref[16:17, :]
        seg_ref[0, :, lanes] = most_seg_ref[:, lanes] + added
    stores = [pltpu.make_async_copy(seg_ref, seg_hbm, sem.at[SPLITS])]
    stores[0].start()
    for j in range(SPLITS):
        a, b = coef_ref[j : j + 1, :], coef_ref[8 + j : 9 + j, :]
        cusum_ref[0, j] = most_ref[j]
        for v, u in enumerate(shards):
            lanes = shard_lanes(where_ref, u)
            cusum_ref[0, j, :, lanes] = most_ref[j, :, lanes] + a * prefix_ref[v] - b * suffix_ref[v]
        store = pltpu.make_async_copy(
            cusum_ref.at[:, pl.ds(j, 1)], cusum_hbm.at[:, pl.ds(j, 1)], sem.at[j]
        )
        store.start()
        stores.append(store)
    for store in stores:
        store.wait()


OUTPUTS = [array(1, SPLITS, WIDTH, CHIPS * PAIR), array(1, WIDTH, CHIPS * PAIR)]
MOST = [array(SPLITS, WIDTH, CHIPS * PAIR), array(WIDTH, CHIPS * PAIR), array(24, WIDTH)]


def most_outputs(where, back, store):
    square = array(8, WIDTH, WIDTH)
    buffers = [array(8, SPLITS, WIDTH, WIDTH), square, square, array(8, 40, WIDTH)]
    buffers += [array(WIDTH, WIDTH)] * 3
    return pl.pallas_call(
        most_kernel,
        out_shape=MOST,
        grid=(1,),
        in_specs=[SM, whole(*back.shape), HBM],
        out_specs=[whole(*value.shape) for value in MOST],
        scratch_shapes=[pltpu.VMEM(value.shape, F32) for value in buffers]
        + [pltpu.SemaphoreType.DMA((5 + SPLITS,))],
        compiler_params=params(24),
        cost_estimate=cost(5),
        name="most_outputs",
    )(where, back, store)


def last_outputs(where, most, opposite, following, before):
    inputs = [*most, opposite, following, before]
    buffers = [*OUTPUTS, array(3, WIDTH, WIDTH), array(3, WIDTH, WIDTH)]
    buffers += [array(WIDTH, WIDTH)] * 2
    return pl.pallas_call(
        last_kernel,
        out_shape=OUTPUTS,
        grid=(1,),
        in_specs=[SM] + [whole(*value.shape) for value in inputs],
        out_specs=[HBM, HBM],
        scratch_shapes=[pltpu.VMEM(value.shape, F32) for value in buffers]
        + [pltpu.SemaphoreType.DMA((SPLITS + 1,))],
        compiler_params=params(24),
        cost_estimate=cost(3),
        name="last_outputs",
    )(where, *inputs)


def window_kernel(
    where_ref, halves, gram_ref, stat_ref, total_ref, out_ref, cent_ref, flip_ref, sum_ref,
):
    live = jnp.where(where_ref[0] > 0, 1.0, 0.0).astype(F32)
    core = where_ref[2]
    at = pl.multiple_of(core * WIDTH, WIDTH)
    off = pl.multiple_of((1 - core) * WIDTH, WIDTH)
    count = ROWS + live * HALO
    scale = wide(1.0 / jnp.full((1, WIDTH), count, F32))
    unbias = wide(1.0 / jnp.full((1, WIDTH), count - 1.0, F32))
    step = 256
    for r in range(CHIPS):
        lanes = (at, off) if r == 0 else (0, WIDTH)
        for raw, lane in zip(halves[2 * r : 2 * r + 2], lanes):
            mean = stat_ref[r, 0:1, pl.ds(lane, WIDTH)]

            def shift(i, _, raw=raw, lane=lane, mean=mean):
                piece = (raw[pl.ds(i * step, step), :].astype(F32) - mean) * live
                cent_ref[pl.ds(i * step, step), pl.ds(lane, WIDTH)] = piece.astype(BF16)
                return 0

            lax.fori_loop(0, HALO // step, shift, 0, unroll=2)
        if r == 0:
            flip_ref[...] = cent_ref[:, pl.ds(at, WIDTH)].T
            flipped = flip_ref[...]
            row_sum = jnp.dot(flipped, jnp.ones((HALO, WIDTH), BF16), preferred_element_type=F32)
            sum_ref[...] = row_sum + total_ref[...]
        cent = cent_ref[...]
        halo = jnp.dot(flip_ref[...], cent, preferred_element_type=F32)
        col_sum = jnp.dot(jnp.ones((16, HALO), BF16), cent, preferred_element_type=F32)[0:1]
        col_sum = col_sum + stat_ref[r, 1:2, :]
        value = (halo + gram_ref[r] - wide(sum_ref[...]) * (col_sum * scale)) * unbias
        for c in range(2):
            lane = pl.multiple_of(where_ref[4 + 2 * r + c] * WIDTH, WIDTH)
            out_ref[0, :, pl.ds(lane, WIDTH)] = value[:, c * WIDTH : (c + 1) * WIDTH]


def late_kernel(
    where_ref, h0, h1, h2, h3, h4, h5, h6, h7, total_ref, sums_ref, gram_ref, stat_ref,
    own_ref, ahead_ref, behind_ref, far_ref, flags_ref,
    turned_ref, cols_ref, coef_ref, before_ref, after_ref, window_ref, vectors, cent_ref, flip_ref, sum_ref,
):
    prep_kernel(
        where_ref, sums_ref, gram_ref, stat_ref, own_ref, ahead_ref, behind_ref, far_ref, flags_ref,
        turned_ref, cols_ref, coef_ref, before_ref, after_ref, vectors,
    )
    window_kernel(
        where_ref, (h0, h1, h2, h3, h4, h5, h6, h7), gram_ref, stat_ref, total_ref,
        window_ref, cent_ref, flip_ref, sum_ref,
    )


def late_terms(where, halves, total, sums, gram, stat, means, flags, store):
    square = (8, WIDTH, WIDTH)
    return call(
        late_kernel,
        "late_terms",
        [where, *halves, total, sums, gram, stat, *means, flags],
        [array(1, WIDTH, CHIPS * PAIR)],
        store=store,
        puts=(
            ((WIDTH, WIDTH), (11, 0)),
            ((8, 40, WIDTH), (10, slice(None), pl.ds(0, 40))),
            ((24, WIDTH), (11, 1, pl.ds(0, 24))),
            (square, 8),
            (square, 9),
        ),
        fetched=(9, 10, 11, 12, 13, 17),
        stored=(0,),
        scratch=[
            ((WIDTH, WIDTH), F32),
            ((HALO, PAIR), BF16),
            ((WIDTH, HALO), BF16),
            ((WIDTH, WIDTH), F32),
        ],
        us=0.1,
    )


def to_chan(value, target):
    count = lax.axis_size("chan")
    return lax.ppermute(value, "chan", [(s, target(s) % count) for s in range(count)])


def exchange(value):
    return lax.all_to_all(value, "tm", 0, 0, tiled=True)


def after(value, *others):
    return lax.optimization_barrier((value, *others))[0]


def local(samples, candidates, segment_start):
    here, index = lax.axis_index("tm"), lax.axis_index("chan")
    chip, core = index // 2, index % 2
    nearby = [2 * chip, 2 * chip + 1]
    for step, side in ((1, core), (3, 1 - core), (2, core), (2, 1 - core), (1, 1 - core), (3, core)):
        nearby.append(2 * ((chip + step) % CHIPS) + side)
    held = jnp.where(chip < CHIPS // 2, 0, 1)
    where = jnp.stack([here, chip, core, held] + nearby).astype(jnp.int32)
    where = jnp.concatenate([where, candidates[0], segment_start])

    behind = to_chan(samples, lambda s: s + 2)
    ahead = to_chan(samples, lambda s: s - 2)
    other = to_chan(samples, lambda s: s ^ 1)
    prior = lax.ppermute(samples[ROWS - HALO :], "tm", [(b, b + 1) for b in range(BLOCKS - 1)])
    flip_shape, square = array(WIDTH, ROWS, dtype=BF16), array(WIDTH, WIDTH)
    store, sums, gram, stat, late_flipped, late_total, flipped, spread0, total, rider = call(
        first_kernel,
        "first_pair",
        [where, samples, other],
        ALL + [flip_shape, square, flip_shape, array(WIDTH, PAIR), square, array(8, WIDTH)],
        puts=((SHARD_PAIR, pl.ds(0, 2)),),
        fetched=(1,),
        stored=(0, 1, 2, 3, 4),
        scratch=[((ROWS, PAIR), BF16)],
    )
    behind, ahead, prior, flipped = lax.optimization_barrier((behind, ahead, prior, flipped))
    half = ROWS // 2
    far_low = to_chan(behind[:half], lambda s: s + 2)
    far_high = to_chan(ahead[half:], lambda s: s - 2)
    behind_other = to_chan(behind, lambda s: s ^ 1)
    ahead_other = to_chan(ahead, lambda s: s ^ 1)
    store, sums, gram, stat, spread1 = call(
        near_kernel,
        "near_pair",
        [where, ahead, behind_other, flipped, total],
        ALL + [array(WIDTH, PAIR)],
        store=store,
        puts=((SHARD_PAIR, pl.ds(2, 2)),),
        stored=(0, 1, 2),
        kept=(sums, gram, stat),
        pair=1,
        scratch=[((ROWS, PAIR), BF16)],
    )
    store, sums, gram, stat = call(
        side_kernel,
        "side_pair",
        [where, ahead_other, behind, flipped],
        ALL,
        store=store,
        puts=((SHARD_PAIR, pl.ds(6, 2)),),
        stored=(0, 1, 2),
        kept=(sums, gram, stat),
        pair=3,
        scratch=[((ROWS, PAIR), BF16)],
        us=2,
    )
    far_low, far_high, stat = lax.optimization_barrier((far_low, far_high, stat))
    far = jnp.concatenate([far_low, far_high], axis=0)
    far_other = to_chan(far, lambda s: s ^ 1)
    gram, stat, pieces = call(
        far_kernel,
        "far_pair",
        [where, far, far_other, flipped, total, spread0, spread1, rider],
        ALL[1:] + [array(BLOCKS, 24, WIDTH)],
        stored=(0, 1),
        kept=(gram, stat),
        pair=2,
        scratch=[((WIDTH, WIDTH), F32), ((ROWS, PAIR), BF16)],
        us=0.1,
    )
    arrived = exchange(pieces)

    store, sums = call(
        rest_kernel,
        "rest_left",
        [where, after(far, pieces), far_other, late_flipped],
        ALL[:1],
        store=store,
        puts=((SHARD_PAIR, pl.ds(4, 2)),),
        fetched=(3,),
        stored=(0,),
        kept=(sums,),
        pair=2,
        scratch=[((ROWS, PAIR), BF16), ((1, 8, PAIR), F32)],
        us=4,
    )
    prior = after(prior, token(pieces))
    prior_ahead = to_chan(prior, lambda s: s - 2)
    prior_behind = to_chan(prior, lambda s: s + 2)
    prior_far = to_chan(prior, lambda s: s + 4)
    arrived, prior_ahead, sums = lax.optimization_barrier((arrived, prior_ahead, sums))
    scanned, own_means, flags = call(
        scan_kernel,
        "scan_pieces",
        [arrived],
        [array(BLOCKS, 40, WIDTH), array(2, BLOCKS, WIDTH), array(BLOCKS, WIDTH)],
        stored=(0, 1, 2),
        us=1,
    )
    back = exchange(scanned)
    ahead_means = to_chan(own_means, lambda s: s - 2)
    behind_means = to_chan(own_means, lambda s: s + 2)
    far_means = to_chan(own_means, lambda s: s + 4)
    means = (own_means, ahead_means, behind_means, far_means)
    halo = (prior, prior_ahead, prior_far, prior_behind)
    mine, other = halo, [to_chan(value, lambda s: s ^ 1) for value in halo]
    halves = (mine[0], other[0], mine[1], other[3], mine[2], other[2], other[1], mine[3])
    store, window_cov = late_terms(
        where, halves, late_total, sums, gram, stat, means, flags, store
    )
    back, store, window_cov = lax.optimization_barrier((back, store, window_cov))
    before = to_chan(back[16:24, 0:32], lambda s: s + 2)
    following = to_chan(back[24:32, 0:32], lambda s: (s - 2) ^ 1)
    opposite = to_chan(back[:, 32:40], lambda s: s + 4 if s < 4 else (s - 4) ^ 1)
    most = most_outputs(where, back, store)
    cusum, segment_cov = last_outputs(where, most, opposite, following, before)
    return window_cov, segment_cov, cusum


def solution(mesh):
    placed = (P("tm", "chan"), P("tm", None), P("tm"))
    return jax.shard_map(
        local,
        mesh=mesh,
        in_specs=placed,
        out_specs=(P("tm", "chan", None), P("tm", "chan", None), P("tm", None, "chan", None)),
        check_vma=False,
    )
```

```python
import jax
import jax.numpy as jnp
from jax import lax
from jax.experimental import pallas as pl
from jax.experimental.pallas import tpu as pltpu
from jax.sharding import PartitionSpec as P

F32, BF16 = jnp.float32, jnp.bfloat16
ROWS, HALO, WIDTH, BLOCKS, SPLITS, CHIPS = 2048, 1024, 128, 32, 8, 4
PAIR = 2 * WIDTH
HIGH = lax.Precision.HIGHEST
TRANSPOSED = (((0,), (0,)), ((), ()))
SM = pl.BlockSpec(memory_space=pltpu.SMEM)
HBM = pl.BlockSpec(memory_space=pltpu.HBM)
MIB = 2**20


def whole(*shape):
    return pl.BlockSpec(shape, lambda *_: (0,) * len(shape))


def array(*shape, dtype=F32):
    return jax.ShapeDtypeStruct(shape, dtype)


def params(grant):
    return pltpu.CompilerParams(
        vmem_limit_bytes=grant * MIB, dimension_semantics=("arbitrary",)
    )


def cost(microseconds):
    return pl.CostEstimate(
        flops=int(microseconds * 1e9), bytes_accessed=MIB, transcendentals=0
    )


def center_shard(raw_ref, out_ref, at):
    step = 256

    def add(i, total):
        piece = raw_ref[pl.ds(i * step, step), :].astype(F32)
        return total + jnp.sum(piece.reshape(step // 8, 8, WIDTH), axis=0)

    total = lax.fori_loop(0, ROWS // step, add, jnp.zeros((8, WIDTH), F32), unroll=2)
    mean = jnp.sum(total, axis=0, keepdims=True) / ROWS

    def shift(i, _):
        piece = raw_ref[pl.ds(i * step, step), :].astype(F32) - mean
        out_ref[pl.ds(i * step, step), pl.ds(at, WIDTH)] = piece.astype(BF16)
        return 0

    lax.fori_loop(0, ROWS // step, shift, 0, unroll=2)
    return mean


def center_pair(first_ref, second_ref, at, off, cent_ref, stat_ref):
    stat_ref[0] = jnp.zeros((8, PAIR), F32)
    stat_ref[0, 0:1, pl.ds(at, WIDTH)] = center_shard(first_ref, cent_ref, at)
    stat_ref[0, 0:1, pl.ds(off, WIDTH)] = center_shard(second_ref, cent_ref, off)
    total = jnp.dot(jnp.ones((16, ROWS), BF16), cent_ref[...], preferred_element_type=F32)[0:1]
    stat_ref[0, 1:2, :] = total
    stat_ref[0, 2:3, :] = stat_ref[0, 0:1, :] + total / ROWS


def turned_dot(left, right):
    return lax.dot_general(left, right, TRANSPOSED, preferred_element_type=F32)


def wide(value):
    return jnp.concatenate([value, value], axis=1)


def left_part(where_ref, flipped, cent_ref, left_ref, sums_ref, block=0):
    index = lax.broadcasted_iota(jnp.int32, (16, ROWS), 0)
    place = lax.broadcasted_iota(jnp.int32, (16, ROWS), 1)
    limit = jnp.zeros((16, ROWS), jnp.int32)
    for j in range(SPLITS):
        limit = jnp.where(index == j, where_ref[12 + j], limit)
    masks = jnp.where(place < limit, 1.0, 0.0).astype(BF16)
    cent = cent_ref[...]
    sums_ref[block] = jnp.dot(masks, cent, preferred_element_type=F32)[0:8]
    for i in range(SPLITS // 4):
        kept = jnp.concatenate([flipped * masks[j : j + 1, :] for j in range(4 * i, 4 * i + 4)], axis=0)
        part = jnp.dot(kept, cent, preferred_element_type=F32)
        for j in range(4):
            for c in range(2):
                rows, lanes = slice(j * WIDTH, (j + 1) * WIDTH), slice(c * WIDTH, (c + 1) * WIDTH)
                left_ref[c, 4 * i + j] = part[rows, lanes]


def first_kernel(
    where_ref, mine_ref, other_ref,
    left_ref, sums_ref, gram_ref, stat_ref, flip_hbm, total_hbm, flip_ref, spread_ref, total_ref, rider_ref, cent_ref,
):
    core = where_ref[2]
    at = pl.multiple_of(core * WIDTH, WIDTH)
    off = pl.multiple_of((1 - core) * WIDTH, WIDTH)
    center_pair(mine_ref, other_ref, at, off, cent_ref, stat_ref)
    rider_ref[...] = jnp.zeros((8, WIDTH), F32)
    rider_ref[0:1, :] = stat_ref[0, 2:3, 0:WIDTH]
    rider_ref[1:2, :] = stat_ref[0, 2:3, WIDTH:PAIR]
    rider_ref[2:3, :] = jnp.full((1, WIDTH), where_ref[20], jnp.int32).astype(F32)
    flip_ref[...] = cent_ref[:, pl.ds(at, WIDTH)].T
    flipped = flip_ref[...]
    flip_hbm[...] = flipped
    gram = jnp.dot(flipped, cent_ref[...], preferred_element_type=F32)
    gram_ref[0] = gram
    total = jnp.dot(flipped, jnp.ones((ROWS, WIDTH), BF16), preferred_element_type=F32)
    total_ref[...] = total
    total_hbm[...] = total
    spread_ref[...] = gram - wide(total) * (stat_ref[0, 1:2, :] / ROWS)
    left_part(where_ref, flipped, cent_ref, left_ref, sums_ref)


def near_kernel(
    where_ref, first_ref, second_ref, flip_ref, total_ref,
    left_ref, sums_ref, gram_ref, stat_ref, spread_ref, cent_ref,
):
    center_pair(first_ref, second_ref, 0, WIDTH, cent_ref, stat_ref)
    flipped = flip_ref[...]
    gram = jnp.dot(flipped, cent_ref[...], preferred_element_type=F32)
    gram_ref[0] = gram
    spread_ref[...] = gram - wide(total_ref[...]) * (stat_ref[0, 1:2, :] / ROWS)
    left_part(where_ref, flipped, cent_ref, left_ref, sums_ref)


def side_kernel(
    where_ref, first_ref, second_ref, flip_ref, left_ref, sums_ref, gram_ref, stat_ref, cent_ref
):
    center_pair(first_ref, second_ref, 0, WIDTH, cent_ref, stat_ref)
    flipped = flip_ref[...]
    gram_ref[0] = jnp.dot(flipped, cent_ref[...], preferred_element_type=F32)
    left_part(where_ref, flipped, cent_ref, left_ref, sums_ref)


def far_kernel(
    where_ref, first_ref, second_ref, flip_ref, total_ref, spread0_ref, spread1_ref, rider_ref,
    gram_ref, stat_ref, out_ref, held_ref, cent_ref,
):
    rider = rider_ref[0:4, :]
    for q in range(BLOCKS):
        spread, lane = ((spread0_ref, spread1_ref)[q // 16], WIDTH * (q // 8 % 2))
        row = 16 * (q % 8)
        out_ref[q, 0:16, :] = spread[row : row + 16, lane : lane + WIDTH]
        out_ref[q, 20:24, :] = rider
    center_pair(first_ref, second_ref, 0, WIDTH, cent_ref, stat_ref)
    gram = jnp.dot(flip_ref[...], cent_ref[...], preferred_element_type=F32)
    gram_ref[0] = gram
    spread = gram - wide(total_ref[...]) * (stat_ref[0, 1:2, :] / ROWS)
    held_ref[...] = jnp.where(where_ref[3] == 0, spread[:, 0:WIDTH], spread[:, WIDTH:PAIR])
    for q in range(BLOCKS):
        out_ref[q, 16:20, :] = held_ref[4 * q : 4 * q + 4, :]


def rest_kernel(where_ref, first_ref, second_ref, flip_ref, left_ref, sums_ref, cent_ref, stat_ref):
    center_pair(first_ref, second_ref, 0, WIDTH, cent_ref, stat_ref)
    left_part(where_ref, flip_ref[...], cent_ref, left_ref, sums_ref)


def token_kernel(pieces_ref, out_ref):
    out_ref[...] = jnp.zeros((8, WIDTH), F32)


def token(pieces):
    return pl.pallas_call(
        token_kernel,
        out_shape=array(8, WIDTH),
        grid=(1,),
        in_specs=[HBM],
        out_specs=whole(8, WIDTH),
        compiler_params=params(16),
        cost_estimate=cost(4),
        name="token",
    )(pieces)


ALL = [
    array(CHIPS, 8, PAIR),
    array(CHIPS, WIDTH, PAIR),
    array(CHIPS, 8, PAIR),
]


STORE = array(96, 8, WIDTH, WIDTH)
SHARD_PAIR = (2, SPLITS, WIDTH, WIDTH)


def call(
    kernel, name, inputs, outputs, *, store=None, puts=(), fetched=(), stored=(), kept=(),
    pair=0, span=1, scratch=(), us=3, grant=24,
):
    kept = (*([store] if store is not None else []), *kept)
    count, made, first = len(inputs), len(outputs), 1 if puts else 0
    sliced = [out in ALL for out in outputs]
    sizes = [(span, *out.shape[1:]) if cut else out.shape for out, cut in zip(outputs, sliced)]
    buffers = [pltpu.VMEM(inputs[i].shape, inputs[i].dtype) for i in fetched]
    buffers += [pltpu.VMEM(shape, F32) for shape, _ in puts]
    buffers += [pltpu.VMEM(sizes[i], outputs[i].dtype) for i in stored]

    def body(*refs):
        ins, refs = list(refs[:count]), refs[count + len(kept) :]
        slots, outs, refs = refs[:first], list(refs[first : first + made]), refs[first + made :]
        own, buffer, sem = refs[: len(scratch)], refs[len(scratch) : -1], refs[-1]
        copies = []
        for c, i in enumerate(fetched):
            copies.append(pltpu.make_async_copy(ins[i], buffer[c], sem.at[c]))
            ins[i] = buffer[c]
        for copy in copies:
            copy.start()
        for copy in copies:
            copy.wait()
        copies, mine = [], []
        for c, (_, place) in enumerate(puts, len(fetched)):
            copies.append(pltpu.make_async_copy(buffer[c], slots[0].at[place], sem.at[c]))
            mine.append(buffer[c])
        for c, i in enumerate(stored, len(fetched) + len(puts)):
            target = outs[i].at[pl.ds(pair, span)] if sliced[i] else outs[i]
            copies.append(pltpu.make_async_copy(buffer[c], target, sem.at[c]))
            outs[i] = buffer[c]
        kernel(*ins, *mine, *outs, *own)
        for copy in copies:
            copy.start()
        for copy in copies:
            copy.wait()

    ins = [SM if value.dtype == jnp.int32 else whole(*value.shape) for value in inputs]
    for i in fetched:
        ins[i] = HBM
    outs = [HBM if i in stored else whole(*out.shape) for i, out in enumerate(outputs)]
    aliased = range(first if store is None else 0, first + len(kept))
    return pl.pallas_call(
        body,
        out_shape=[STORE] * first + outputs,
        grid=(1,),
        in_specs=ins + [HBM] * len(kept),
        out_specs=[HBM] * first + outs,
        input_output_aliases={count + i: out for i, out in zip(range(len(kept)), aliased)},
        scratch_shapes=[pltpu.VMEM(shape, dtype) for shape, dtype in scratch]
        + buffers
        + [pltpu.SemaphoreType.DMA((max(len(buffers), 1),))],
        compiler_params=params(grant),
        cost_estimate=cost(us),
        name=name,
    )(*inputs, *kept)


def scan_kernel(arrived_ref, both_ref, means_ref, flags_ref):
    for b in range(BLOCKS):
        rider = arrived_ref[b, 16:24, :]
        means_ref[0, b : b + 1, :] = rider[4:5, :]
        means_ref[1, b : b + 1, :] = rider[5:6, :]
        flags_ref[b : b + 1, :] = rider[6:7, :]
    scan(arrived_ref, flags_ref, both_ref, 0, 16, 0)
    scan(arrived_ref, flags_ref, both_ref, 16, 4, 32)


def scan(arrived_ref, flags_ref, both_ref, row, size, at):
    zero = jnp.zeros((size, WIDTH), F32)
    running = zero
    for b in range(BLOCKS):
        begins = flags_ref[b : b + 1, :] > 0.5
        running = jnp.where(begins, zero, running)
        both_ref[b, at : at + size, :] = running
        running = running + arrived_ref[b, row : row + size, :]
    running = zero
    for b in reversed(range(BLOCKS)):
        begins = flags_ref[b : b + 1, :] > 0.5
        both_ref[b, at + size : at + 2 * size, :] = running
        running = jnp.where(begins, zero, running + arrived_ref[b, row : row + size, :])


def prep_kernel(
    where_ref, sums_ref, gram_ref, stat_ref, own_means_ref, ahead_ref, behind_ref, far_ref, flags_ref,
    turned_ref, cols_ref, coef_ref, before_ref, after_ref, vectors,
):
    here = where_ref[0]
    core = where_ref[2]
    away = 1 - core
    flags = flags_ref[...]
    spot = lax.broadcasted_iota(jnp.int32, (BLOCKS, WIDTH), 0)
    low = lax.broadcasted_iota(jnp.int32, (BLOCKS, BLOCKS), 1)
    high = lax.broadcasted_iota(jnp.int32, (BLOCKS, BLOCKS), 0)
    upto = jnp.dot((low <= high).astype(F32), flags, preferred_element_type=F32)
    mine = jnp.sum(jnp.where(spot <= here, flags, 0.0), axis=0, keepdims=True)
    same = jnp.abs(upto - mine) < 0.5
    masks = [
        jnp.where(same & (spot < here), 1.0, 0.0),
        jnp.where(same & (spot > here), 1.0, 0.0),
    ]
    totals = [jnp.sum(mask, axis=0, keepdims=True) for mask in masks]
    count_p, count_s = totals[0] * ROWS, totals[1] * ROWS

    def pooled(means, side):
        mask = masks[side]
        mean = jnp.sum(means * mask, axis=0, keepdims=True) / jnp.maximum(totals[side], 1.0)
        return mean, (means - mean) * mask

    def pick(value):
        return jnp.where(core == 0, value[:, 0:WIDTH], value[:, WIDTH:PAIR])

    row_means = own_means_ref[core]
    row_p, row_part_p = pooled(row_means, 0)
    row_s, row_part_s = pooled(row_means, 1)
    row_stat = pick(stat_ref[0])
    row_sums = pick(sums_ref[0])

    index = lax.broadcasted_iota(jnp.int32, (SPLITS, WIDTH), 0)
    k = jnp.zeros((SPLITS, WIDTH), jnp.int32)
    for j in range(SPLITS):
        k = jnp.where(index == j, where_ref[12 + j], k)
    k = k.astype(F32)
    rest = ROWS - k
    row_right = row_stat[1:2] - row_sums
    row_d = row_stat[0:1] + row_sums / k - row_p
    row_e = row_s - (row_stat[0:1] + row_right / rest)
    n_left, n_right = count_p + k, rest + count_s
    n = n_left + n_right
    weight = n_left * n_right / (n * n)
    a, b = weight / n_left, weight / n_right
    coef_ref[0:8, :] = a
    coef_ref[8:16, :] = b
    vectors[0:8, :] = -a * row_sums / k
    vectors[8:16, :] = a * (count_p * k / n_left) * row_d
    vectors[16:24, :] = b * row_right / rest
    vectors[24:32, :] = -b * (rest * count_s / n_right) * row_e
    total = count_p + ROWS
    n = total + count_s
    row_d = row_stat[2:3] - row_p
    row_e = row_s - (row_p + row_d * (ROWS / total))
    coef_ref[16:24, :] = jnp.broadcast_to(1.0 / n, (8, WIDTH))
    vectors[32:WIDTH, :] = jnp.zeros((WIDTH - 32, WIDTH), F32)
    vectors[32:33, :] = row_stat[1:2] / -ROWS / n
    vectors[33:34, :] = (count_p * ROWS / total) / n * row_d
    vectors[34:35, :] = (total * count_s / n) / n * row_e
    turned_ref[...] = vectors[...].T

    columns = (
        (own_means_ref[0], own_means_ref[1]),
        (ahead_ref[core], behind_ref[away]),
        (far_ref[core], far_ref[away]),
        (ahead_ref[away], behind_ref[core]),
    )
    for u in range(8):
        r, lanes = u // 2, slice(WIDTH * (u % 2), WIDTH * (u % 2) + WIDTH)
        means = columns[r][u % 2]
        col_p, col_part_p = pooled(means, 0)
        col_s, col_part_s = pooled(means, 1)
        stat = stat_ref[r, :, lanes]
        col_left = sums_ref[r, :, lanes]
        col_right = stat[1:2] - col_left
        cols_ref[u, 0:8, :] = col_left
        cols_ref[u, 8:16, :] = stat[0:1] + col_left / k - col_p
        cols_ref[u, 16:24, :] = col_right
        cols_ref[u, 24:32, :] = col_s - (stat[0:1] + col_right / rest)
        col_d = stat[2:3] - col_p
        cols_ref[u, 32:40, :] = jnp.zeros((8, WIDTH), F32)
        cols_ref[u, 32:33, :] = stat[1:2]
        cols_ref[u, 33:34, :] = col_d
        cols_ref[u, 34:35, :] = col_s - (col_p + col_d * (ROWS / total))

        def between(row_part, col_part):
            return ROWS * lax.dot_general(
                row_part, col_part, TRANSPOSED, precision=HIGH, preferred_element_type=F32
            )

        before_ref[u] = between(row_part_p, col_part_p)
        after_ref[u] = gram_ref[r, :, lanes] + between(row_part_s, col_part_s)


def load_near(ref, p_ref, s_ref):
    for g in range(8):
        p_ref[16 * g : 16 * g + 16, :] = ref[g, 0:16, :]
        s_ref[16 * g : 16 * g + 16, :] = ref[g, 16:32, :]


def load_far(ref, p_ref, s_ref):
    for q in range(BLOCKS):
        p_ref[4 * q : 4 * q + 4, :] = ref[q, 0:4, :]
        s_ref[4 * q : 4 * q + 4, :] = ref[q, 4:8, :]


def shard_lanes(where_ref, u):
    return pl.ds(pl.multiple_of(where_ref[4 + u] * WIDTH, WIDTH), WIDTH)


def most_kernel(
    where_ref, back_ref, store_hbm, most_ref, seg_ref, coef_ref,
    left_ref, prefix_ref, suffix_ref, cols_ref, turned_ref, p_ref, s_ref, sem,
):
    loads = [
        pltpu.make_async_copy(source, target, sem.at[c])
        for c, (source, target) in enumerate(
            (
                (store_hbm.at[8], prefix_ref),
                (store_hbm.at[9], suffix_ref),
                (store_hbm.at[10, :, pl.ds(0, 40)], cols_ref),
                (store_hbm.at[11, 0], turned_ref),
                (store_hbm.at[11, 1, pl.ds(0, 24)], coef_ref),
                *(
                    (store_hbm.at[pl.ds(0, 8), j], left_ref.at[:, j])
                    for j in range(SPLITS)
                ),
            )
        )
    ]
    for load in loads:
        load.start()
    held = where_ref[3]
    for load in loads[:5]:
        load.wait()

    def add(u):
        prefix_ref[u] = prefix_ref[u] + p_ref[...]
        suffix_ref[u] = suffix_ref[u] + s_ref[...]

    for u in range(4):
        load_near(back_ref.at[pl.ds(8 * u, 8)], p_ref, s_ref)
        add(u)
    load_far(back_ref.at[:, pl.ds(32, 8)], p_ref, s_ref)
    add(4 + held)

    def spread_out(rows):
        return [jnp.broadcast_to(turned_ref[:, i : i + 1], (WIDTH, WIDTH)) for i in rows]

    turned = spread_out(range(32, 35))
    for u in range(8):
        value = (prefix_ref[u] + suffix_ref[u]) * coef_ref[16:17, :]
        for i in range(3):
            value = value + turned[i] * cols_ref[u, 32 + i : 33 + i, :]
        seg_ref[:, shard_lanes(where_ref, u)] = value
    for j in range(SPLITS):
        loads[5 + j].wait()
        turned = spread_out(range(j, 32, 8))
        a, b = coef_ref[j : j + 1, :], coef_ref[8 + j : 9 + j, :]
        for u in range(8):
            value = (a + b) * left_ref[u, j] + a * prefix_ref[u] - b * suffix_ref[u]
            for i in range(4):
                value = value + turned[i] * cols_ref[u, 8 * i + j : 8 * i + j + 1, :]
            most_ref[j, :, shard_lanes(where_ref, u)] = value


def last_kernel(
    where_ref, most_ref, most_seg_ref, coef_ref, opposite_ref, next_ref, before_ref, cusum_hbm, seg_hbm,
    cusum_ref, seg_ref, prefix_ref, suffix_ref, p_ref, s_ref, sem,
):
    shards = (5 - where_ref[3], 6, 7)
    for v, (ref, load) in enumerate(
        ((opposite_ref, load_far), (next_ref, load_near), (before_ref, load_near))
    ):
        load(ref, p_ref, s_ref)
        prefix_ref[v] = p_ref[...].T
        suffix_ref[v] = s_ref[...].T
    seg_ref[0] = most_seg_ref[...]
    for v, u in enumerate(shards):
        lanes = shard_lanes(where_ref, u)
        added = (prefix_ref[v] + suffix_ref[v]) * coef_ref[16:17, :]
        seg_ref[0, :, lanes] = most_seg_ref[:, lanes] + added
    stores = [pltpu.make_async_copy(seg_ref, seg_hbm, sem.at[SPLITS])]
    stores[0].start()
    for j in range(SPLITS):
        a, b = coef_ref[j : j + 1, :], coef_ref[8 + j : 9 + j, :]
        cusum_ref[0, j] = most_ref[j]
        for v, u in enumerate(shards):
            lanes = shard_lanes(where_ref, u)
            cusum_ref[0, j, :, lanes] = most_ref[j, :, lanes] + a * prefix_ref[v] - b * suffix_ref[v]
        store = pltpu.make_async_copy(
            cusum_ref.at[:, pl.ds(j, 1)], cusum_hbm.at[:, pl.ds(j, 1)], sem.at[j]
        )
        store.start()
        stores.append(store)
    for store in stores:
        store.wait()


OUTPUTS = [array(1, SPLITS, WIDTH, CHIPS * PAIR), array(1, WIDTH, CHIPS * PAIR)]
MOST = [array(SPLITS, WIDTH, CHIPS * PAIR), array(WIDTH, CHIPS * PAIR), array(24, WIDTH)]


def most_outputs(where, back, store):
    square = array(8, WIDTH, WIDTH)
    buffers = [array(8, SPLITS, WIDTH, WIDTH), square, square, array(8, 40, WIDTH)]
    buffers += [array(WIDTH, WIDTH)] * 3
    return pl.pallas_call(
        most_kernel,
        out_shape=MOST,
        grid=(1,),
        in_specs=[SM, whole(*back.shape), HBM],
        out_specs=[whole(*value.shape) for value in MOST],
        scratch_shapes=[pltpu.VMEM(value.shape, F32) for value in buffers]
        + [pltpu.SemaphoreType.DMA((5 + SPLITS,))],
        compiler_params=params(24),
        cost_estimate=cost(5),
        name="most_outputs",
    )(where, back, store)


def last_outputs(where, most, opposite, following, before):
    inputs = [*most, opposite, following, before]
    buffers = [*OUTPUTS, array(3, WIDTH, WIDTH), array(3, WIDTH, WIDTH)]
    buffers += [array(WIDTH, WIDTH)] * 2
    return pl.pallas_call(
        last_kernel,
        out_shape=OUTPUTS,
        grid=(1,),
        in_specs=[SM] + [whole(*value.shape) for value in inputs],
        out_specs=[HBM, HBM],
        scratch_shapes=[pltpu.VMEM(value.shape, F32) for value in buffers]
        + [pltpu.SemaphoreType.DMA((SPLITS + 1,))],
        compiler_params=params(24),
        cost_estimate=cost(3),
        name="last_outputs",
    )(where, *inputs)


def window_kernel(
    where_ref, halves, gram_ref, stat_ref, total_ref, out_ref, cent_ref, flip_ref, sum_ref,
):
    live = jnp.where(where_ref[0] > 0, 1.0, 0.0).astype(F32)
    core = where_ref[2]
    at = pl.multiple_of(core * WIDTH, WIDTH)
    off = pl.multiple_of((1 - core) * WIDTH, WIDTH)
    count = ROWS + live * HALO
    scale = wide(1.0 / jnp.full((1, WIDTH), count, F32))
    unbias = wide(1.0 / jnp.full((1, WIDTH), count - 1.0, F32))
    step = 256
    for r in range(CHIPS):
        lanes = (at, off) if r == 0 else (0, WIDTH)
        for raw, lane in zip(halves[2 * r : 2 * r + 2], lanes):
            mean = stat_ref[r, 0:1, pl.ds(lane, WIDTH)]

            def shift(i, _, raw=raw, lane=lane, mean=mean):
                piece = (raw[pl.ds(i * step, step), :].astype(F32) - mean) * live
                cent_ref[pl.ds(i * step, step), pl.ds(lane, WIDTH)] = piece.astype(BF16)
                return 0

            lax.fori_loop(0, HALO // step, shift, 0, unroll=2)
        if r == 0:
            flip_ref[...] = cent_ref[:, pl.ds(at, WIDTH)].T
            flipped = flip_ref[...]
            row_sum = jnp.dot(flipped, jnp.ones((HALO, WIDTH), BF16), preferred_element_type=F32)
            sum_ref[...] = row_sum + total_ref[...]
        cent = cent_ref[...]
        halo = jnp.dot(flip_ref[...], cent, preferred_element_type=F32)
        col_sum = jnp.dot(jnp.ones((16, HALO), BF16), cent, preferred_element_type=F32)[0:1]
        col_sum = col_sum + stat_ref[r, 1:2, :]
        value = (halo + gram_ref[r] - wide(sum_ref[...]) * (col_sum * scale)) * unbias
        for c in range(2):
            lane = pl.multiple_of(where_ref[4 + 2 * r + c] * WIDTH, WIDTH)
            out_ref[0, :, pl.ds(lane, WIDTH)] = value[:, c * WIDTH : (c + 1) * WIDTH]


def late_kernel(
    where_ref, h0, h1, h2, h3, h4, h5, h6, h7, total_ref, sums_ref, gram_ref, stat_ref,
    own_ref, ahead_ref, behind_ref, far_ref, flags_ref,
    turned_ref, cols_ref, coef_ref, before_ref, after_ref, window_ref, vectors, cent_ref, flip_ref, sum_ref,
):
    prep_kernel(
        where_ref, sums_ref, gram_ref, stat_ref, own_ref, ahead_ref, behind_ref, far_ref, flags_ref,
        turned_ref, cols_ref, coef_ref, before_ref, after_ref, vectors,
    )
    window_kernel(
        where_ref, (h0, h1, h2, h3, h4, h5, h6, h7), gram_ref, stat_ref, total_ref,
        window_ref, cent_ref, flip_ref, sum_ref,
    )


def late_terms(where, halves, total, sums, gram, stat, means, flags, store):
    square = (8, WIDTH, WIDTH)
    return call(
        late_kernel,
        "late_terms",
        [where, *halves, total, sums, gram, stat, *means, flags],
        [array(1, WIDTH, CHIPS * PAIR)],
        store=store,
        puts=(
            ((WIDTH, WIDTH), (11, 0)),
            ((8, 40, WIDTH), (10, slice(None), pl.ds(0, 40))),
            ((24, WIDTH), (11, 1, pl.ds(0, 24))),
            (square, 8),
            (square, 9),
        ),
        fetched=(9, 10, 11, 12, 13, 17),
        stored=(0,),
        scratch=[
            ((WIDTH, WIDTH), F32),
            ((HALO, PAIR), BF16),
            ((WIDTH, HALO), BF16),
            ((WIDTH, WIDTH), F32),
        ],
        us=0.1,
    )


def to_chan(value, target):
    count = lax.axis_size("chan")
    return lax.ppermute(value, "chan", [(s, target(s) % count) for s in range(count)])


def exchange(value):
    return lax.all_to_all(value, "tm", 0, 0, tiled=True)


def after(value, *others):
    return lax.optimization_barrier((value, *others))[0]


def local(samples, candidates, segment_start):
    here, index = lax.axis_index("tm"), lax.axis_index("chan")
    chip, core = index // 2, index % 2
    nearby = [2 * chip, 2 * chip + 1]
    for step, side in ((1, core), (3, 1 - core), (2, core), (2, 1 - core), (1, 1 - core), (3, core)):
        nearby.append(2 * ((chip + step) % CHIPS) + side)
    held = jnp.where(chip < CHIPS // 2, 0, 1)
    where = jnp.stack([here, chip, core, held] + nearby).astype(jnp.int32)
    where = jnp.concatenate([where, candidates[0], segment_start])

    behind = to_chan(samples, lambda s: s + 2)
    ahead = to_chan(samples, lambda s: s - 2)
    other = to_chan(samples, lambda s: s ^ 1)
    prior = lax.ppermute(samples[ROWS - HALO :], "tm", [(b, b + 1) for b in range(BLOCKS - 1)])
    flip_shape, square = array(WIDTH, ROWS, dtype=BF16), array(WIDTH, WIDTH)
    store, sums, gram, stat, late_flipped, late_total, flipped, spread0, total, rider = call(
        first_kernel,
        "first_pair",
        [where, samples, other],
        ALL + [flip_shape, square, flip_shape, array(WIDTH, PAIR), square, array(8, WIDTH)],
        puts=((SHARD_PAIR, pl.ds(0, 2)),),
        fetched=(1,),
        stored=(0, 1, 2, 3, 4),
        scratch=[((ROWS, PAIR), BF16)],
    )
    behind, ahead, prior, flipped = lax.optimization_barrier((behind, ahead, prior, flipped))
    half = ROWS // 2
    far_low = to_chan(behind[:half], lambda s: s + 2)
    far_high = to_chan(ahead[half:], lambda s: s - 2)
    behind_other = to_chan(behind, lambda s: s ^ 1)
    ahead_other = to_chan(ahead, lambda s: s ^ 1)
    store, sums, gram, stat, spread1 = call(
        near_kernel,
        "near_pair",
        [where, ahead, behind_other, flipped, total],
        ALL + [array(WIDTH, PAIR)],
        store=store,
        puts=((SHARD_PAIR, pl.ds(2, 2)),),
        stored=(0, 1, 2),
        kept=(sums, gram, stat),
        pair=1,
        scratch=[((ROWS, PAIR), BF16)],
    )
    store, sums, gram, stat = call(
        side_kernel,
        "side_pair",
        [where, ahead_other, behind, flipped],
        ALL,
        store=store,
        puts=((SHARD_PAIR, pl.ds(6, 2)),),
        stored=(0, 1, 2),
        kept=(sums, gram, stat),
        pair=3,
        scratch=[((ROWS, PAIR), BF16)],
        us=2,
    )
    far_low, far_high, stat = lax.optimization_barrier((far_low, far_high, stat))
    far = jnp.concatenate([far_low, far_high], axis=0)
    far_other = to_chan(far, lambda s: s ^ 1)
    gram, stat, pieces = call(
        far_kernel,
        "far_pair",
        [where, far, far_other, flipped, total, spread0, spread1, rider],
        ALL[1:] + [array(BLOCKS, 24, WIDTH)],
        stored=(0, 1),
        kept=(gram, stat),
        pair=2,
        scratch=[((WIDTH, WIDTH), F32), ((ROWS, PAIR), BF16)],
        us=0.1,
    )
    arrived = exchange(pieces)

    store, sums = call(
        rest_kernel,
        "rest_left",
        [where, after(far, pieces), far_other, late_flipped],
        ALL[:1],
        store=store,
        puts=((SHARD_PAIR, pl.ds(4, 2)),),
        fetched=(3,),
        stored=(0,),
        kept=(sums,),
        pair=2,
        scratch=[((ROWS, PAIR), BF16), ((1, 8, PAIR), F32)],
        us=4,
    )
    prior = after(prior, token(pieces))
    prior_ahead = to_chan(prior, lambda s: s - 2)
    prior_behind = to_chan(prior, lambda s: s + 2)
    prior_far = to_chan(prior, lambda s: s + 4)
    arrived, prior_ahead, prior_behind, prior_far, sums = lax.optimization_barrier(
        (arrived, prior_ahead, prior_behind, prior_far, sums)
    )
    scanned, own_means, flags = call(
        scan_kernel,
        "scan_pieces",
        [arrived],
        [array(BLOCKS, 40, WIDTH), array(2, BLOCKS, WIDTH), array(BLOCKS, WIDTH)],
        stored=(0, 1, 2),
        us=1,
    )
    back = exchange(scanned)
    ahead_means = to_chan(own_means, lambda s: s - 2)
    behind_means = to_chan(own_means, lambda s: s + 2)
    far_means = to_chan(own_means, lambda s: s + 4)
    means = (own_means, ahead_means, behind_means, far_means)
    halo = (prior, prior_ahead, prior_far, prior_behind)
    halo, means = lax.optimization_barrier((halo, means))
    mine, other = halo, [to_chan(value, lambda s: s ^ 1) for value in halo]
    halves = (mine[0], other[0], mine[1], other[3], mine[2], other[2], other[1], mine[3])
    store, window_cov = late_terms(
        where, halves, late_total, sums, gram, stat, means, flags, store
    )
    back, store, window_cov = lax.optimization_barrier((back, store, window_cov))
    before = to_chan(back[16:24, 0:32], lambda s: s + 2)
    following = to_chan(back[24:32, 0:32], lambda s: (s - 2) ^ 1)
    opposite = to_chan(back[:, 32:40], lambda s: s + 4 if s < 4 else (s - 4) ^ 1)
    most = most_outputs(where, back, store)
    cusum, segment_cov = last_outputs(where, most, opposite, following, before)
    return window_cov, segment_cov, cusum


def solution(mesh):
    placed = (P("tm", "chan"), P("tm", None), P("tm"))
    return jax.shard_map(
        local,
        mesh=mesh,
        in_specs=placed,
        out_specs=(P("tm", "chan", None), P("tm", "chan", None), P("tm", None, "chan", None)),
        check_vma=False,
    )
```
